32 devices in a mesh: head: 8 (over y, x, core), seq: 4 (over z).
Axes of the slice: x: 2, y: 2, z: 4, core: 2. Of those that a mesh axis runs over, the one named last changes fastest.
Arguments:
- tokens: bfloat16 [4096, 2048], P(('head', 'seq')), may hold values from -6 to 6
- keys: bfloat16 [4096, 2048], P(('head', 'seq')), may hold values from -6 to 6
- values: bfloat16 [4096, 2048], P(('head', 'seq')), may hold values from -6 to 6
- q_weight: bfloat16 [2048, 2048], P(('head', 'seq')), may hold values from -0.125 to 0.125
- o_weight: bfloat16 [2048, 2048], P(('head', 'seq')), may hold values from -0.75 to 0.75
- gate_weight: bfloat16 [2048, 5504], P(('head', 'seq')), may hold values from -0.125 to 0.125
- up_weight: bfloat16 [2048, 5504], P(('head', 'seq')), may hold values from -0.125 to 0.125
- down_weight: bfloat16 [5504, 2048], P(None, ('head', 'seq')), may hold values from -0.078125 to 0.078125
- attn_gain: bfloat16 [2048], P(('head', 'seq')), may hold values from 0.099609375 to 1.8984375
- ffn_gain: bfloat16 [2048], P(('head', 'seq')), may hold values from 0.099609375 to 1.8984375
- span_order: int32 [4, 16], P('seq'), may hold values from 0 to 15, as said below
- doc_lengths: int32 [4, 4], P('seq'), may hold values from 1 to 512, 1024 in all within a row
- cotangent: bfloat16 [4096, 2048], P(('head', 'seq')), may hold values from -6 to 6
Outputs:
- mixed_out: bfloat16 [4096, 2048], P(('head', 'seq'))
- d_tokens: bfloat16 [4096, 2048], P(('head', 'seq'))
- d_keys: bfloat16 [4096, 2048], P(('head', 'seq'))
- d_values: bfloat16 [4096, 2048], P(('head', 'seq'))
- d_q_weight: float32 [2048, 2048], P(('head', 'seq'))
- d_o_weight: float32 [2048, 2048], P(('head', 'seq'))
- d_gate_weight: float32 [2048, 5504], P(('head', 'seq'))
- d_up_weight: float32 [2048, 5504], P(('head', 'seq'))
- d_down_weight: float32 [5504, 2048], P(None, ('head', 'seq'))
- d_attn_gain: float32 [2048], P(('head', 'seq'))
- d_ffn_gain: float32 [2048], P(('head', 'seq'))
The draws below stay inside these ranges and needn't reach their ends.
Inputs may be any that keep to these rules, and one draw needn't show every extreme that they name: Each row is a permutation of the span numbers; a device holds spans span_order[s, 2 h] and span_order[s, 2 h + 1] of its group. `doc_lengths`: each row sums to 1024; its largest entry is 512.
All inputs are finite; a program needn't handle non-finite values.
Results may differ from the reference program's by a relative error of at most 0.013.
Values may be sent and summed in bfloat16 or wider, within the bound.
A program may use at most 320 MiB of HBM per device.

```python
import math
import jax
import jax.numpy as jnp
import numpy as np
from jax import lax

D = 2048
FF = 5504
HEADS = 16
HEAD_DIM = 128
TOK_DEV = 128
DOCS = 4
GROUPS = 4
GROUP = 1024
SPANS = 16
TOKENS = 4096
N_HEAD = 8
N_SEQ = 4


def draw_span_order(key, part):
    key = jax.random.fold_in(key, 11)
    row_keys = jax.random.split(key, GROUPS)
    return jax.vmap(lambda row_key: jax.random.permutation(row_key, SPANS))(row_keys).astype(jnp.int32)


def strengthened(values, own_key, source, target, blocks, factor):
    def block_of(dim):
        return (jnp.arange(values.shape[dim]) // (values.shape[dim] // blocks)).reshape((-1,) + (1,) * (values.ndim - 1 - dim))

    first = jax.random.permutation(own_key, blocks)[block_of(target)]
    other_side = (block_of(target) + blocks // 2) % blocks
    return jnp.where((block_of(source) == first) | (block_of(source) == other_side), factor * values, values)


def steps_of(own_key, extent, cuts, low, top_value):
    level, own = 1.0, jax.random.fold_in(own_key, 6)
    for dim, blocks in cuts:
        steps = jnp.exp(jax.random.uniform(jax.random.fold_in(own, dim), (blocks,), jnp.float32, low / len(cuts), top_value / len(cuts)))
        level = level * jnp.repeat(steps, extent[dim] // blocks).reshape([-1 if axis == dim else 1 for axis in range(len(extent))])
    return level


def split_up(count, total, reach, lean):
    loads = [(1 << 20) // math.isqrt(grade ** lean) + 1 for grade in range(2, count + 1)]
    spare, given = total - reach - (count - 1), [1] * (count - 1)
    while spare > 0:
        free = [i for i in range(count - 1) if given[i] < reach]
        pool, left = sum([loads[i] for i in free]), spare
        for i in free:
            extra = min(reach - given[i], max(1, left * loads[i] // pool), spare)
            given[i] = given[i] + extra
            spare = spare - extra
    return np.array([reach] + given)


def ragged(own_key, count, total, most, skew):
    if count == 2:
        one = jax.random.randint(own_key, (), max(1, total - most), min(most, total - 1) + 1)
        return jnp.stack([one, total - one])
    sizes = jnp.asarray(split_up(count, total, most, skew), jnp.int32)
    couples = (count - 1) // 2
    source_of, taker = sizes[1:1 + 2 * couples:2], sizes[2:2 + 2 * couples:2]
    margin = jnp.minimum(source_of - 1, most - taker)
    passed = jax.random.randint(jax.random.fold_in(own_key, 1), (couples,), 0, 1 << 20) % (margin + 1)
    sizes = sizes.at[1:1 + 2 * couples:2].set(source_of - passed).at[2:2 + 2 * couples:2].set(taker + passed)
    return sizes[jax.random.permutation(jax.random.fold_in(own_key, 2), count)]


def noise(rng, extent, scale, reach, pieces=(), held_as=jnp.bfloat16):
    factor_of = steps_of(rng, extent, pieces, -0.22, 0.18) if pieces else 1.0
    entries = jax.random.normal(rng, extent, jnp.float32) * scale * factor_of
    return jnp.minimum(jnp.maximum(entries, -reach), reach).astype(held_as)


def bell_draw_with(stream_key, extent, scale, most, shards, heavy, kind=jnp.bfloat16):
    values = scale * jax.random.normal(stream_key, extent, jnp.float32)
    if shards:
        values = values * steps_of(stream_key, extent, shards, -0.22, 0.18)
    return jnp.clip(strengthened(values, jax.random.fold_in(stream_key, 3), *heavy), -most, most).astype(kind)


def setup_inputs(seed: int = 0) -> dict:
    arg_keys = jax.random.split(jax.random.key(seed), 14)
    tokens = bell_draw_with(arg_keys[0], (TOKENS, D), 1.0, 6.0, ((0, 32),), (0, 1, 32, 2.75))
    keys = noise(arg_keys[1], (TOKENS, D), 1.0, 6.0, ((0, 32),))
    values = noise(arg_keys[2], (TOKENS, D), 1.0, 6.0, ((0, 32),))
    q_weight = noise(arg_keys[3], (D, D), D ** -0.5, 0.125, ((0, 32),))
    o_weight = noise(arg_keys[4], (D, D), (D // 32) ** -0.5, 0.75, ((0, 32),))
    gate_weight = noise(arg_keys[5], (D, FF), D ** -0.5, 0.125, ((0, 32),))
    up_weight = noise(arg_keys[6], (D, FF), D ** -0.5, 0.125, ((0, 32),))
    down_weight = noise(arg_keys[7], (FF, D), FF ** -0.5, 0.078125, ((1, 32),))
    attn_gain = jnp.clip(1.0 + 0.18 * jax.random.normal(arg_keys[8], (D,), jnp.float32), 0.099609375, 1.8984375).astype(jnp.bfloat16)
    ffn_gain = jnp.clip(1.0 + 0.18 * jax.random.normal(arg_keys[9], (D,), jnp.float32), 0.099609375, 1.8984375).astype(jnp.bfloat16)
    span_order = draw_span_order(jax.random.fold_in(arg_keys[13], 71), 0)
    doc_lengths = jax.vmap(lambda own: ragged(own, DOCS, GROUP, GROUP // 2, 2))(jax.random.split(arg_keys[11], GROUPS)).reshape((GROUPS, DOCS)).astype(jnp.int32)
    cotangent = bell_draw_with(arg_keys[12], (TOKENS, D), 1.0, 6.0, ((0, 32),), (0, 1, 32, 2.75))
    return {"tokens": tokens, "keys": keys, "values": values, "q_weight": q_weight, "o_weight": o_weight, "gate_weight": gate_weight, "up_weight": up_weight, "down_weight": down_weight, "attn_gain": attn_gain, "ffn_gain": ffn_gain, "span_order": span_order, "doc_lengths": doc_lengths, "cotangent": cotangent}


@jax.custom_vjp
def low(v):
    return lax.optimization_barrier(v.astype(jnp.bfloat16)).astype(jnp.float32)

@jax.custom_vjp
def low_back(v):
    return v

def low_keep(v):
    return (low(v), None)

def low_pass(kept, grad):
    return (grad,)

def back_keep(v):
    return (v, None)

def back_low(kept, grad):
    return (low(grad),)
low.defvjp(low_keep, low_pass)
low_back.defvjp(back_keep, back_low)
EPS = 1e-06
HIGH = lax.Precision.HIGHEST

def matmul(left, right):
    return jnp.dot(left, right, precision=HIGH)

def rms_scale(field):
    return lax.rsqrt(lax.optimization_barrier(jnp.mean(field * field, axis=-1, keepdims=True)) + EPS)

def to_groups(field):
    rest = field.shape[1:]
    field = field.reshape((N_HEAD, N_SEQ, TOK_DEV) + rest)
    return jnp.swapaxes(field, 0, 1).reshape((N_SEQ, N_HEAD * TOK_DEV) + rest)

def from_groups(field):
    rest = field.shape[2:]
    field = field.reshape((N_SEQ, N_HEAD, TOK_DEV) + rest)
    return jnp.swapaxes(field, 0, 1).reshape((N_SEQ * N_HEAD * TOK_DEV,) + rest)

def places(order_row, length_row, group):
    count = order_row.shape[0]
    width = group // count
    slots = jnp.arange(group, dtype=jnp.int32)
    which = slots // width
    picked = jnp.where(which[:, None] == jnp.arange(count, dtype=jnp.int32)[None, :], order_row[None, :], 0)
    seq_span = lax.optimization_barrier(jnp.sum(picked, axis=1)).astype(jnp.int32)
    position = (seq_span * width + slots % width).astype(jnp.int32)
    bounds = jnp.cumsum(length_row).astype(jnp.int32)
    segment = lax.optimization_barrier(jnp.sum((position[:, None] >= bounds[None, :]).astype(jnp.int32), axis=1)).astype(jnp.int32)
    return (position, segment)

def attend_group(packed):
    query, key_rows, value_rows, order_row, length_row = packed
    group = query.shape[0]
    rows = math.gcd(group, 512)
    position, segment = places(order_row, length_row, group)
    scale = 1.0 / math.sqrt(query.shape[-1])

    def block(start):
        query_rows = lax.dynamic_slice_in_dim(query, start, rows, 0)
        query_place = lax.dynamic_slice_in_dim(position, start, rows, 0)
        query_segment = lax.dynamic_slice_in_dim(segment, start, rows, 0)
        raw = jnp.einsum('qhd,khd->hqk', query_rows, key_rows, precision=HIGH)
        logits = low_back(raw) * scale
        allowed = (segment[None, :] == query_segment[:, None]) & (position[None, :] <= query_place[:, None])
        logits = jnp.where(allowed[None], logits, -1e+30)
        probs = jax.nn.softmax(logits, axis=-1)
        return jnp.einsum('hqk,khd->qhd', low(probs), value_rows, precision=HIGH)
    starts = jnp.arange(group // rows, dtype=jnp.int32) * rows
    blocks = lax.map(jax.checkpoint(block), starts)
    return blocks.reshape(query.shape)

def layer(tokens, keys, values, q_weight, o_weight, gate_weight, up_weight, down_weight, attn_gain, ffn_gain, span_order, doc_lengths):
    total_rows = tokens.shape[0]
    shape3 = (total_rows, HEADS, HEAD_DIM)
    attn_in = low(tokens * rms_scale(tokens) * attn_gain)
    query = low(low_back(matmul(attn_in, q_weight)))
    key_rows = low_back(keys)
    value_rows = low_back(values)
    mixed = lax.map(attend_group, (to_groups(query.reshape(shape3)), to_groups(key_rows.reshape(shape3)), to_groups(value_rows.reshape(shape3)), span_order, doc_lengths))
    attended = low(low_back(from_groups(mixed).reshape(total_rows, HEADS * HEAD_DIM)))
    hidden = tokens + low_back(matmul(attended, o_weight))
    ffn_in = low(hidden * rms_scale(hidden) * ffn_gain)
    gate = low_back(matmul(ffn_in, gate_weight))
    up_part = low_back(matmul(ffn_in, up_weight))
    act = low(jax.nn.silu(gate) * up_part)
    return hidden + matmul(act, down_weight)

def reference(tokens, keys, values, q_weight, o_weight, gate_weight, up_weight, down_weight, attn_gain, ffn_gain, span_order, doc_lengths, cotangent):
    floats = tuple((item.astype(jnp.float32) for item in (tokens, keys, values, q_weight, o_weight, gate_weight, up_weight, down_weight, attn_gain, ffn_gain)))

    def forward(*inputs):
        return layer(*inputs, span_order, doc_lengths)
    result, pull = jax.vjp(forward, *floats)
    grads = pull(cotangent.astype(jnp.float32))
    return (result.astype(jnp.bfloat16), grads[0].astype(jnp.bfloat16), grads[1].astype(jnp.bfloat16), grads[2].astype(jnp.bfloat16), grads[3], grads[4], grads[5], grads[6], grads[7], grads[8], grads[9])
```

```python
import functools
import math

import jax
import jax.numpy as jnp
from jax import lax
from jax.experimental import pallas as pl
from jax.experimental.pallas import tpu as pltpu
from jax.sharding import PartitionSpec as P

HEAD_DIM = 128
EPS = 1e-06
BF16 = jnp.bfloat16
F32 = jnp.float32


def rms_scale(field):
    return lax.rsqrt(jnp.mean(field * field, axis=-1, keepdims=True) + EPS)


def dot(left, right, dims):
    return lax.dot_general(left, right, (dims, ((), ())), preferred_element_type=F32)


def places(order_row, length_row, group):
    count = order_row.shape[0]
    width = group // count
    slots = jnp.arange(group, dtype=jnp.int32)
    which = slots // width
    picked = jnp.where(
        which[:, None] == jnp.arange(count, dtype=jnp.int32)[None, :], order_row[None, :], 0
    )
    position = jnp.sum(picked, axis=1) * width + slots % width
    bounds = jnp.cumsum(length_row)
    segment = jnp.sum((position[:, None] >= bounds[None, :]).astype(jnp.int32), axis=1)
    return (position, segment)


def attend_kernel(q_ref, k_ref, v_ref, place_q, place_k, out_ref, lse_ref):
    scale = 1.0 / math.sqrt(HEAD_DIM)
    raw = dot(q_ref[...], k_ref[...], ((1,), (1,)))
    allowed = (place_q[:, 1:2] == place_k[1:2, :]) & (place_k[0:1, :] <= place_q[:, 0:1])
    logits = jnp.where(allowed, raw * scale, -1e30)
    top = jnp.max(logits, axis=-1, keepdims=True)
    expo = jnp.exp(logits - top)
    total = jnp.sum(expo, axis=-1, keepdims=True)
    probs = expo * (1.0 / total)
    out_ref[...] = dot(probs.astype(BF16), v_ref[...], ((1,), (0,))).astype(BF16)
    lse_ref[...] = jnp.broadcast_to(top + jnp.log(total), lse_ref.shape)


def attend(query, keys, values, place_q, place_k):
    group, width = query.shape
    heads = width // HEAD_DIM
    rows = min(group, 256)
    block = pl.BlockSpec((rows, HEAD_DIM), lambda h, i: (i, h))
    whole = pl.BlockSpec((group, HEAD_DIM), lambda h, i: (0, h))
    return pl.pallas_call(
        attend_kernel,
        grid=(heads, group // rows),
        in_specs=[
            block,
            whole,
            whole,
            pl.BlockSpec((rows, 2), lambda h, i: (i, 0)),
            pl.BlockSpec((2, group), lambda h, i: (0, 0)),
        ],
        out_specs=[block, block],
        out_shape=[
            jax.ShapeDtypeStruct((group, width), BF16),
            jax.ShapeDtypeStruct((group, width), F32),
        ],
        compiler_params=pltpu.CompilerParams(vmem_limit_bytes=48 << 20),
        cost_estimate=pl.CostEstimate(
            flops=4 * group * group * width,
            bytes_accessed=12 * group * width,
            transcendentals=heads * group * group,
        ),
        name="attend",
    )(query, keys, values, place_q, place_k)


def attend_back_kernel(
    q_ref, k_ref, v_ref, do_ref, lse_ref, place_q, place_k, dq_ref, dk_ref, dv_ref, dk_sum, dv_sum
):
    step = pl.program_id(1)
    scale = 1.0 / math.sqrt(HEAD_DIM)
    query, keys, grad = q_ref[...], k_ref[...], do_ref[...]
    raw = dot(query, keys, ((1,), (1,)))
    allowed = (place_q[:, 1:2] == place_k[1:2, :]) & (place_k[0:1, :] <= place_q[:, 0:1])
    logits = jnp.where(allowed, raw * scale, -1e30)
    probs = jnp.exp(logits - lse_ref[:, :1])
    grad_probs = dot(grad, v_ref[...], ((1,), (1,)))
    inner = jnp.sum(probs * grad_probs, axis=-1, keepdims=True)
    grad_raw = (probs * (grad_probs - inner) * scale).astype(BF16)
    dq_ref[...] = dot(grad_raw, keys, ((1,), (0,))).astype(BF16)

    @pl.when(step == 0)
    def _():
        dk_sum[...] = jnp.zeros_like(dk_sum)
        dv_sum[...] = jnp.zeros_like(dv_sum)

    dk_sum[...] += dot(grad_raw, query, ((0,), (0,)))
    dv_sum[...] += dot(probs.astype(BF16), grad, ((0,), (0,)))

    @pl.when(step == pl.num_programs(1) - 1)
    def _():
        dk_ref[...] = dk_sum[...].astype(BF16)
        dv_ref[...] = dv_sum[...].astype(BF16)


def attend_back(query, keys, values, grad, lse, place_q, place_k):
    group, width = query.shape
    heads = width // HEAD_DIM
    rows = min(group, 256)
    block = pl.BlockSpec((rows, HEAD_DIM), lambda h, i: (i, h))
    whole = pl.BlockSpec((group, HEAD_DIM), lambda h, i: (0, h))
    full = jax.ShapeDtypeStruct((group, width), BF16)
    return pl.pallas_call(
        attend_back_kernel,
        grid=(heads, group // rows),
        in_specs=[
            block,
            whole,
            whole,
            block,
            block,
            pl.BlockSpec((rows, 2), lambda h, i: (i, 0)),
            pl.BlockSpec((2, group), lambda h, i: (0, 0)),
        ],
        out_specs=[block, whole, whole],
        out_shape=[full, full, full],
        scratch_shapes=[pltpu.VMEM((group, HEAD_DIM), F32)] * 2,
        compiler_params=pltpu.CompilerParams(vmem_limit_bytes=48 << 20),
        cost_estimate=pl.CostEstimate(
            flops=10 * group * group * width,
            bytes_accessed=18 * group * width,
            transcendentals=heads * group * group,
        ),
        name="attend_back",
    )(query, keys, values, grad, lse, place_q, place_k)


def to_slices(weight, nh):
    rows, cols = weight.shape
    parts = weight.reshape(rows, nh, cols // nh).swapaxes(0, 1)
    return lax.all_to_all(parts, "head", 0, 0, tiled=False).reshape(nh * rows, cols // nh)


def from_slices(part, nh):
    rows, cols = part.shape
    parts = part.reshape(nh, rows // nh, cols)
    parts = lax.all_to_all(parts, "head", 0, 0, tiled=False)
    return parts.swapaxes(0, 1).reshape(rows // nh, nh * cols)


def gather_seq(part):
    return lax.all_gather(part, "seq", axis=0, tiled=True)


def scatter_seq(full):
    return lax.psum_scatter(full.astype(BF16), "seq", scatter_dimension=0, tiled=True)


def gather_head(part):
    return lax.all_gather(part, "head", axis=0, tiled=True)


def scatter_head(full):
    return lax.psum_scatter(full.astype(BF16), "head", scatter_dimension=0, tiled=True)


def per_device(
    nh,
    ns,
    tokens,
    keys,
    values,
    q_weight,
    o_weight,
    gate_weight,
    up_weight,
    down_weight,
    attn_gain,
    ffn_gain,
    span_order,
    doc_lengths,
    cotangent,
):
    local, width = tokens.shape
    rows = q_weight.shape[0]

    def shuffle(field):
        return field.reshape(local, nh, ns, rows).swapaxes(1, 2).reshape(local, width)

    def unshuffle(field):
        return field.reshape(local, ns, nh, rows).swapaxes(1, 2).reshape(local, width)

    gain_one = attn_gain.astype(F32)[:, None]
    gain_two = ffn_gain.astype(F32)[:, None]
    inputs = tokens.astype(F32)
    scale_one = rms_scale(inputs)
    normed_one = inputs * scale_one
    normed_one_all = gather_head(shuffle(normed_one.astype(BF16)))
    w_q = gather_seq(to_slices((q_weight * gain_one).astype(BF16), nh))
    key_heads = to_slices(keys, nh)
    value_heads = to_slices(values, nh)
    w_o = gather_seq(o_weight)
    w_gate = gather_seq(to_slices((gate_weight * gain_two).astype(BF16), nh))
    w_up = gather_seq(to_slices((up_weight * gain_two).astype(BF16), nh))
    w_down = gather_seq(to_slices(down_weight.T, nh))
    cotangent_all = gather_head(shuffle(cotangent))

    group = normed_one_all.shape[0]
    position, segment = places(span_order[0], doc_lengths[0], group)
    place_q = jnp.stack([position, segment], axis=1)
    place_k = jnp.stack([position, segment], axis=0)

    query = dot(normed_one_all, w_q, ((1,), (0,))).astype(BF16)
    attended, lse = attend(query, key_heads, value_heads, place_q, place_k)
    hidden = inputs + scatter_head(dot(attended, w_o, ((1,), (0,)))).astype(F32)
    scale_two = rms_scale(hidden)
    normed_two = hidden * scale_two
    normed_two_all = gather_head(shuffle(normed_two.astype(BF16)))

    gate = dot(normed_two_all, w_gate, ((1,), (0,)))
    up = dot(normed_two_all, w_up, ((1,), (0,)))
    sigma = jax.nn.sigmoid(gate)
    act = (gate * sigma * up).astype(BF16)
    down_sum = scatter_seq(dot(cotangent_all, act, ((0,), (0,))))
    grad_act = dot(cotangent_all, w_down, ((1,), (0,)))
    grad_gate = (grad_act * up * sigma * (1.0 + gate * (1.0 - sigma))).astype(BF16)
    grad_up = (grad_act * gate * sigma).astype(BF16)
    spread_two = dot(grad_gate, w_gate, ((1,), (1,))) + dot(grad_up, w_up, ((1,), (1,)))
    scaled_two = unshuffle(scatter_head(spread_two)).astype(F32)
    gate_sum = scatter_seq(dot(normed_two_all, grad_gate, ((0,), (0,))))
    up_sum = scatter_seq(dot(normed_two_all, grad_up, ((0,), (0,))))
    mixed = unshuffle(scatter_head(dot(act, w_down, ((1,), (1,)))))
    mixed_out = (hidden + mixed.astype(F32)).astype(BF16)

    grad_hidden = cotangent.astype(F32) + scale_two * (
        scaled_two - normed_two * jnp.mean(scaled_two * normed_two, axis=-1, keepdims=True)
    )
    grad_hidden_all = gather_head(grad_hidden.astype(BF16))
    grad_attended = dot(grad_hidden_all, w_o, ((1,), (1,))).astype(BF16)
    o_sum = scatter_seq(dot(attended, grad_hidden_all, ((0,), (0,))))
    grad_query, grad_keys, grad_values = attend_back(
        query, key_heads, value_heads, grad_attended, lse, place_q, place_k
    )
    grad_keys = from_slices(grad_keys, nh)
    grad_values = from_slices(grad_values, nh)
    scaled_one = unshuffle(scatter_head(dot(grad_query, w_q, ((1,), (1,))))).astype(F32)
    q_sum = scatter_seq(dot(normed_one_all, grad_query, ((0,), (0,))))
    grad_tokens = grad_hidden + scale_one * (
        scaled_one - normed_one * jnp.mean(scaled_one * normed_one, axis=-1, keepdims=True)
    )
    q_sum = from_slices(q_sum, nh).astype(F32)
    gate_sum = from_slices(gate_sum, nh).astype(F32)
    up_sum = from_slices(up_sum, nh).astype(F32)
    down_sum = from_slices(down_sum, nh).astype(F32)
    grad_gain_one = jnp.sum(q_weight.astype(F32) * q_sum, axis=1)
    grad_gain_two = jnp.sum(
        gate_weight.astype(F32) * gate_sum + up_weight.astype(F32) * up_sum, axis=1
    )
    return (
        mixed_out,
        grad_tokens.astype(BF16),
        grad_keys,
        grad_values,
        gain_one * q_sum,
        o_sum.astype(F32),
        gain_two * gate_sum,
        gain_two * up_sum,
        down_sum.T,
        grad_gain_one,
        grad_gain_two,
    )


def solution(mesh):
    both = ("head", "seq")
    rows, cols, line, own = P(both, None), P(None, both), P(both), P("seq", None)
    return jax.shard_map(
        functools.partial(per_device, mesh.shape["head"], mesh.shape["seq"]),
        mesh=mesh,
        in_specs=(rows,) * 7 + (cols, line, line, own, own, rows),
        out_specs=(rows,) * 8 + (cols, line, line),
        check_vma=False,
    )
```

```python
import functools
import math

import jax
import jax.numpy as jnp
from jax import lax
from jax.experimental import pallas as pl
from jax.experimental.pallas import tpu as pltpu
from jax.sharding import PartitionSpec as P

HEAD_DIM = 128
NH, NS = 8, 4
EPS = 1e-06
BF16 = jnp.bfloat16
F32 = jnp.float32


def rms_scale(field):
    return lax.rsqrt(jnp.mean(field * field, axis=-1, keepdims=True) + EPS)


def dot(left, right, dims):
    return lax.dot_general(left, right, (dims, ((), ())), preferred_element_type=F32)


def places(order_row, length_row, group):
    count = order_row.shape[0]
    width = group // count
    slots = jnp.arange(group, dtype=jnp.int32)
    which = slots // width
    picked = jnp.where(
        which[:, None] == jnp.arange(count, dtype=jnp.int32)[None, :], order_row[None, :], 0
    )
    position = jnp.sum(picked, axis=1) * width + slots % width
    bounds = jnp.cumsum(length_row)
    segment = jnp.sum((position[:, None] >= bounds[None, :]).astype(jnp.int32), axis=1)
    return (position, segment)


def attend_kernel(q_ref, k_ref, v_ref, place_q, place_k, out_ref, lse_ref):
    scale = 1.0 / math.sqrt(HEAD_DIM)
    raw = dot(q_ref[...], k_ref[...], ((1,), (1,)))
    allowed = (place_q[:, 1:2] == place_k[1:2, :]) & (place_k[0:1, :] <= place_q[:, 0:1])
    logits = jnp.where(allowed, raw * scale, -1e30)
    top = jnp.max(logits, axis=-1, keepdims=True)
    expo = jnp.exp(logits - top)
    total = jnp.sum(expo, axis=-1, keepdims=True)
    probs = expo * (1.0 / total)
    out_ref[...] = dot(probs.astype(BF16), v_ref[...], ((1,), (0,))).astype(BF16)
    lse_ref[...] = jnp.broadcast_to(top + jnp.log(total), lse_ref.shape)


def attend(query, keys, values, place_q, place_k):
    group, width = query.shape
    heads = width // HEAD_DIM
    rows = min(group, 256)
    block = pl.BlockSpec((rows, HEAD_DIM), lambda h, i: (i, h))
    whole = pl.BlockSpec((group, HEAD_DIM), lambda h, i: (0, h))
    return pl.pallas_call(
        attend_kernel,
        grid=(heads, group // rows),
        in_specs=[
            block,
            whole,
            whole,
            pl.BlockSpec((rows, 2), lambda h, i: (i, 0)),
            pl.BlockSpec((2, group), lambda h, i: (0, 0)),
        ],
        out_specs=[block, block],
        out_shape=[
            jax.ShapeDtypeStruct((group, width), BF16),
            jax.ShapeDtypeStruct((group, width), F32),
        ],
        compiler_params=pltpu.CompilerParams(vmem_limit_bytes=48 << 20),
        cost_estimate=pl.CostEstimate(
            flops=4 * group * group * width,
            bytes_accessed=12 * group * width,
            transcendentals=heads * group * group,
        ),
        name="attend",
    )(query, keys, values, place_q, place_k)


def attend_back_kernel(
    q_ref, k_ref, v_ref, do_ref, lse_ref, place_q, place_k, dq_ref, dk_ref, dv_ref, dk_sum, dv_sum
):
    step = pl.program_id(1)
    scale = 1.0 / math.sqrt(HEAD_DIM)
    query, keys, grad = q_ref[...], k_ref[...], do_ref[...]
    raw = dot(query, keys, ((1,), (1,)))
    allowed = (place_q[:, 1:2] == place_k[1:2, :]) & (place_k[0:1, :] <= place_q[:, 0:1])
    logits = jnp.where(allowed, raw * scale, -1e30)
    probs = jnp.exp(logits - lse_ref[:, :1])
    grad_probs = dot(grad, v_ref[...], ((1,), (1,)))
    inner = jnp.sum(probs * grad_probs, axis=-1, keepdims=True)
    grad_raw = (probs * (grad_probs - inner) * scale).astype(BF16)
    dq_ref[...] = dot(grad_raw, keys, ((1,), (0,))).astype(BF16)

    @pl.when(step == 0)
    def _():
        dk_sum[...] = jnp.zeros_like(dk_sum)
        dv_sum[...] = jnp.zeros_like(dv_sum)

    dk_sum[...] += dot(grad_raw, query, ((0,), (0,)))
    dv_sum[...] += dot(probs.astype(BF16), grad, ((0,), (0,)))

    @pl.when(step == pl.num_programs(1) - 1)
    def _():
        dk_ref[...] = dk_sum[...].astype(BF16)
        dv_ref[...] = dv_sum[...].astype(BF16)


def attend_back(query, keys, values, grad, lse, place_q, place_k):
    group, width = query.shape
    heads = width // HEAD_DIM
    rows = min(group, 256)
    block = pl.BlockSpec((rows, HEAD_DIM), lambda h, i: (i, h))
    whole = pl.BlockSpec((group, HEAD_DIM), lambda h, i: (0, h))
    full = jax.ShapeDtypeStruct((group, width), BF16)
    return pl.pallas_call(
        attend_back_kernel,
        grid=(heads, group // rows),
        in_specs=[
            block,
            whole,
            whole,
            block,
            block,
            pl.BlockSpec((rows, 2), lambda h, i: (i, 0)),
            pl.BlockSpec((2, group), lambda h, i: (0, 0)),
        ],
        out_specs=[block, whole, whole],
        out_shape=[full, full, full],
        scratch_shapes=[pltpu.VMEM((group, HEAD_DIM), F32)] * 2,
        compiler_params=pltpu.CompilerParams(vmem_limit_bytes=48 << 20),
        cost_estimate=pl.CostEstimate(
            flops=10 * group * group * width,
            bytes_accessed=18 * group * width,
            transcendentals=heads * group * group,
        ),
        name="attend_back",
    )(query, keys, values, grad, lse, place_q, place_k)


MESH = pl.DeviceIdType.MESH
ANY = pl.BlockSpec(memory_space=pl.ANY)
VMEM = pl.BlockSpec(memory_space=pltpu.VMEM)


def peers_of(nh):
    h = lax.axis_index("head")
    s = lax.axis_index("seq")
    if nh == 8:
        others = [lax.bitwise_xor(h, k) for k in range(1, 8)]
    else:
        others = [lax.rem(h + k, nh) for k in range(1, nh)]
    return h, s, others


def greet(s, others):
    barrier = pltpu.get_barrier_semaphore()
    for p in others:
        pl.semaphore_signal(barrier, inc=1, device_id=(p, s), device_id_type=MESH)
    pl.semaphore_wait(barrier, len(others))


def ag_kernel(nh, x_ref, o_ref, send, recv, own):
    h, s, others = peers_of(nh)
    r = x_ref.shape[0]
    half = r // 2

    def put(i, src, dst, to):
        cp = pltpu.make_async_remote_copy(src_ref=src, dst_ref=dst, send_sem=send.at[i], recv_sem=recv.at[i], device_id=(to, s), device_id_type=MESH)
        cp.start()
        return cp

    mine = pltpu.make_async_copy(x_ref, o_ref.at[h], own)
    mine.start()
    greet(s, others)
    if nh != 8:
        cps = [put(i, x_ref, o_ref.at[h], p) for i, p in enumerate(others)]
        for cp in cps:
            cp.wait()
        mine.wait()
        return
    pc, px, _, py, _, _, _ = others
    pd = lax.bitwise_xor(h, 6)
    lo, hi = pl.ds(0, half), pl.ds(half, half)
    xa = put(0, x_ref.at[lo], o_ref.at[h, lo], px)
    yb = put(1, x_ref.at[hi], o_ref.at[h, hi], py)
    c0 = put(2, x_ref, o_ref.at[h], pc)
    xb = put(3, x_ref.at[hi], o_ref.at[h, hi], px)
    ya = put(4, x_ref.at[lo], o_ref.at[h, lo], py)
    xa.wait_recv()
    fy = put(5, o_ref.at[px, lo], o_ref.at[px, lo], py)
    c1 = put(6, o_ref.at[px, lo], o_ref.at[px, lo], pc)
    yb.wait_recv()
    fx = put(7, o_ref.at[py, hi], o_ref.at[py, hi], px)
    c2 = put(8, o_ref.at[py, hi], o_ref.at[py, hi], pc)
    xb.wait_recv()
    c3 = put(9, o_ref.at[px, hi], o_ref.at[px, hi], pc)
    ya.wait_recv()
    c4 = put(10, o_ref.at[py, lo], o_ref.at[py, lo], pc)
    fy.wait_recv()
    c5 = put(11, o_ref.at[pd, lo], o_ref.at[pd, lo], pc)
    fx.wait_recv()
    c6 = put(12, o_ref.at[pd, hi], o_ref.at[pd, hi], pc)
    for cp in (c0, c1, c2, c3, c4, c5, c6):
        cp.wait_recv()
    for cp in (xa, yb, xb, ya, fy, fx, c0, c1, c2, c3, c4, c5, c6):
        cp.wait_send()
    mine.wait()


def ag_head(x, nh, cid, name):
    r, d = x.shape
    return pl.pallas_call(
        functools.partial(ag_kernel, nh),
        out_shape=jax.ShapeDtypeStruct((nh, r, d), x.dtype),
        in_specs=[ANY], out_specs=ANY,
        scratch_shapes=[pltpu.SemaphoreType.DMA((16,)), pltpu.SemaphoreType.DMA((16,)), pltpu.SemaphoreType.DMA],
        compiler_params=pltpu.CompilerParams(collective_id=cid, has_side_effects=True),
        name=name,
    )(x).reshape(nh * r, d)


def rs_kernel(nh, p_ref, o_ref, core_in, held, far_in, send, recv):
    h, s, others = peers_of(nh)

    def put(i, src, dst, to):
        cp = pltpu.make_async_remote_copy(src_ref=src, dst_ref=dst, send_sem=send.at[i], recv_sem=recv.at[i], device_id=(to, s), device_id_type=MESH)
        cp.start()
        return cp

    greet(s, others)
    if nh != 8:
        cps = [put(i, p_ref.at[p], far_in.at[i], p) for i, p in enumerate(others)]
        total = p_ref[h].astype(F32)
        for i, cp in enumerate(cps):
            cp.wait_recv()
            total = total + far_in[i].astype(F32)
        o_ref[...] = total
        for cp in cps:
            cp.wait_send()
        return
    pc = others[0]
    ks = (6, 2, 4, 0)
    near = [put(i, p_ref.at[lax.bitwise_xor(pc, k)], core_in.at[i], pc) for i, k in enumerate(ks)]
    far = []
    for i, k in enumerate(ks):
        near[i].wait_recv()
        to = lax.bitwise_xor(h, k)
        total = p_ref[to].astype(F32) + core_in[i].astype(F32)
        if k:
            held[i] = total.astype(BF16)
            far.append(put(4 + i, held.at[i], far_in.at[i], to))
        else:
            o_ref[...] = total
    for i in (1, 2, 0):
        far[i].wait_recv()
        o_ref[...] += far_in[i].astype(F32)
    for cp in near + far:
        cp.wait_send()


def rs_head(x, nh, cid, name):
    n, d = x.shape
    r = n // nh
    near = 4 if nh == 8 else 1
    return pl.pallas_call(
        functools.partial(rs_kernel, nh),
        out_shape=jax.ShapeDtypeStruct((r, d), F32),
        in_specs=[VMEM], out_specs=VMEM,
        scratch_shapes=[pltpu.VMEM((near, r, d), BF16), pltpu.VMEM((3, r, d), BF16), pltpu.VMEM((3 if nh == 8 else nh - 1, r, d), BF16),
                        pltpu.SemaphoreType.DMA((16,)), pltpu.SemaphoreType.DMA((16,))],
        compiler_params=pltpu.CompilerParams(collective_id=cid, has_side_effects=True, vmem_limit_bytes=48 << 20),
        name=name,
    )(x.reshape(nh, r, d))


def a2a_kernel(nh, m, *refs):
    xs, os, (send, recv, own) = refs[:m], refs[m:2 * m], refs[2 * m:]
    h, s, others = peers_of(nh)
    mine = [pltpu.make_async_copy(x.at[h], o.at[h], own.at[j]) for j, (x, o) in enumerate(zip(xs, os))]
    for cp in mine:
        cp.start()
    greet(s, others)
    cps = []
    order = [5, 1, 3, 0, 4, 2, 6] if nh == 8 else range(nh - 1)
    for j, (x, o) in enumerate(zip(xs, os)):
        for i in order:
            p = others[i]
            cp = pltpu.make_async_remote_copy(src_ref=x.at[p], dst_ref=o.at[h], send_sem=send.at[j, i], recv_sem=recv.at[j, i], device_id=(p, s), device_id_type=MESH)
            cp.start()
            cps.append(cp)
    for cp in cps:
        cp.wait()
    for cp in mine:
        cp.wait()


def a2a_head(xs, nh, cid, name):
    m = len(xs)
    return pl.pallas_call(
        functools.partial(a2a_kernel, nh, m),
        out_shape=[jax.ShapeDtypeStruct(x.shape, x.dtype) for x in xs],
        in_specs=[ANY] * m, out_specs=[ANY] * m,
        scratch_shapes=[pltpu.SemaphoreType.DMA((m, nh - 1)), pltpu.SemaphoreType.DMA((m, nh - 1)), pltpu.SemaphoreType.DMA((m,))],
        compiler_params=pltpu.CompilerParams(collective_id=cid, has_side_effects=True),
        name=name,
    )(*xs)


def slices_of(weight, nh):
    rows, cols = weight.shape
    return weight.reshape(rows, nh, cols // nh).swapaxes(0, 1)


def rows_of(parts):
    nh, rows, cols = parts.shape
    return parts.swapaxes(0, 1).reshape(rows, nh * cols)


def flat(parts):
    return parts.reshape(parts.shape[0] * parts.shape[1], parts.shape[2])


def cut(part, nh):
    return part.reshape(nh, part.shape[0] // nh, part.shape[1])


def gather_seq(part):
    return lax.all_gather(part, "seq", axis=0, tiled=True)


def scatter_seq(full):
    return lax.psum_scatter(full.astype(BF16), "seq", scatter_dimension=0, tiled=True)


def remote(src, dst, send, recv, to):
    return pltpu.make_async_remote_copy(
        src_ref=src, dst_ref=dst, send_sem=send, recv_sem=recv, device_id=to, device_id_type=MESH
    )


class Net:
    def __init__(self):
        self.h = lax.axis_index("head")
        self.s = lax.axis_index("seq")
        self.open = []

    def peer(self, k):
        return (lax.bitwise_xor(self.h, k), self.s)

    def greet(self):
        barrier = pltpu.get_barrier_semaphore()
        for k in range(1, NH):
            pl.semaphore_signal(barrier, inc=1, device_id=self.peer(k), device_id_type=MESH)
        for k in range(1, NS):
            there = (self.h, lax.rem(self.s + k, NS))
            pl.semaphore_signal(barrier, inc=1, device_id=there, device_id_type=MESH)
        pl.semaphore_wait(barrier, NH - 1 + NS - 1)

    def put(self, src, dst, send, recv, to):
        copy = remote(src, dst, send, recv, to)
        copy.start()
        self.open.append(copy)
        return copy

    def swap(self, src, dst, send, recv, own):
        mine = pltpu.make_async_copy(src.at[self.h], dst(self.h), own)
        mine.start()
        copies = []
        for k in (6, 2, 4, 1, 5, 3, 7):
            to = self.peer(k)
            copies.append(
                self.put(src.at[to[0]], dst(self.h), send.at[k - 1], recv.at[k - 1], to)
            )

        def finish():
            for copy in copies:
                copy.wait_recv()
            mine.wait()

        return finish

    def gather(self, src, dst, send, recv, own):
        half = src.shape[0] // 2
        lo, hi = pl.ds(0, half), pl.ds(half, half)
        h, core, px, py = self.h, self.peer(1), self.peer(2), self.peer(4)
        x, y, d = px[0], py[0], lax.bitwise_xor(h, 6)
        mine = pltpu.make_async_copy(src, dst.at[h], own)
        mine.start()

        def put(i, a, b, to):
            return self.put(a, b, send.at[i], recv.at[i], to)

        xa = put(0, src.at[lo], dst.at[h, lo], px)
        yb = put(1, src.at[hi], dst.at[h, hi], py)
        c0 = put(2, src, dst.at[h], core)
        xb = put(3, src.at[hi], dst.at[h, hi], px)
        ya = put(4, src.at[lo], dst.at[h, lo], py)

        def finish():
            near = [c0]
            xa.wait_recv()
            fy = put(5, dst.at[x, lo], dst.at[x, lo], py)
            near.append(put(6, dst.at[x, lo], dst.at[x, lo], core))
            yb.wait_recv()
            fx = put(7, dst.at[y, hi], dst.at[y, hi], px)
            near.append(put(8, dst.at[y, hi], dst.at[y, hi], core))
            xb.wait_recv()
            near.append(put(9, dst.at[x, hi], dst.at[x, hi], core))
            ya.wait_recv()
            near.append(put(10, dst.at[y, lo], dst.at[y, lo], core))
            fy.wait_recv()
            near.append(put(11, dst.at[d, lo], dst.at[d, lo], core))
            fx.wait_recv()
            near.append(put(12, dst.at[d, hi], dst.at[d, hi], core))
            for copy in near:
                copy.wait_recv()
            mine.wait()

        return finish

    def scatter(self, block, near_out, core_in, held, far_in, send, recv):
        core = self.peer(1)
        order = (6, 2, 4, 0)
        near, far = [], []
        for i, k in enumerate(order):
            near_out[i] = block(lax.bitwise_xor(core[0], k)).astype(BF16)
            near.append(self.put(near_out.at[i], core_in.at[i], send.at[i], recv.at[i], core))
        for i, k in enumerate(order):
            total = block(lax.bitwise_xor(self.h, k))
            near[i].wait_recv()
            total = total + core_in[i].astype(F32)
            if k:
                held[i] = total.astype(BF16)
                far.append(
                    self.put(held.at[i], far_in.at[i], send.at[4 + i], recv.at[4 + i], self.peer(k))
                )

        def finish():
            result = total
            for i in (1, 2, 0):
                far[i].wait_recv()
                result = result + far_in[i].astype(F32)
            return result

        return finish

    def z_gather(self, src, block, send, recv):
        s = self.s
        steps = (2, -2, 1, -1)

        def there(d):
            return (self.h, s + d)

        def copy(n):
            return remote(src, block(s), send.at[n], recv.at[s], there(steps[n]))

        def valid(d):
            return (s + d >= 0) & (s + d < NS)

        middle = (s == 1) | (s == 2)
        origin = jnp.where(s == 2, 0, NS - 1)
        target = (self.h, NS - 1 - origin)

        def relay():
            return remote(block(origin), block(origin), send.at[4], recv.at[origin], target)

        for n, d in enumerate(steps):

            @pl.when(valid(d))
            def _():
                copy(n).start()

        def forward():
            @pl.when(middle)
            def _():
                relay().wait_recv()
                relay().start()

        def finish():
            for t in range(NS):
                waited = ((s == 2) & (t == 0)) | ((s == 1) & (t == NS - 1))

                @pl.when((s != t) & jnp.logical_not(waited))
                def _():
                    remote(block(t), block(t), send.at[0], recv.at[t], (self.h, s)).wait_recv()

        def drain():
            for n, d in enumerate(steps):

                @pl.when(valid(d))
                def _():
                    copy(n).wait_send()

            @pl.when(middle)
            def _():
                relay().wait_send()

        return forward, finish, drain

    def close(self):
        for copy in self.open:
            copy.wait_send()


def fetch(pairs, sems):
    copies = [pltpu.make_async_copy(a, b, sems.at[i]) for i, (a, b) in enumerate(pairs)]
    for copy in copies:
        copy.start()
    for copy in copies:
        copy.wait()


def forward_kernel(
    q_own,
    gate_own,
    up_own,
    down_own,
    o_own,
    n1_own,
    k_own,
    v_own,
    cot_own,
    tokens,
    place_q,
    place_k,
    w_q,
    w_gate,
    w_up,
    w_down,
    w_o,
    n1_all,
    k_all,
    v_all,
    cot_all,
    n2_all,
    query,
    attended,
    lse,
    hidden_out,
    wq_v,
    wo_v,
    n1_v,
    k_v,
    v_v,
    n2_v,
    near_out,
    core_in,
    held,
    far_in,
    swap_send,
    swap_recv,
    ag_send,
    ag_recv,
    rs_send,
    rs_recv,
    z_send,
    z_recv,
    own,
    fetch_sem,
):
    net = Net()
    h, s = net.h, net.s
    net.greet()

    def swap(j, src, dst):
        return net.swap(src, dst, swap_send.at[j], swap_recv.at[j], own.at[j])

    def gather(j, src, dst):
        return net.gather(src, dst, ag_send.at[j], ag_recv.at[j], own.at[8 + j])

    def z_gather(j, src, block):
        return net.z_gather(src, block, z_send.at[j], z_recv.at[j])

    def slab(w):
        return lambda t: w.at[:, t]

    q_there = swap(0, q_own, lambda p: w_q.at[p, s])
    n1_there = gather(0, n1_own, n1_all)
    mine = pltpu.make_async_copy(o_own, w_o.at[s], own.at[15])
    mine.start()
    gate_there = swap(1, gate_own, lambda p: w_gate.at[p, s])
    q_there()
    zq = z_gather(0, w_q.at[:, s], slab(w_q))
    k_there = swap(2, k_own, lambda p: k_all.at[p])
    v_there = swap(3, v_own, lambda p: v_all.at[p])
    n1_there()
    gate_there()
    zo = z_gather(1, o_own, lambda t: w_o.at[t])
    zg = z_gather(2, w_gate.at[:, s], slab(w_gate))
    up_there = swap(4, up_own, lambda p: w_up.at[p, s])
    down_there = swap(5, down_own, lambda p: w_down.at[p, s])
    zq[0]()
    k_there()
    v_there()
    fetch([(n1_all, n1_v), (k_all, k_v), (v_all, v_v)], fetch_sem)
    zq[1]()
    fetch([(w_q, wq_v)], fetch_sem)

    group = NH * n1_own.shape[0]
    local = n1_own.shape[0]
    width = n1_own.shape[1]
    wide = query.shape[1]
    step = 256
    weight = wq_v[...].reshape(width, wide)

    @pl.loop(0, group // step)
    def _(i):
        part = n1_v[pl.ds(i * (step // local), step // local)].reshape(step, width)
        query[pl.ds(pl.multiple_of(i * step, step), step), :] = dot(
            part, weight, ((1,), (0,))
        ).astype(BF16)

    up_there()
    zu = z_gather(3, w_up.at[:, s], slab(w_up))
    zo[0]()

    scale = 1.0 / math.sqrt(HEAD_DIM)
    for head in range(wide // HEAD_DIM):
        cols = slice(head * HEAD_DIM, (head + 1) * HEAD_DIM)

        @pl.loop(0, group // step)
        def _(i):
            rows = pl.ds(pl.multiple_of(i * step, step), step)
            keys = k_v[:, :, cols].reshape(group, HEAD_DIM)
            values = v_v[:, :, cols].reshape(group, HEAD_DIM)
            raw = dot(query[rows, cols], keys, ((1,), (1,)))
            allowed = (place_q[rows, 1:2] == place_k[1:2, :]) & (
                place_k[0:1, :] <= place_q[rows, 0:1]
            )
            logits = jnp.where(allowed, raw * scale, -1e30)
            top = jnp.max(logits, axis=-1, keepdims=True)
            expo = jnp.exp(logits - top)
            total = jnp.sum(expo, axis=-1, keepdims=True)
            probs = (expo * (1.0 / total)).astype(BF16)
            attended[rows, cols] = dot(probs, values, ((1,), (0,))).astype(BF16)
            lse[rows, cols] = jnp.broadcast_to(top + jnp.log(total), (step, HEAD_DIM))

    down_there()
    zd = z_gather(4, w_down.at[:, s], slab(w_down))
    zo[1]()
    mine.wait()
    fetch([(w_o, wo_v)], fetch_sem)

    def o_block(p):
        rows = pl.ds(pl.multiple_of(p * local, local), local)
        return dot(attended[rows, :], wo_v[...].reshape(wide, width), ((1,), (0,)))

    o_sum = net.scatter(o_block, near_out, core_in, held, far_in, rs_send, rs_recv)
    zg[0]()
    hidden = tokens[...].astype(F32) + o_sum()
    hidden_out[...] = hidden
    n2_v[...] = (hidden * rms_scale(hidden)).astype(BF16)
    n2_there = gather(1, n2_v, n2_all)
    n2_there()
    cot_there = gather(2, cot_own, cot_all)
    zu[0]()
    cot_there()
    zd[0]()
    for z in (zg, zu, zd):
        z[1]()
    for z in (zq, zo, zg, zu, zd):
        z[2]()
    net.close()


def forward_call(q_own, gate_own, up_own, down_own, o_own, n1_own, k_own, v_own, cot_own, tokens, place_q, place_k):
    local, width = tokens.shape
    group = NH * local
    rows = o_own.shape[0]
    wide, hid = q_own.shape[2], gate_own.shape[2]

    def bf(*shape):
        return jax.ShapeDtypeStruct(shape, BF16)

    out_shape = [
        bf(NH, NS, rows, wide),
        bf(NH, NS, rows, hid),
        bf(NH, NS, rows, hid),
        bf(NH, NS, rows, hid),
        bf(NS, rows, width),
        bf(NH, local, width),
        bf(NH, local, wide),
        bf(NH, local, wide),
        bf(NH, local, width),
        bf(NH, local, width),
        bf(group, wide),
        bf(group, wide),
        jax.ShapeDtypeStruct((group, wide), F32),
        jax.ShapeDtypeStruct((local, width), F32),
    ]
    dma = pltpu.SemaphoreType.DMA
    return pl.pallas_call(
        forward_kernel,
        out_shape=out_shape,
        in_specs=[ANY] * 9 + [VMEM] * 3,
        out_specs=[ANY] * 10 + [VMEM] * 4,
        scratch_shapes=[
            pltpu.VMEM((NH, NS, rows, wide), BF16),
            pltpu.VMEM((NS, rows, width), BF16),
            pltpu.VMEM((NH, local, width), BF16),
            pltpu.VMEM((NH, local, wide), BF16),
            pltpu.VMEM((NH, local, wide), BF16),
            pltpu.VMEM((local, width), BF16),
            pltpu.VMEM((4, local, width), BF16),
            pltpu.VMEM((4, local, width), BF16),
            pltpu.VMEM((3, local, width), BF16),
            pltpu.VMEM((3, local, width), BF16),
            dma((6, 7)),
            dma((6, 7)),
            dma((3, 13)),
            dma((3, 13)),
            dma((7,)),
            dma((7,)),
            dma((5, 5)),
            dma((5, NS)),
            dma((16,)),
            dma((4,)),
        ],
        compiler_params=pltpu.CompilerParams(
            collective_id=0, has_side_effects=True, vmem_limit_bytes=56 << 20
        ),
        name="forward",
    )(q_own, gate_own, up_own, down_own, o_own, n1_own, k_own, v_own, cot_own, tokens, place_q, place_k)


def per_device(
    nh,
    ns,
    tokens,
    keys,
    values,
    q_weight,
    o_weight,
    gate_weight,
    up_weight,
    down_weight,
    attn_gain,
    ffn_gain,
    span_order,
    doc_lengths,
    cotangent,
):
    local, width = tokens.shape
    rows = q_weight.shape[0]

    def regroup(term):
        cols = term.shape[1]
        return term.reshape(nh, ns, rows, cols).swapaxes(0, 1).reshape(width, cols)

    gain_one = attn_gain.astype(F32)[:, None]
    gain_two = ffn_gain.astype(F32)[:, None]
    inputs = tokens.astype(F32)
    scale_one = rms_scale(inputs)
    normed_one = inputs * scale_one
    group = nh * local
    position, segment = places(span_order[0], doc_lengths[0], group)
    place_q = jnp.stack([position, segment], axis=1)
    place_k = jnp.stack([position, segment], axis=0)
    (w_q, w_gate, w_up, w_down, w_o, normed_one_all, key_heads, value_heads,
     cotangent_all, normed_two_all, query, attended, lse, hidden) = forward_call(
        slices_of((q_weight * gain_one).astype(BF16), nh),
        slices_of((gate_weight * gain_two).astype(BF16), nh),
        slices_of((up_weight * gain_two).astype(BF16), nh),
        slices_of(down_weight.T, nh),
        o_weight,
        normed_one.astype(BF16),
        slices_of(keys, nh),
        slices_of(values, nh),
        cotangent,
        tokens,
        place_q,
        place_k,
    )
    w_q, w_gate, w_up, w_down = (w.reshape(width, w.shape[-1]) for w in (w_q, w_gate, w_up, w_down))
    w_o = flat(w_o)
    normed_one_all, key_heads, value_heads, cotangent_all, normed_two_all = (
        flat(v) for v in (normed_one_all, key_heads, value_heads, cotangent_all, normed_two_all)
    )
    scale_two = rms_scale(hidden)
    normed_two = hidden * scale_two
    gate = dot(normed_two_all, w_gate, ((1,), (0,)))
    up = dot(normed_two_all, w_up, ((1,), (0,)))
    sigma = jax.nn.sigmoid(gate)
    act = (gate * sigma * up).astype(BF16)
    down_term = dot(cotangent_all, act, ((0,), (0,))).astype(BF16)
    w_down, down_term = lax.optimization_barrier((w_down, down_term))
    down_sum = scatter_seq(regroup(down_term))
    grad_act = dot(cotangent_all, w_down, ((1,), (0,)))
    grad_gate = (grad_act * up * sigma * (1.0 + gate * (1.0 - sigma))).astype(BF16)
    grad_up = (grad_act * gate * sigma).astype(BF16)
    spread_two = dot(grad_gate, w_gate, ((1,), (1,))) + dot(grad_up, w_up, ((1,), (1,)))
    scaled_two = (rs_head(spread_two.astype(BF16), nh, 7, "sum_ffn"))
    gate_term = dot(normed_two_all, grad_gate, ((0,), (0,))).astype(BF16)
    up_term = dot(normed_two_all, grad_up, ((0,), (0,))).astype(BF16)
    scaled_two, gate_term, up_term = lax.optimization_barrier((scaled_two, gate_term, up_term))
    gate_sum = scatter_seq(regroup(gate_term))
    up_sum = scatter_seq(regroup(up_term))

    grad_hidden = cotangent.astype(F32) + scale_two * (
        scaled_two - normed_two * jnp.mean(scaled_two * normed_two, axis=-1, keepdims=True)
    )
    grad_hidden_all = ag_head(grad_hidden.astype(BF16), nh, 8, "gather_dh")
    grad_attended = dot(grad_hidden_all, w_o, ((1,), (1,))).astype(BF16)
    o_sum = scatter_seq(dot(attended, grad_hidden_all, ((0,), (0,))))
    grad_query, grad_keys, grad_values = attend_back(
        query, key_heads, value_heads, grad_attended, lse, place_q, place_k
    )
    q_term = dot(normed_one_all, grad_query, ((0,), (0,))).astype(BF16)
    grad_query, q_term = lax.optimization_barrier((grad_query, q_term))
    q_sum = scatter_seq(regroup(q_term))
    scaled_one = (rs_head(dot(grad_query, w_q, ((1,), (1,))).astype(BF16), nh, 9, "sum_q"))
    grad_tokens = grad_hidden + scale_one * (
        scaled_one - normed_one * jnp.mean(scaled_one * normed_one, axis=-1, keepdims=True)
    )
    mixed = (rs_head(dot(act, w_down, ((1,), (1,))).astype(BF16), nh, 10, "sum_mixed"))
    mixed_out = (hidden + mixed).astype(BF16)
    grad_keys, grad_values = a2a_head([cut(grad_keys, nh), cut(grad_values, nh)], nh, 11, "back_kv")
    gate_sum, down_sum = a2a_head([cut(gate_sum, nh), cut(down_sum, nh)], nh, 12, "back_ffn")
    q_sum, up_sum = a2a_head([cut(q_sum, nh), cut(up_sum, nh)], nh, 13, "back_q")
    q_sum = rows_of(q_sum).astype(F32)
    gate_sum = rows_of(gate_sum).astype(F32)
    up_sum = rows_of(up_sum).astype(F32)
    down_sum = rows_of(down_sum).astype(F32)
    grad_gain_one = jnp.sum(q_weight.astype(F32) * q_sum, axis=1)
    grad_gain_two = jnp.sum(
        gate_weight.astype(F32) * gate_sum + up_weight.astype(F32) * up_sum, axis=1
    )
    return (
        mixed_out,
        grad_tokens.astype(BF16),
        rows_of(grad_keys),
        rows_of(grad_values),
        gain_one * q_sum,
        o_sum.astype(F32),
        gain_two * gate_sum,
        gain_two * up_sum,
        down_sum.T,
        grad_gain_one,
        grad_gain_two,
    )


def to_slices(weight, nh):
    rows, cols = weight.shape
    parts = weight.reshape(rows, nh, cols // nh).swapaxes(0, 1)
    return lax.all_to_all(parts, "head", 0, 0, tiled=False).reshape(nh * rows, cols // nh)


def from_slices(part, nh):
    rows, cols = part.shape
    parts = part.reshape(nh, rows // nh, cols)
    parts = lax.all_to_all(parts, "head", 0, 0, tiled=False)
    return parts.swapaxes(0, 1).reshape(rows // nh, nh * cols)


def gather_head(part):
    return lax.all_gather(part, "head", axis=0, tiled=True)


def scatter_head(full):
    return lax.psum_scatter(full.astype(BF16), "head", scatter_dimension=0, tiled=True)


def per_device_plain(
    nh,
    ns,
    tokens,
    keys,
    values,
    q_weight,
    o_weight,
    gate_weight,
    up_weight,
    down_weight,
    attn_gain,
    ffn_gain,
    span_order,
    doc_lengths,
    cotangent,
):
    local, width = tokens.shape
    rows = q_weight.shape[0]

    def shuffle(field):
        return field.reshape(local, nh, ns, rows).swapaxes(1, 2).reshape(local, width)

    def unshuffle(field):
        return field.reshape(local, ns, nh, rows).swapaxes(1, 2).reshape(local, width)

    gain_one = attn_gain.astype(F32)[:, None]
    gain_two = ffn_gain.astype(F32)[:, None]
    inputs = tokens.astype(F32)
    scale_one = rms_scale(inputs)
    normed_one = inputs * scale_one
    normed_one_all = gather_head(shuffle(normed_one.astype(BF16)))
    w_q = gather_seq(to_slices((q_weight * gain_one).astype(BF16), nh))
    key_heads = to_slices(keys, nh)
    value_heads = to_slices(values, nh)
    w_o = gather_seq(o_weight)
    w_gate = gather_seq(to_slices((gate_weight * gain_two).astype(BF16), nh))
    w_up = gather_seq(to_slices((up_weight * gain_two).astype(BF16), nh))
    w_down = gather_seq(to_slices(down_weight.T, nh))
    cotangent_all = gather_head(shuffle(cotangent))

    group = normed_one_all.shape[0]
    position, segment = places(span_order[0], doc_lengths[0], group)
    place_q = jnp.stack([position, segment], axis=1)
    place_k = jnp.stack([position, segment], axis=0)

    query = dot(normed_one_all, w_q, ((1,), (0,))).astype(BF16)
    attended, lse = attend(query, key_heads, value_heads, place_q, place_k)
    hidden = inputs + scatter_head(dot(attended, w_o, ((1,), (0,)))).astype(F32)
    scale_two = rms_scale(hidden)
    normed_two = hidden * scale_two
    normed_two_all = gather_head(shuffle(normed_two.astype(BF16)))

    gate = dot(normed_two_all, w_gate, ((1,), (0,)))
    up = dot(normed_two_all, w_up, ((1,), (0,)))
    sigma = jax.nn.sigmoid(gate)
    act = (gate * sigma * up).astype(BF16)
    down_sum = scatter_seq(dot(cotangent_all, act, ((0,), (0,))))
    grad_act = dot(cotangent_all, w_down, ((1,), (0,)))
    grad_gate = (grad_act * up * sigma * (1.0 + gate * (1.0 - sigma))).astype(BF16)
    grad_up = (grad_act * gate * sigma).astype(BF16)
    spread_two = dot(grad_gate, w_gate, ((1,), (1,))) + dot(grad_up, w_up, ((1,), (1,)))
    scaled_two = unshuffle(scatter_head(spread_two)).astype(F32)
    gate_sum = scatter_seq(dot(normed_two_all, grad_gate, ((0,), (0,))))
    up_sum = scatter_seq(dot(normed_two_all, grad_up, ((0,), (0,))))
    mixed = unshuffle(scatter_head(dot(act, w_down, ((1,), (1,)))))
    mixed_out = (hidden + mixed.astype(F32)).astype(BF16)

    grad_hidden = cotangent.astype(F32) + scale_two * (
        scaled_two - normed_two * jnp.mean(scaled_two * normed_two, axis=-1, keepdims=True)
    )
    grad_hidden_all = gather_head(grad_hidden.astype(BF16))
    grad_attended = dot(grad_hidden_all, w_o, ((1,), (1,))).astype(BF16)
    o_sum = scatter_seq(dot(attended, grad_hidden_all, ((0,), (0,))))
    grad_query, grad_keys, grad_values = attend_back(
        query, key_heads, value_heads, grad_attended, lse, place_q, place_k
    )
    grad_keys = from_slices(grad_keys, nh)
    grad_values = from_slices(grad_values, nh)
    scaled_one = unshuffle(scatter_head(dot(grad_query, w_q, ((1,), (1,))))).astype(F32)
    q_sum = scatter_seq(dot(normed_one_all, grad_query, ((0,), (0,))))
    grad_tokens = grad_hidden + scale_one * (
        scaled_one - normed_one * jnp.mean(scaled_one * normed_one, axis=-1, keepdims=True)
    )
    q_sum = from_slices(q_sum, nh).astype(F32)
    gate_sum = from_slices(gate_sum, nh).astype(F32)
    up_sum = from_slices(up_sum, nh).astype(F32)
    down_sum = from_slices(down_sum, nh).astype(F32)
    grad_gain_one = jnp.sum(q_weight.astype(F32) * q_sum, axis=1)
    grad_gain_two = jnp.sum(
        gate_weight.astype(F32) * gate_sum + up_weight.astype(F32) * up_sum, axis=1
    )
    return (
        mixed_out,
        grad_tokens.astype(BF16),
        grad_keys,
        grad_values,
        gain_one * q_sum,
        o_sum.astype(F32),
        gain_two * gate_sum,
        gain_two * up_sum,
        down_sum.T,
        grad_gain_one,
        grad_gain_two,
    )


def solution(mesh):
    both = ("head", "seq")
    nh, ns = mesh.shape["head"], mesh.shape["seq"]
    body = per_device if (nh, ns) == (NH, NS) else per_device_plain
    rows, cols, line, own = P(both, None), P(None, both), P(both), P("seq", None)
    return jax.shard_map(
        functools.partial(body, nh, ns),
        mesh=mesh,
        in_specs=(rows,) * 7 + (cols, line, line, own, own, rows),
        out_specs=(rows,) * 8 + (cols, line, line),
        check_vma=False,
    )
```

```python
import functools
import math

import jax
import jax.numpy as jnp
from jax import lax
from jax.experimental import pallas as pl
from jax.experimental.pallas import tpu as pltpu
from jax.sharding import PartitionSpec as P

HEAD_DIM = 128
NH, NS = 8, 4
EPS = 1e-06
BF16 = jnp.bfloat16
F32 = jnp.float32


def rms_scale(field):
    return lax.rsqrt(jnp.mean(field * field, axis=-1, keepdims=True) + EPS)


def dot(left, right, dims):
    return lax.dot_general(left, right, (dims, ((), ())), preferred_element_type=F32)


def places(order_row, length_row, group):
    count = order_row.shape[0]
    width = group // count
    slots = jnp.arange(group, dtype=jnp.int32)
    which = slots // width
    picked = jnp.where(
        which[:, None] == jnp.arange(count, dtype=jnp.int32)[None, :], order_row[None, :], 0
    )
    position = jnp.sum(picked, axis=1) * width + slots % width
    bounds = jnp.cumsum(length_row)
    segment = jnp.sum((position[:, None] >= bounds[None, :]).astype(jnp.int32), axis=1)
    return (position, segment)


def attend_kernel(q_ref, k_ref, v_ref, place_q, place_k, out_ref, lse_ref):
    scale = 1.0 / math.sqrt(HEAD_DIM)
    raw = dot(q_ref[...], k_ref[...], ((1,), (1,)))
    allowed = (place_q[:, 1:2] == place_k[1:2, :]) & (place_k[0:1, :] <= place_q[:, 0:1])
    logits = jnp.where(allowed, raw * scale, -1e30)
    top = jnp.max(logits, axis=-1, keepdims=True)
    expo = jnp.exp(logits - top)
    total = jnp.sum(expo, axis=-1, keepdims=True)
    probs = expo * (1.0 / total)
    out_ref[...] = dot(probs.astype(BF16), v_ref[...], ((1,), (0,))).astype(BF16)
    lse_ref[...] = jnp.broadcast_to(top + jnp.log(total), lse_ref.shape)


def attend(query, keys, values, place_q, place_k):
    group, width = query.shape
    heads = width // HEAD_DIM
    rows = min(group, 256)
    block = pl.BlockSpec((rows, HEAD_DIM), lambda h, i: (i, h))
    whole = pl.BlockSpec((group, HEAD_DIM), lambda h, i: (0, h))
    return pl.pallas_call(
        attend_kernel,
        grid=(heads, group // rows),
        in_specs=[
            block,
            whole,
            whole,
            pl.BlockSpec((rows, 2), lambda h, i: (i, 0)),
            pl.BlockSpec((2, group), lambda h, i: (0, 0)),
        ],
        out_specs=[block, block],
        out_shape=[
            jax.ShapeDtypeStruct((group, width), BF16),
            jax.ShapeDtypeStruct((group, width), F32),
        ],
        compiler_params=pltpu.CompilerParams(vmem_limit_bytes=48 << 20),
        cost_estimate=pl.CostEstimate(
            flops=4 * group * group * width,
            bytes_accessed=12 * group * width,
            transcendentals=heads * group * group,
        ),
        name="attend",
    )(query, keys, values, place_q, place_k)


def attend_back_kernel(
    q_ref, k_ref, v_ref, do_ref, lse_ref, place_q, place_k, dq_ref, dk_ref, dv_ref, dk_sum, dv_sum
):
    step = pl.program_id(1)
    scale = 1.0 / math.sqrt(HEAD_DIM)
    query, keys, grad = q_ref[...], k_ref[...], do_ref[...]
    raw = dot(query, keys, ((1,), (1,)))
    allowed = (place_q[:, 1:2] == place_k[1:2, :]) & (place_k[0:1, :] <= place_q[:, 0:1])
    logits = jnp.where(allowed, raw * scale, -1e30)
    probs = jnp.exp(logits - lse_ref[:, :1])
    grad_probs = dot(grad, v_ref[...], ((1,), (1,)))
    inner = jnp.sum(probs * grad_probs, axis=-1, keepdims=True)
    grad_raw = (probs * (grad_probs - inner) * scale).astype(BF16)
    dq_ref[...] = dot(grad_raw, keys, ((1,), (0,))).astype(BF16)

    @pl.when(step == 0)
    def _():
        dk_sum[...] = jnp.zeros_like(dk_sum)
        dv_sum[...] = jnp.zeros_like(dv_sum)

    dk_sum[...] += dot(grad_raw, query, ((0,), (0,)))
    dv_sum[...] += dot(probs.astype(BF16), grad, ((0,), (0,)))

    @pl.when(step == pl.num_programs(1) - 1)
    def _():
        dk_ref[...] = dk_sum[...].astype(BF16)
        dv_ref[...] = dv_sum[...].astype(BF16)


def attend_back(query, keys, values, grad, lse, place_q, place_k):
    group, width = query.shape
    heads = width // HEAD_DIM
    rows = min(group, 256)
    block = pl.BlockSpec((rows, HEAD_DIM), lambda h, i: (i, h))
    whole = pl.BlockSpec((group, HEAD_DIM), lambda h, i: (0, h))
    full = jax.ShapeDtypeStruct((group, width), BF16)
    return pl.pallas_call(
        attend_back_kernel,
        grid=(heads, group // rows),
        in_specs=[
            block,
            whole,
            whole,
            block,
            block,
            pl.BlockSpec((rows, 2), lambda h, i: (i, 0)),
            pl.BlockSpec((2, group), lambda h, i: (0, 0)),
        ],
        out_specs=[block, whole, whole],
        out_shape=[full, full, full],
        scratch_shapes=[pltpu.VMEM((group, HEAD_DIM), F32)] * 2,
        compiler_params=pltpu.CompilerParams(vmem_limit_bytes=48 << 20),
        cost_estimate=pl.CostEstimate(
            flops=10 * group * group * width,
            bytes_accessed=18 * group * width,
            transcendentals=heads * group * group,
        ),
        name="attend_back",
    )(query, keys, values, grad, lse, place_q, place_k)


MESH = pl.DeviceIdType.MESH
ANY = pl.BlockSpec(memory_space=pl.ANY)
VMEM = pl.BlockSpec(memory_space=pltpu.VMEM)
SMEM = pl.BlockSpec(memory_space=pltpu.SMEM)


def slices_of(weight, nh):
    rows, cols = weight.shape
    return weight.reshape(rows, nh, cols // nh).swapaxes(0, 1)


def rows_of(parts):
    nh, rows, cols = parts.shape
    return parts.swapaxes(0, 1).reshape(rows, nh * cols)


def flat(parts):
    return parts.reshape(parts.shape[0] * parts.shape[1], parts.shape[2])


def remote(src, dst, send, recv, to):
    return pltpu.make_async_remote_copy(
        src_ref=src, dst_ref=dst, send_sem=send, recv_sem=recv, device_id=to, device_id_type=MESH
    )


class Net:
    def __init__(self):
        self.h = lax.axis_index("head")
        self.s = lax.axis_index("seq")
        self.open = []

    def peer(self, k):
        return (lax.bitwise_xor(self.h, k), self.s)

    def greet(self):
        barrier = pltpu.get_barrier_semaphore()
        for k in range(1, NH):
            pl.semaphore_signal(barrier, inc=1, device_id=self.peer(k), device_id_type=MESH)
        for k in range(1, NS):
            there = (self.h, lax.rem(self.s + k, NS))
            pl.semaphore_signal(barrier, inc=1, device_id=there, device_id_type=MESH)
        pl.semaphore_wait(barrier, NH - 1 + NS - 1)

    def put(self, src, dst, send, recv, to):
        copy = remote(src, dst, send, recv, to)
        copy.start()
        self.open.append(copy)
        return copy

    def swap(self, src, dst, send, recv, own):
        mine = pltpu.make_async_copy(src(self.h), dst(self.h), own)
        mine.start()
        copies = []
        for k in (6, 2, 4, 1, 5, 3, 7):
            to = self.peer(k)
            copy = remote(src(to[0]), dst(self.h), send.at[k - 1], recv.at[k - 1], to)
            copy.start()
            copies.append(copy)

        def finish():
            for copy in copies:
                copy.wait()
            mine.wait()

        return finish

    def gather(self, src, dst, send, recv, own):
        half = src.shape[0] // 2
        lo, hi = pl.ds(0, half), pl.ds(half, half)
        h, core, px, py = self.h, self.peer(1), self.peer(2), self.peer(4)
        x, y, d = px[0], py[0], lax.bitwise_xor(h, 6)
        mine = pltpu.make_async_copy(src, dst.at[h], own)
        mine.start()

        def put(i, a, b, to):
            return self.put(a, b, send.at[i], recv.at[i], to)

        xa = put(0, src.at[lo], dst.at[h, lo], px)
        yb = put(1, src.at[hi], dst.at[h, hi], py)
        c0 = put(2, src, dst.at[h], core)
        xb = put(3, src.at[hi], dst.at[h, hi], px)
        ya = put(4, src.at[lo], dst.at[h, lo], py)

        def finish():
            near = [c0]
            xa.wait_recv()
            fy = put(5, dst.at[x, lo], dst.at[x, lo], py)
            near.append(put(6, dst.at[x, lo], dst.at[x, lo], core))
            yb.wait_recv()
            fx = put(7, dst.at[y, hi], dst.at[y, hi], px)
            near.append(put(8, dst.at[y, hi], dst.at[y, hi], core))
            xb.wait_recv()
            near.append(put(9, dst.at[x, hi], dst.at[x, hi], core))
            ya.wait_recv()
            near.append(put(10, dst.at[y, lo], dst.at[y, lo], core))
            fy.wait_recv()
            near.append(put(11, dst.at[d, lo], dst.at[d, lo], core))
            fx.wait_recv()
            near.append(put(12, dst.at[d, hi], dst.at[d, hi], core))
            for copy in near:
                copy.wait_recv()
            mine.wait()

        return finish

    def scatter(self, source, block, core_in, held, far_in, send, recv):
        core = self.peer(1)
        order = (6, 2, 4, 0)

        def put(i, a, b, to):
            copy = remote(a, b, send.at[i], recv.at[i], to)
            copy.start()
            return copy

        near = [
            put(i, source(i, lax.bitwise_xor(core[0], k)), core_in.at[i], core)
            for i, k in enumerate(order)
        ]
        far = []
        for i, k in enumerate(order):
            value = block(i, lax.bitwise_xor(self.h, k))
            near[i].wait_recv()
            value = value + core_in[i].astype(F32)
            if k:
                held[i] = value.astype(BF16)
                far.append(put(4 + i, held.at[i], far_in.at[i], self.peer(k)))

        def finish():
            result = value
            for i in (1, 2, 0):
                far[i].wait_recv()
                result = result + far_in[i].astype(F32)
            for copy in near + far:
                copy.wait_send()
            return result

        return finish

    def z_gather(self, src, block, send, recv):
        s = self.s
        steps = (2, -2, 1, -1)

        def there(d):
            return (self.h, s + d)

        def copy(n):
            return remote(src, block(s), send.at[n], recv.at[s], there(steps[n]))

        def valid(d):
            return (s + d >= 0) & (s + d < NS)

        middle = (s == 1) | (s == 2)
        origin = jnp.where(s == 2, 0, NS - 1)
        target = (self.h, NS - 1 - origin)

        def relay():
            return remote(block(origin), block(origin), send.at[4], recv.at[origin], target)

        for n, d in enumerate(steps):

            @pl.when(valid(d))
            def _():
                copy(n).start()

        def forward():
            @pl.when(middle)
            def _():
                relay().wait_recv()
                relay().start()

        def finish():
            for t in range(NS):
                waited = ((s == 2) & (t == 0)) | ((s == 1) & (t == NS - 1))

                @pl.when((s != t) & jnp.logical_not(waited))
                def _():
                    remote(block(t), block(t), send.at[0], recv.at[t], (self.h, s)).wait_recv()

        def drain():
            for n, d in enumerate(steps):

                @pl.when(valid(d))
                def _():
                    copy(n).wait_send()

            @pl.when(middle)
            def _():
                relay().wait_send()

        return forward, finish, drain

    def close(self):
        for copy in self.open:
            copy.wait_send()


def fetch(pairs, sems):
    copies = [pltpu.make_async_copy(a, b, sems.at[i]) for i, (a, b) in enumerate(pairs)]
    for copy in copies:
        copy.start()
    for copy in copies:
        copy.wait()


def z_scatter(net, block, got, comb, send, recv):
    s = net.s
    first, last = s == 0, s == NS - 1
    middle = (s == 1) | (s == 2)
    far = jnp.where(s == 1, NS - 1, 0)
    inner = jnp.where(first, 1, NS - 2)

    def joined(src):
        return remote(src, got.at[s], send.at[0], recv.at[s], (net.h, far))

    def to_join():
        return remote(block(NS - 1 - s), comb, send.at[0], recv.at[NS], (net.h, inner))

    def direct(n, d):
        return remote(block(s + d), got.at[s], send.at[n], recv.at[s], (net.h, s + d))

    steps = ((1, 2, first), (2, -2, last), (3, 1, s < NS - 1), (4, -1, s > 0))

    def start_join():
        @pl.when(first | last)
        def _():
            to_join().start()

    def start():
        for n, d, where in steps:

            @pl.when(where)
            def _():
                direct(n, d).start()

    def join(one, two, sems):
        @pl.when(middle)
        def _():
            to_join().wait_recv()
            fetch([(comb, one), (block(far), two)], sems)
            one[...] = (one[...].astype(F32) + two[...].astype(F32)).astype(BF16)
            joined(one).start()

    def finish(total, bufs, sems):
        mine = pltpu.make_async_copy(block(s), bufs.at[NS], sems.at[NS])
        mine.start()

        def comes(t):
            return (s != t) & (s + t != NS - 1) if t in (0, NS - 1) else (s != t)

        for t in range(NS):

            @pl.when(comes(t))
            def _():
                remote(got.at[t], got.at[t], send.at[0], recv.at[t], (net.h, s)).wait_recv()
                pltpu.make_async_copy(got.at[t], bufs.at[t], sems.at[t]).start()

        mine.wait()
        total[...] = bufs[NS].astype(F32)
        for t in range(NS):

            @pl.when(comes(t))
            def _():
                pltpu.make_async_copy(got.at[t], bufs.at[t], sems.at[t]).wait()
                total[...] += bufs[t].astype(F32)

    def drain():
        @pl.when(first | last)
        def _():
            to_join().wait_send()

        for n, d, where in steps:

            @pl.when(where)
            def _():
                direct(n, d).wait_send()

        @pl.when(middle)
        def _():
            joined(comb).wait_send()

    return start_join, start, join, finish, drain


def make_places(order, lengths, place_q, place_k):
    group, count = place_q.shape[0], order.shape[1]
    width = group // count
    for shape, dim in (((group, 1), 0), ((1, group), 1)):
        slots = lax.broadcasted_iota(jnp.int32, shape, dim)
        position = slots
        for c in range(count):
            inside = (slots >= c * width) & (slots < (c + 1) * width)
            position = jnp.where(inside, slots + (order[0, c] - c) * width, position)
        segment = jnp.zeros(shape, jnp.int32)
        bound = 0
        for j in range(lengths.shape[1]):
            bound = bound + lengths[0, j]
            segment = segment + (position >= bound).astype(jnp.int32)
        if dim == 0:
            place_q[:, 0:1] = position
            place_q[:, 1:2] = segment
        else:
            place_k[0:1, :] = position
            place_k[1:2, :] = segment


def mask(place_q, place_k, rows):
    return (place_q[rows, 1:2] == place_k[1:2, :]) & (place_k[0:1, :] <= place_q[rows, 0:1])


def lane_block(w, p, wide):
    return w.at[:, pl.ds(pl.multiple_of(p * wide, wide), wide)]


def load(pairs, sems, base):
    copies = [pltpu.make_async_copy(a, b, sems.at[base + i]) for i, (a, b) in enumerate(pairs)]
    for copy in copies:
        copy.start()

    def finish():
        for copy in copies:
            copy.wait()

    return finish


def forward_kernel(
    q_weight,
    gate_weight,
    up_weight,
    down_rows,
    gain_one,
    gain_two,
    tokens,
    o_own,
    keys,
    values,
    cot_own,
    order,
    lengths,
    w_q,
    w_o,
    w_gate,
    w_up,
    w_down,
    n1_all,
    k_all,
    v_all,
    cot_all,
    n2_all,
    got_down,
    comb_down,
    spread,
    query,
    attended,
    lse,
    hidden_out,
    mixed_out,
    gate_term,
    up_term,
    down_sum,
    q_own,
    place_q,
    place_k,
    wq_v,
    wo_v,
    wg_v,
    wu_v,
    wd_v,
    norm_v,
    cot_v,
    k_v,
    v_v,
    n1_own,
    n2_own,
    near_out,
    core_in,
    held,
    far_in,
    act_v,
    grad_gate,
    grad_up,
    down_term,
    join_v,
    bufs,
    total,
    swap_send,
    swap_recv,
    ag_send,
    ag_recv,
    rs_send,
    rs_recv,
    z_send,
    z_recv,
    own,
    load_sem,
):
    net = Net()
    s = net.s
    local, width = tokens.shape
    group = NH * local
    wide, hid = query.shape[1], act_v.shape[1]
    step = 256
    tiles = group // step
    net.greet()
    gate_own, up_own, down_own = (bufs.at[i] for i in range(3))

    def swap(j, src, dst):
        return net.swap(src, dst, swap_send.at[j], swap_recv.at[j], own.at[j])

    def gather(j, src, dst):
        return net.gather(src, dst, ag_send.at[j], ag_recv.at[j], own.at[8 + j])

    def z_gather(j, src, block):
        return net.z_gather(src, block, z_send.at[j], z_recv.at[j])

    def slab(w):
        return lambda t: w.at[:, t]

    def slices(weight, gain, out):
        field = weight[...]
        if gain is not None:
            field = (field.astype(F32) * gain[...]).astype(BF16)
        cols = out.shape[2]
        for p in range(NH):
            out[p] = field[:, p * cols : (p + 1) * cols]

    zo = z_gather(0, o_own, lambda t: w_o.at[t])
    mine = pltpu.make_async_copy(o_own, w_o.at[s], own.at[15])
    mine.start()
    slices(q_weight, gain_one, q_own)
    q_there = swap(0, lambda p: q_own.at[p], lambda p: w_q.at[p, s])
    slices(gate_weight, gain_two, gate_own)
    gate_there = swap(1, lambda p: gate_own.at[p], lambda p: w_gate.at[p, s])
    inputs = tokens[...].astype(F32)
    n1_own[...] = (inputs * rms_scale(inputs)).astype(BF16)
    n1_there = gather(0, n1_own, n1_all)
    q_there()
    zq = z_gather(1, w_q.at[:, s], slab(w_q))
    slices(up_weight, gain_two, up_own)
    k_there = swap(2, lambda p: lane_block(keys, p, wide), lambda p: k_all.at[p])
    v_there = swap(3, lambda p: lane_block(values, p, wide), lambda p: v_all.at[p])
    gate_there()
    zg = z_gather(2, w_gate.at[:, s], slab(w_gate))
    up_there = swap(4, lambda p: up_own.at[p], lambda p: w_up.at[p, s])
    slices(down_rows, None, down_own)
    make_places(order, lengths, place_q, place_k)
    n1_there()
    zo[0]()
    zq[0]()
    down_there = swap(5, lambda p: down_own.at[p], lambda p: w_down.at[p, s])
    cot_there = gather(2, cot_own, cot_all)
    n1_here = load([(n1_all, norm_v)], load_sem, 0)
    up_there()
    zu = z_gather(3, w_up.at[:, s], slab(w_up))
    k_there()
    v_there()
    kv_here = load([(k_all, k_v), (v_all, v_v)], load_sem, 1)
    zq[1]()
    wq_here = load([(w_q, wq_v)], load_sem, 3)
    down_there()
    zd = z_gather(4, w_down.at[:, s], slab(w_down))
    n1_here()
    wq_here()

    @pl.loop(0, tiles)
    def _(i):
        rows = pl.ds(pl.multiple_of(i * step, step), step)
        part = norm_v[pl.ds(i * (step // local), step // local)].reshape(step, width)
        query[rows, :] = dot(part, wq_v[...].reshape(width, wide), ((1,), (0,))).astype(BF16)

    cot_there()
    cot_here = load([(cot_all, cot_v)], load_sem, 0)
    kv_here()
    zo[1]()
    mine.wait()
    wo_here = load([(w_o, wo_v)], load_sem, 3)

    scale = 1.0 / math.sqrt(HEAD_DIM)
    for head in range(wide // HEAD_DIM):
        cols = slice(head * HEAD_DIM, (head + 1) * HEAD_DIM)

        @pl.loop(0, tiles)
        def _(i):
            rows = pl.ds(pl.multiple_of(i * step, step), step)
            raw = dot(query[rows, cols], k_v[:, :, cols].reshape(group, HEAD_DIM), ((1,), (1,)))
            logits = jnp.where(mask(place_q, place_k, rows), raw * scale, -1e30)
            top = jnp.max(logits, axis=-1, keepdims=True)
            expo = jnp.exp(logits - top)
            norm = jnp.sum(expo, axis=-1, keepdims=True)
            probs = (expo * (1.0 / norm)).astype(BF16)
            attended[rows, cols] = dot(
                probs, v_v[:, :, cols].reshape(group, HEAD_DIM), ((1,), (0,))
            ).astype(BF16)
            lse[rows, cols] = jnp.broadcast_to(top + jnp.log(norm), (step, HEAD_DIM))

    wo_here()

    def o_block(i, p):
        rows = pl.ds(pl.multiple_of(p * local, local), local)
        return dot(attended[rows, :], wo_v[...].reshape(wide, width), ((1,), (0,)))

    def o_near(i, p):
        near_out[i] = o_block(i, p).astype(BF16)
        return near_out.at[i]

    o_sum = net.scatter(o_near, o_block, core_in, held, far_in, rs_send.at[0], rs_recv.at[0])
    cot_here()
    hidden = inputs + o_sum()
    hidden_out[...] = hidden
    n2_own[...] = (hidden * rms_scale(hidden)).astype(BF16)
    n2_there = gather(1, n2_own, n2_all)
    zg[0]()
    n2_there()
    n2_here = load([(n2_all, norm_v)], load_sem, 0)
    zg[1]()
    wg_here = load([(w_gate, wg_v)], load_sem, 1)
    zu[0]()
    zu[1]()
    wu_here = load([(w_up, wu_v)], load_sem, 2)
    n2_here()
    wg_here()
    wu_here()

    def matrix(w):
        return w[...].reshape(width, hid)

    @pl.loop(0, tiles)
    def _(i):
        rows = pl.ds(pl.multiple_of(i * step, step), step)
        part = norm_v[pl.ds(i * (step // local), step // local)].reshape(step, width)
        gate = dot(part, matrix(wg_v), ((1,), (0,)))
        up = dot(part, matrix(wu_v), ((1,), (0,)))
        sigma = jax.nn.sigmoid(gate)
        silu = gate * sigma
        act_v[rows, :] = (silu * up).astype(BF16)
        grad_gate[rows, :] = (up * sigma * (1.0 + gate * (1.0 - sigma))).astype(BF16)
        grad_up[rows, :] = silu.astype(BF16)

    fold = width // NH

    def columns(field, i):
        cols = pl.ds(pl.multiple_of(i * fold, fold), fold)
        return field[:, :, cols].reshape(group, fold)

    def term(left, right):
        return dot(left, right, ((0,), (0,))).astype(BF16).reshape(NS, fold // NS, hid)

    @pl.loop(0, NH)
    def _(i):
        down_term[i] = term(columns(cot_v, i), act_v[...])

    z_down = z_scatter(
        net, lambda t: down_term.at[:, t], got_down, comb_down, z_send.at[5], z_recv.at[5]
    )
    z_down[0]()
    z_down[1]()
    zd[0]()
    zd[1]()
    load([(w_down, wd_v)], load_sem, 3)()

    @pl.loop(0, tiles)
    def _(i):
        rows = pl.ds(pl.multiple_of(i * step, step), step)
        part = cot_v[pl.ds(i * (step // local), step // local)].reshape(step, width)
        grad_act = dot(part, matrix(wd_v), ((1,), (0,)))
        grad_gate[rows, :] = (grad_act * grad_gate[rows, :].astype(F32)).astype(BF16)
        grad_up[rows, :] = (grad_act * grad_up[rows, :].astype(F32)).astype(BF16)

    def mixed_block(i, p):
        rows = pl.ds(pl.multiple_of(p * local, local), local)
        return dot(act_v[rows, :], matrix(wd_v), ((1,), (1,)))

    def mixed_near(i, p):
        near_out[i] = mixed_block(i, p).astype(BF16)
        return near_out.at[i]

    mixed_sum = net.scatter(
        mixed_near, mixed_block, core_in, held, far_in, rs_send.at[1], rs_recv.at[1]
    )
    z_down[2](join_v, bufs.at[NS], load_sem)

    @pl.loop(0, NH)
    def _(i):
        part = columns(norm_v, i)
        gate_term[i] = term(part, grad_gate[...])
        up_term[i] = term(part, grad_up[...])

    @pl.loop(0, tiles)
    def _(i):
        rows = pl.ds(pl.multiple_of(i * step, step), step)
        part = dot(grad_gate[rows, :], matrix(wg_v), ((1,), (1,)))
        part = part + dot(grad_up[rows, :], matrix(wu_v), ((1,), (1,)))
        norm_v[pl.ds(i * (step // local), step // local)] = part.astype(BF16).reshape(
            step // local, local, width
        )

    spread_there = load([(norm_v, spread)], load_sem, 5)
    mixed_out[...] = (hidden_out[...] + mixed_sum()).astype(BF16)
    z_down[3](total, bufs, load_sem)
    down_sum[...] = total[...].astype(BF16)
    spread_there()
    for z in (zo, zq, zg, zu, zd):
        z[2]()
    z_down[4]()
    net.close()


def forward_call(q_weight, gate_weight, up_weight, down_rows, gain_one, gain_two, tokens, o_own, keys, values, cot_own, order, lengths):
    local, width = tokens.shape
    group = NH * local
    rows = o_own.shape[0]
    wide, hid = width // NH, gate_weight.shape[1] // NH

    def bf(*shape):
        return jax.ShapeDtypeStruct(shape, BF16)

    out_shape = [
        bf(NH, NS, rows, wide),
        bf(NS, rows, width),
        bf(NH, NS, rows, hid),
        bf(NH, NS, rows, hid),
        bf(NH, NS, rows, hid),
        bf(NH, local, width),
        bf(NH, local, wide),
        bf(NH, local, wide),
        bf(NH, local, width),
        bf(NH, local, width),
        bf(NS, NH, rows, hid),
        bf(NH, rows, hid),
        bf(NH, local, width),
        bf(group, wide),
        bf(group, wide),
        jax.ShapeDtypeStruct((group, wide), F32),
        jax.ShapeDtypeStruct((local, width), F32),
        bf(local, width),
        bf(NH, NS, rows, hid),
        bf(NH, NS, rows, hid),
        bf(NH, rows, hid),
    ]
    dma = pltpu.SemaphoreType.DMA
    vm = pltpu.VMEM
    return pl.pallas_call(
        forward_kernel,
        out_shape=out_shape,
        in_specs=[VMEM] * 7 + [ANY] * 4 + [SMEM] * 2,
        out_specs=[ANY] * 13 + [VMEM] * 8,
        scratch_shapes=[
            vm((NH, rows, wide), BF16),
            vm((group, 2), jnp.int32),
            vm((2, group), jnp.int32),
            vm((NH, NS, rows, wide), BF16),
            vm((NS, rows, width), BF16),
            vm((NH, NS, rows, hid), BF16),
            vm((NH, NS, rows, hid), BF16),
            vm((NH, NS, rows, hid), BF16),
            vm((NH, local, width), BF16),
            vm((NH, local, width), BF16),
            vm((NH, local, wide), BF16),
            vm((NH, local, wide), BF16),
            vm((local, width), BF16),
            vm((local, width), BF16),
            vm((4, local, width), BF16),
            vm((4, local, width), BF16),
            vm((3, local, width), BF16),
            vm((3, local, width), BF16),
            vm((group, hid), BF16),
            vm((group, hid), BF16),
            vm((group, hid), BF16),
            vm((NH, NS, rows, hid), BF16),
            vm((NH, rows, hid), BF16),
            vm((NS + 1, NH, rows, hid), BF16),
            vm((NH, rows, hid), F32),
            dma((6, 7)),
            dma((6, 7)),
            dma((3, 13)),
            dma((3, 13)),
            dma((2, 7)),
            dma((2, 7)),
            dma((6, 5)),
            dma((6, NS + 1)),
            dma((16,)),
            dma((8,)),
        ],
        compiler_params=pltpu.CompilerParams(
            collective_id=0, has_side_effects=True, vmem_limit_bytes=63 << 20
        ),
        name="forward",
    )(q_weight, gate_weight, up_weight, down_rows, gain_one, gain_two, tokens, o_own, keys, values, cot_own, order, lengths)


def backward_kernel(
    tokens,
    cot_own,
    hidden_in,
    gate_term,
    up_term,
    spread,
    down_sum,
    w_o,
    w_q,
    n1_all,
    query,
    k_all,
    v_all,
    attended,
    lse,
    order,
    lengths,
    d_tokens,
    o_out,
    d_keys,
    d_values,
    q_out,
    gate_out,
    up_out,
    down_out,
    got_ffn,
    comb_ffn,
    got_q,
    comb_q,
    got_o,
    comb_o,
    place_q,
    place_k,
    own_v,
    near_out,
    core_in,
    held,
    far_in,
    dh_v,
    dh_own,
    dh_all,
    n1_v,
    wo_v,
    wq_v,
    q_v,
    k_v,
    v_v,
    att_v,
    lse_v,
    da_v,
    dq_v,
    dk_v,
    dv_v,
    dk_sum,
    dv_sum,
    q_term,
    o_term,
    joins,
    q_join,
    o_join,
    bufs,
    q_bufs,
    o_bufs,
    total,
    results,
    q_total,
    q_result,
    o_total,
    z_send,
    z_recv,
    swap_send,
    swap_recv,
    ag_send,
    ag_recv,
    rs_send,
    rs_recv,
    own,
    load_sem,
):
    net = Net()
    h, s = net.h, net.s
    local, width = tokens.shape
    group = NH * local
    wide = query.shape[1]
    step = 256
    tiles = group // step
    scale = 1.0 / math.sqrt(HEAD_DIM)
    net.greet()

    def swap(j, src, dst):
        return net.swap(src, dst, swap_send.at[j], swap_recv.at[j], own.at[j])

    def scatter(j, source, block):
        return net.scatter(
            source, block, core_in.at[j], held.at[j], far_in.at[j], rs_send.at[j], rs_recv.at[j]
        )

    def z_sum(j, block, got, comb):
        z = z_scatter(net, block, got, comb, z_send.at[j], z_recv.at[j])
        z[0]()
        z[1]()
        return z

    z_gate = z_sum(0, lambda t: gate_term.at[:, t], got_ffn.at[0], comb_ffn.at[0])
    z_up = z_sum(1, lambda t: up_term.at[:, t], got_ffn.at[1], comb_ffn.at[1])
    own_here = [
        load([(spread.at[lax.bitwise_xor(h, k)], own_v.at[i])], load_sem, i)
        for i, k in enumerate((6, 2, 4, 0))
    ]

    def spread_block(i, p):
        own_here[i]()
        return own_v[i].astype(F32)

    ffn_sum = scatter(0, lambda i, p: spread.at[p], spread_block)
    backs = [swap(2, lambda p: down_sum.at[p], lambda p: down_out.at[p])]
    here = load(
        [
            (w_o, wo_v),
            (w_q, wq_v),
            (query, q_v),
            (k_all, k_v),
            (v_all, v_v),
            (attended, att_v),
            (lse, lse_v),
            (n1_all, n1_v),
        ],
        load_sem,
        8,
    )
    make_places(order, lengths, place_q, place_k)
    hidden = hidden_in[...]
    scale_two = rms_scale(hidden)
    normed_two = hidden * scale_two
    here()
    scaled_two = ffn_sum()
    grad_hidden = cot_own[...].astype(F32) + scale_two * (
        scaled_two - normed_two * jnp.mean(scaled_two * normed_two, axis=-1, keepdims=True)
    )
    dh_v[...] = grad_hidden
    dh_own[...] = grad_hidden.astype(BF16)
    dh_there = net.gather(dh_own, dh_all, ag_send, ag_recv, own.at[8])
    z_gate[2](joins.at[0], bufs.at[NS], load_sem)
    dh_there()

    @pl.loop(0, tiles)
    def _(i):
        rows = pl.ds(pl.multiple_of(i * step, step), step)
        part = dh_all[pl.ds(i * (step // local), step // local)].reshape(step, width)
        da_v[rows, :] = dot(part, wo_v[...].reshape(wide, width), ((1,), (1,))).astype(BF16)

    for head in range(wide // HEAD_DIM):
        cols = slice(head * HEAD_DIM, (head + 1) * HEAD_DIM)
        dk_sum[...] = jnp.zeros_like(dk_sum)
        dv_sum[...] = jnp.zeros_like(dv_sum)

        @pl.loop(0, tiles)
        def _(i):
            rows = pl.ds(pl.multiple_of(i * step, step), step)
            keys = k_v[:, :, cols].reshape(group, HEAD_DIM)
            part, grad = q_v[rows, cols], da_v[rows, cols]
            raw = dot(part, keys, ((1,), (1,)))
            logits = jnp.where(mask(place_q, place_k, rows), raw * scale, -1e30)
            probs = jnp.exp(logits - lse_v[rows, cols][:, :1])
            grad_probs = dot(grad, v_v[:, :, cols].reshape(group, HEAD_DIM), ((1,), (1,)))
            inner = jnp.sum(probs * grad_probs, axis=-1, keepdims=True)
            grad_raw = (probs * (grad_probs - inner) * scale).astype(BF16)
            dq_v[rows, cols] = dot(grad_raw, keys, ((1,), (0,))).astype(BF16)
            dk_sum[...] += dot(grad_raw, part, ((0,), (0,)))
            dv_sum[...] += dot(probs.astype(BF16), grad, ((0,), (0,)))

        dk_v[:, :, cols] = dk_sum[...].astype(BF16).reshape(NH, local, HEAD_DIM)
        dv_v[:, :, cols] = dv_sum[...].astype(BF16).reshape(NH, local, HEAD_DIM)

    z_up[2](joins.at[1], bufs.at[NS], load_sem)

    def q_block(i, p):
        rows = pl.ds(pl.multiple_of(p * local, local), local)
        return dot(dq_v[rows, :], wq_v[...].reshape(width, wide), ((1,), (1,)))

    def q_near(i, p):
        near_out[i] = q_block(i, p).astype(BF16)
        return near_out.at[i]

    q_sum = scatter(1, q_near, q_block)
    fold = width // NH

    @pl.loop(0, NH)
    def _(i):
        cols = pl.ds(pl.multiple_of(i * fold, fold), fold)
        part = dot(n1_v[:, :, cols].reshape(group, fold), dq_v[...], ((0,), (0,)))
        q_term[i] = part.astype(BF16).reshape(NS, fold // NS, wide)

    zq = z_sum(2, lambda t: q_term.at[:, t], got_q, comb_q)

    @pl.loop(0, NH)
    def _(i):
        cols = pl.ds(pl.multiple_of(i * fold, fold), fold)
        part = dot(att_v[...], dh_all[:, :, cols].reshape(group, fold), ((0,), (0,)))
        o_term[:, :, cols] = part.astype(BF16).reshape(NS, wide // NS, fold)

    zo = z_sum(3, lambda t: o_term.at[t], got_o, comb_o)
    backs.append(swap(0, lambda p: dk_v.at[p], lambda p: lane_block(d_keys, p, wide)))
    backs.append(swap(1, lambda p: dv_v.at[p], lambda p: lane_block(d_values, p, wide)))
    z_gate[3](total, bufs, load_sem)
    results[0] = total[...].astype(BF16)
    backs.append(swap(3, lambda p: results.at[0, p], lambda p: gate_out.at[p]))

    inputs = tokens[...].astype(F32)
    scale_one = rms_scale(inputs)
    normed_one = inputs * scale_one
    scaled_one = q_sum()
    d_tokens[...] = (
        dh_v[...]
        + scale_one
        * (scaled_one - normed_one * jnp.mean(scaled_one * normed_one, axis=-1, keepdims=True))
    ).astype(BF16)
    zq[2](q_join, q_bufs.at[NS], load_sem)
    zo[2](o_join, o_bufs.at[NS], load_sem)
    z_up[3](total, bufs, load_sem)
    results[1] = total[...].astype(BF16)
    backs.append(swap(4, lambda p: results.at[1, p], lambda p: up_out.at[p]))
    zq[3](q_total, q_bufs, load_sem)
    q_result[...] = q_total[...].astype(BF16)
    backs.append(swap(5, lambda p: q_result.at[p], lambda p: lane_block(q_out, p, wide)))
    zo[3](o_total, o_bufs, load_sem)
    o_out[...] = o_total[...]
    for back in backs:
        back()
    for z in (z_gate, z_up, zq, zo):
        z[4]()
    net.close()


def backward_call(tokens, cot_own, hidden, gate_term, up_term, spread, down_sum, w_o, w_q, n1_all, query, k_all, v_all, attended, lse, order, lengths):
    local, width = tokens.shape
    group = NH * local
    rows, wide, hid = w_q.shape[2], w_q.shape[3], gate_term.shape[3]

    def bf(*shape):
        return jax.ShapeDtypeStruct(shape, BF16)

    out_shape = [
        bf(local, width),
        jax.ShapeDtypeStruct((rows, width), F32),
        bf(local, width),
        bf(local, width),
        bf(rows, width),
        bf(NH, rows, hid),
        bf(NH, rows, hid),
        bf(NH, rows, hid),
        bf(2, NS, NH, rows, hid),
        bf(2, NH, rows, hid),
        bf(NS, NH, rows, wide),
        bf(NH, rows, wide),
        bf(NS, rows, width),
        bf(rows, width),
    ]
    dma = pltpu.SemaphoreType.DMA
    vm = pltpu.VMEM
    return pl.pallas_call(
        backward_kernel,
        out_shape=out_shape,
        in_specs=[VMEM] * 3 + [ANY] * 12 + [SMEM] * 2,
        out_specs=[VMEM] * 2 + [ANY] * 12,
        scratch_shapes=[
            vm((group, 2), jnp.int32),
            vm((2, group), jnp.int32),
            vm((4, local, width), BF16),
            vm((4, local, width), BF16),
            vm((2, 4, local, width), BF16),
            vm((2, 3, local, width), BF16),
            vm((2, 3, local, width), BF16),
            vm((local, width), F32),
            vm((local, width), BF16),
            vm((NH, local, width), BF16),
            vm((NH, local, width), BF16),
            vm((NS, rows, width), BF16),
            vm((NH, NS, rows, wide), BF16),
            vm((group, wide), BF16),
            vm((NH, local, wide), BF16),
            vm((NH, local, wide), BF16),
            vm((group, wide), BF16),
            vm((group, wide), F32),
            vm((group, wide), BF16),
            vm((group, wide), BF16),
            vm((NH, local, wide), BF16),
            vm((NH, local, wide), BF16),
            vm((group, HEAD_DIM), F32),
            vm((group, HEAD_DIM), F32),
            vm((NH, NS, rows, wide), BF16),
            vm((NS, rows, width), BF16),
            vm((2, NH, rows, hid), BF16),
            vm((NH, rows, wide), BF16),
            vm((rows, width), BF16),
            vm((NS + 1, NH, rows, hid), BF16),
            vm((NS + 1, NH, rows, wide), BF16),
            vm((NS + 1, rows, width), BF16),
            vm((NH, rows, hid), F32),
            vm((2, NH, rows, hid), BF16),
            vm((NH, rows, wide), F32),
            vm((NH, rows, wide), BF16),
            vm((rows, width), F32),
            dma((4, 5)),
            dma((4, NS + 1)),
            dma((6, 7)),
            dma((6, 7)),
            dma((13,)),
            dma((13,)),
            dma((2, 7)),
            dma((2, 7)),
            dma((9,)),
            dma((16,)),
        ],
        compiler_params=pltpu.CompilerParams(
            collective_id=1, has_side_effects=True, vmem_limit_bytes=62 << 20
        ),
        name="backward",
    )(tokens, cot_own, hidden, gate_term, up_term, spread, down_sum, w_o, w_q, n1_all, query, k_all, v_all, attended, lse, order, lengths)


def per_device(
    nh,
    ns,
    tokens,
    keys,
    values,
    q_weight,
    o_weight,
    gate_weight,
    up_weight,
    down_weight,
    attn_gain,
    ffn_gain,
    span_order,
    doc_lengths,
    cotangent,
):
    gain_one = attn_gain.astype(F32)[:, None]
    gain_two = ffn_gain.astype(F32)[:, None]
    (
        w_q, w_o, _, _, _, n1_all, k_all, v_all, _, _, _, _, spread,
        query, attended, lse, hidden, mixed_out, gate_term, up_term, down_sum,
    ) = forward_call(
        q_weight,
        gate_weight,
        up_weight,
        down_weight.T,
        gain_one,
        gain_two,
        tokens,
        o_weight,
        keys,
        values,
        cotangent,
        span_order,
        doc_lengths,
    )
    grad_tokens, o_sum, grad_keys, grad_values, q_sum, gate_sum, up_sum, down_sum = backward_call(
        tokens,
        cotangent,
        hidden,
        gate_term,
        up_term,
        spread,
        down_sum,
        w_o,
        w_q,
        n1_all,
        query,
        k_all,
        v_all,
        attended,
        lse,
        span_order,
        doc_lengths,
    )[:8]
    q_sum = q_sum.astype(F32)
    gate_sum = rows_of(gate_sum).astype(F32)
    up_sum = rows_of(up_sum).astype(F32)
    down_sum = rows_of(down_sum).astype(F32)
    grad_gain_one = jnp.sum(q_weight.astype(F32) * q_sum, axis=1)
    grad_gain_two = jnp.sum(
        gate_weight.astype(F32) * gate_sum + up_weight.astype(F32) * up_sum, axis=1
    )
    return (
        mixed_out,
        grad_tokens,
        grad_keys,
        grad_values,
        gain_one * q_sum,
        o_sum,
        gain_two * gate_sum,
        gain_two * up_sum,
        down_sum.T,
        grad_gain_one,
        grad_gain_two,
    )


def to_slices(weight, nh):
    rows, cols = weight.shape
    parts = weight.reshape(rows, nh, cols // nh).swapaxes(0, 1)
    return lax.all_to_all(parts, "head", 0, 0, tiled=False).reshape(nh * rows, cols // nh)


def from_slices(part, nh):
    rows, cols = part.shape
    parts = part.reshape(nh, rows // nh, cols)
    parts = lax.all_to_all(parts, "head", 0, 0, tiled=False)
    return parts.swapaxes(0, 1).reshape(rows // nh, nh * cols)


def gather_seq(part):
    return lax.all_gather(part, "seq", axis=0, tiled=True)


def scatter_seq(full):
    return lax.psum_scatter(full.astype(BF16), "seq", scatter_dimension=0, tiled=True)


def gather_head(part):
    return lax.all_gather(part, "head", axis=0, tiled=True)


def scatter_head(full):
    return lax.psum_scatter(full.astype(BF16), "head", scatter_dimension=0, tiled=True)


def per_device_plain(
    nh,
    ns,
    tokens,
    keys,
    values,
    q_weight,
    o_weight,
    gate_weight,
    up_weight,
    down_weight,
    attn_gain,
    ffn_gain,
    span_order,
    doc_lengths,
    cotangent,
):
    local, width = tokens.shape
    rows = q_weight.shape[0]

    def shuffle(field):
        return field.reshape(local, nh, ns, rows).swapaxes(1, 2).reshape(local, width)

    def unshuffle(field):
        return field.reshape(local, ns, nh, rows).swapaxes(1, 2).reshape(local, width)

    gain_one = attn_gain.astype(F32)[:, None]
    gain_two = ffn_gain.astype(F32)[:, None]
    inputs = tokens.astype(F32)
    scale_one = rms_scale(inputs)
    normed_one = inputs * scale_one
    normed_one_all = gather_head(shuffle(normed_one.astype(BF16)))
    w_q = gather_seq(to_slices((q_weight * gain_one).astype(BF16), nh))
    key_heads = to_slices(keys, nh)
    value_heads = to_slices(values, nh)
    w_o = gather_seq(o_weight)
    w_gate = gather_seq(to_slices((gate_weight * gain_two).astype(BF16), nh))
    w_up = gather_seq(to_slices((up_weight * gain_two).astype(BF16), nh))
    w_down = gather_seq(to_slices(down_weight.T, nh))
    cotangent_all = gather_head(shuffle(cotangent))

    group = normed_one_all.shape[0]
    position, segment = places(span_order[0], doc_lengths[0], group)
    place_q = jnp.stack([position, segment], axis=1)
    place_k = jnp.stack([position, segment], axis=0)

    query = dot(normed_one_all, w_q, ((1,), (0,))).astype(BF16)
    attended, lse = attend(query, key_heads, value_heads, place_q, place_k)
    hidden = inputs + scatter_head(dot(attended, w_o, ((1,), (0,)))).astype(F32)
    scale_two = rms_scale(hidden)
    normed_two = hidden * scale_two
    normed_two_all = gather_head(shuffle(normed_two.astype(BF16)))

    gate = dot(normed_two_all, w_gate, ((1,), (0,)))
    up = dot(normed_two_all, w_up, ((1,), (0,)))
    sigma = jax.nn.sigmoid(gate)
    act = (gate * sigma * up).astype(BF16)
    down_sum = scatter_seq(dot(cotangent_all, act, ((0,), (0,))))
    grad_act = dot(cotangent_all, w_down, ((1,), (0,)))
    grad_gate = (grad_act * up * sigma * (1.0 + gate * (1.0 - sigma))).astype(BF16)
    grad_up = (grad_act * gate * sigma).astype(BF16)
    spread_two = dot(grad_gate, w_gate, ((1,), (1,))) + dot(grad_up, w_up, ((1,), (1,)))
    scaled_two = unshuffle(scatter_head(spread_two)).astype(F32)
    gate_sum = scatter_seq(dot(normed_two_all, grad_gate, ((0,), (0,))))
    up_sum = scatter_seq(dot(normed_two_all, grad_up, ((0,), (0,))))
    mixed = unshuffle(scatter_head(dot(act, w_down, ((1,), (1,)))))
    mixed_out = (hidden + mixed.astype(F32)).astype(BF16)

    grad_hidden = cotangent.astype(F32) + scale_two * (
        scaled_two - normed_two * jnp.mean(scaled_two * normed_two, axis=-1, keepdims=True)
    )
    grad_hidden_all = gather_head(grad_hidden.astype(BF16))
    grad_attended = dot(grad_hidden_all, w_o, ((1,), (1,))).astype(BF16)
    o_sum = scatter_seq(dot(attended, grad_hidden_all, ((0,), (0,))))
    grad_query, grad_keys, grad_values = attend_back(
        query, key_heads, value_heads, grad_attended, lse, place_q, place_k
    )
    grad_keys = from_slices(grad_keys, nh)
    grad_values = from_slices(grad_values, nh)
    scaled_one = unshuffle(scatter_head(dot(grad_query, w_q, ((1,), (1,))))).astype(F32)
    q_sum = scatter_seq(dot(normed_one_all, grad_query, ((0,), (0,))))
    grad_tokens = grad_hidden + scale_one * (
        scaled_one - normed_one * jnp.mean(scaled_one * normed_one, axis=-1, keepdims=True)
    )
    q_sum = from_slices(q_sum, nh).astype(F32)
    gate_sum = from_slices(gate_sum, nh).astype(F32)
    up_sum = from_slices(up_sum, nh).astype(F32)
    down_sum = from_slices(down_sum, nh).astype(F32)
    grad_gain_one = jnp.sum(q_weight.astype(F32) * q_sum, axis=1)
    grad_gain_two = jnp.sum(
        gate_weight.astype(F32) * gate_sum + up_weight.astype(F32) * up_sum, axis=1
    )
    return (
        mixed_out,
        grad_tokens.astype(BF16),
        grad_keys,
        grad_values,
        gain_one * q_sum,
        o_sum.astype(F32),
        gain_two * gate_sum,
        gain_two * up_sum,
        down_sum.T,
        grad_gain_one,
        grad_gain_two,
    )


def solution(mesh):
    both = ("head", "seq")
    nh, ns = mesh.shape["head"], mesh.shape["seq"]
    body = per_device if (nh, ns) == (NH, NS) else per_device_plain
    rows, cols, line, own = P(both, None), P(None, both), P(both), P("seq", None)
    return jax.shard_map(
        functools.partial(body, nh, ns),
        mesh=mesh,
        in_specs=(rows,) * 7 + (cols, line, line, own, own, rows),
        out_specs=(rows,) * 8 + (cols, line, line),
        check_vma=False,
    )
```

```python
import functools
import math

import jax
import jax.numpy as jnp
from jax import lax
from jax.experimental import pallas as pl
from jax.experimental.pallas import tpu as pltpu
from jax.sharding import PartitionSpec as P

HEAD_DIM = 128
NH, NS = 8, 4
EPS = 1e-06
BF16 = jnp.bfloat16
F32 = jnp.float32


def rms_scale(field):
    return lax.rsqrt(jnp.mean(field * field, axis=-1, keepdims=True) + EPS)


def dot(left, right, dims):
    return lax.dot_general(left, right, (dims, ((), ())), preferred_element_type=F32)


def places(order_row, length_row, group):
    count = order_row.shape[0]
    width = group // count
    slots = jnp.arange(group, dtype=jnp.int32)
    which = slots // width
    picked = jnp.where(
        which[:, None] == jnp.arange(count, dtype=jnp.int32)[None, :], order_row[None, :], 0
    )
    position = jnp.sum(picked, axis=1) * width + slots % width
    bounds = jnp.cumsum(length_row)
    segment = jnp.sum((position[:, None] >= bounds[None, :]).astype(jnp.int32), axis=1)
    return (position, segment)


def attend_kernel(q_ref, k_ref, v_ref, place_q, place_k, out_ref, lse_ref):
    scale = 1.0 / math.sqrt(HEAD_DIM)
    raw = dot(q_ref[...], k_ref[...], ((1,), (1,)))
    allowed = (place_q[:, 1:2] == place_k[1:2, :]) & (place_k[0:1, :] <= place_q[:, 0:1])
    logits = jnp.where(allowed, raw * scale, -1e30)
    top = jnp.max(logits, axis=-1, keepdims=True)
    expo = jnp.exp(logits - top)
    total = jnp.sum(expo, axis=-1, keepdims=True)
    probs = expo * (1.0 / total)
    out_ref[...] = dot(probs.astype(BF16), v_ref[...], ((1,), (0,))).astype(BF16)
    lse_ref[...] = jnp.broadcast_to(top + jnp.log(total), lse_ref.shape)


def attend(query, keys, values, place_q, place_k):
    group, width = query.shape
    heads = width // HEAD_DIM
    rows = min(group, 256)
    block = pl.BlockSpec((rows, HEAD_DIM), lambda h, i: (i, h))
    whole = pl.BlockSpec((group, HEAD_DIM), lambda h, i: (0, h))
    return pl.pallas_call(
        attend_kernel,
        grid=(heads, group // rows),
        in_specs=[
            block,
            whole,
            whole,
            pl.BlockSpec((rows, 2), lambda h, i: (i, 0)),
            pl.BlockSpec((2, group), lambda h, i: (0, 0)),
        ],
        out_specs=[block, block],
        out_shape=[
            jax.ShapeDtypeStruct((group, width), BF16),
            jax.ShapeDtypeStruct((group, width), F32),
        ],
        compiler_params=pltpu.CompilerParams(vmem_limit_bytes=48 << 20),
        cost_estimate=pl.CostEstimate(
            flops=4 * group * group * width,
            bytes_accessed=12 * group * width,
            transcendentals=heads * group * group,
        ),
        name="attend",
    )(query, keys, values, place_q, place_k)


def attend_back_kernel(
    q_ref, k_ref, v_ref, do_ref, lse_ref, place_q, place_k, dq_ref, dk_ref, dv_ref, dk_sum, dv_sum
):
    step = pl.program_id(1)
    scale = 1.0 / math.sqrt(HEAD_DIM)
    query, keys, grad = q_ref[...], k_ref[...], do_ref[...]
    raw = dot(query, keys, ((1,), (1,)))
    allowed = (place_q[:, 1:2] == place_k[1:2, :]) & (place_k[0:1, :] <= place_q[:, 0:1])
    logits = jnp.where(allowed, raw * scale, -1e30)
    probs = jnp.exp(logits - lse_ref[:, :1])
    grad_probs = dot(grad, v_ref[...], ((1,), (1,)))
    inner = jnp.sum(probs * grad_probs, axis=-1, keepdims=True)
    grad_raw = (probs * (grad_probs - inner) * scale).astype(BF16)
    dq_ref[...] = dot(grad_raw, keys, ((1,), (0,))).astype(BF16)

    @pl.when(step == 0)
    def _():
        dk_sum[...] = jnp.zeros_like(dk_sum)
        dv_sum[...] = jnp.zeros_like(dv_sum)

    dk_sum[...] += dot(grad_raw, query, ((0,), (0,)))
    dv_sum[...] += dot(probs.astype(BF16), grad, ((0,), (0,)))

    @pl.when(step == pl.num_programs(1) - 1)
    def _():
        dk_ref[...] = dk_sum[...].astype(BF16)
        dv_ref[...] = dv_sum[...].astype(BF16)


def attend_back(query, keys, values, grad, lse, place_q, place_k):
    group, width = query.shape
    heads = width // HEAD_DIM
    rows = min(group, 256)
    block = pl.BlockSpec((rows, HEAD_DIM), lambda h, i: (i, h))
    whole = pl.BlockSpec((group, HEAD_DIM), lambda h, i: (0, h))
    full = jax.ShapeDtypeStruct((group, width), BF16)
    return pl.pallas_call(
        attend_back_kernel,
        grid=(heads, group // rows),
        in_specs=[
            block,
            whole,
            whole,
            block,
            block,
            pl.BlockSpec((rows, 2), lambda h, i: (i, 0)),
            pl.BlockSpec((2, group), lambda h, i: (0, 0)),
        ],
        out_specs=[block, whole, whole],
        out_shape=[full, full, full],
        scratch_shapes=[pltpu.VMEM((group, HEAD_DIM), F32)] * 2,
        compiler_params=pltpu.CompilerParams(vmem_limit_bytes=48 << 20),
        cost_estimate=pl.CostEstimate(
            flops=10 * group * group * width,
            bytes_accessed=18 * group * width,
            transcendentals=heads * group * group,
        ),
        name="attend_back",
    )(query, keys, values, grad, lse, place_q, place_k)


MESH = pl.DeviceIdType.MESH
ANY = pl.BlockSpec(memory_space=pl.ANY)
VMEM = pl.BlockSpec(memory_space=pltpu.VMEM)
SMEM = pl.BlockSpec(memory_space=pltpu.SMEM)
LANES = 128


def slices_of(weight, nh):
    rows, cols = weight.shape
    return weight.reshape(rows, nh, cols // nh).swapaxes(0, 1)


def rows_of(parts):
    nh, rows, cols = parts.shape
    return parts.swapaxes(0, 1).reshape(rows, nh * cols)


def flat(parts):
    return parts.reshape(parts.shape[0] * parts.shape[1], parts.shape[2])


def remote(src, dst, send, recv, to):
    return pltpu.make_async_remote_copy(
        src_ref=src, dst_ref=dst, send_sem=send, recv_sem=recv, device_id=to, device_id_type=MESH
    )


class Net:
    def __init__(self):
        self.h = lax.axis_index("head")
        self.s = lax.axis_index("seq")

    def peer(self, k):
        return (lax.bitwise_xor(self.h, k), self.s)

    def greet(self):
        barrier = pltpu.get_barrier_semaphore()
        for k in range(1, NH):
            pl.semaphore_signal(barrier, inc=1, device_id=self.peer(k), device_id_type=MESH)
        for k in range(1, NS):
            there = (self.h, lax.rem(self.s + k, NS))
            pl.semaphore_signal(barrier, inc=1, device_id=there, device_id_type=MESH)
        pl.semaphore_wait(barrier, NH - 1 + NS - 1)

    def swap(self, src, dst, send, recv, own):
        mine = pltpu.make_async_copy(src(self.h), dst(self.h), own)
        mine.start()
        copies = []
        for k in (6, 2, 4, 1, 5, 3, 7):
            to = self.peer(k)
            copy = remote(src(to[0]), dst(self.h), send.at[k - 1], recv.at[k - 1], to)
            copy.start()
            copies.append(copy)

        def finish():
            for copy in copies:
                copy.wait()
            mine.wait()

        return finish

    def gather(self, src, dst, send, recv, own):
        half = src.shape[0] // 2
        lo, hi = pl.ds(0, half), pl.ds(half, half)
        h, core, px, py = self.h, self.peer(1), self.peer(2), self.peer(4)
        x, y, d = px[0], py[0], lax.bitwise_xor(h, 6)
        mine = pltpu.make_async_copy(src, dst.at[h], own)
        mine.start()

        def put(i, a, b, to):
            copy = remote(a, b, send.at[i], recv.at[i], to)
            copy.start()
            return copy

        xa = put(0, src.at[lo], dst.at[h, lo], px)
        yb = put(1, src.at[hi], dst.at[h, hi], py)
        c0 = put(2, src, dst.at[h], core)
        xb = put(3, src.at[hi], dst.at[h, hi], px)
        ya = put(4, src.at[lo], dst.at[h, lo], py)

        def finish():
            near = [c0]
            xa.wait_recv()
            fy = put(5, dst.at[x, lo], dst.at[x, lo], py)
            near.append(put(6, dst.at[x, lo], dst.at[x, lo], core))
            yb.wait_recv()
            fx = put(7, dst.at[y, hi], dst.at[y, hi], px)
            near.append(put(8, dst.at[y, hi], dst.at[y, hi], core))
            xb.wait_recv()
            near.append(put(9, dst.at[x, hi], dst.at[x, hi], core))
            ya.wait_recv()
            near.append(put(10, dst.at[y, lo], dst.at[y, lo], core))
            fy.wait_recv()
            near.append(put(11, dst.at[d, lo], dst.at[d, lo], core))
            fx.wait_recv()
            near.append(put(12, dst.at[d, hi], dst.at[d, hi], core))
            for copy in near:
                copy.wait_recv()
            mine.wait()
            for copy in [xa, xb, ya, yb, fx, fy] + near:
                copy.wait_send()

        return finish

    def scatter(self, source, block, core_in, held, far_in, send, recv, read):
        core = self.peer(1)
        order = (6, 2, 4, 0)

        def put(i, a, b, to):
            copy = remote(a, b, send.at[i], recv.at[i], to)
            copy.start()
            return copy

        near = [
            put(i, source(i, lax.bitwise_xor(core[0], k)), core_in.at[i], core)
            for i, k in enumerate(order)
        ]
        far = []
        for i, k in enumerate(order):
            value = block(i, lax.bitwise_xor(self.h, k))
            near[i].wait_recv()
            value = value + read(core_in.at[i]).astype(F32)
            if k:
                held[i] = value.astype(BF16)
                far.append(put(4 + i, held.at[i], far_in.at[i], self.peer(k)))

        def finish():
            result = value
            for i in (1, 2, 0):
                far[i].wait_recv()
                result = result + read(far_in.at[i]).astype(F32)
            for copy in near + far:
                copy.wait_send()
            return result

        return finish

    def z_gather(self, src, block, send, recv):
        s = self.s
        steps = (2, -2, 1, -1)

        def there(d):
            return (self.h, s + d)

        def copy(n):
            return remote(src, block(s), send.at[n], recv.at[s], there(steps[n]))

        def valid(d):
            return (s + d >= 0) & (s + d < NS)

        middle = (s == 1) | (s == 2)
        origin = jnp.where(s == 2, 0, NS - 1)
        target = (self.h, NS - 1 - origin)

        def relay():
            return remote(block(origin), block(origin), send.at[4], recv.at[origin], target)

        for n, d in enumerate(steps):

            @pl.when(valid(d))
            def _():
                copy(n).start()

        def forward():
            @pl.when(middle)
            def _():
                relay().wait_recv()
                relay().start()

        def finish():
            for t in range(NS):
                waited = ((s == 2) & (t == 0)) | ((s == 1) & (t == NS - 1))

                @pl.when((s != t) & jnp.logical_not(waited))
                def _():
                    remote(block(t), block(t), send.at[0], recv.at[t], (self.h, s)).wait_recv()

        def drain():
            for n, d in enumerate(steps):

                @pl.when(valid(d))
                def _():
                    copy(n).wait_send()

            @pl.when(middle)
            def _():
                relay().wait_send()

        return forward, finish, drain


def z_scatter(net, block, value, got, comb, join_v, bufs, send, recv, sems):
    s = net.s
    first, last = s == 0, s == NS - 1
    ends = first | last
    middle = jnp.logical_not(ends)
    far = jnp.where(s == 1, NS - 1, 0)
    inner = jnp.where(first, 1, NS - 2)

    def joined():
        return remote(join_v, got.at[s], send.at[0], recv.at[s], (net.h, far))

    def to_join():
        return remote(block(NS - 1 - s), comb, send.at[0], recv.at[NS], (net.h, inner))

    def direct(n, d):
        return remote(block(s + d), got.at[s], send.at[n], recv.at[s], (net.h, s + d))

    steps = ((1, 2, first), (2, -2, last), (3, 1, s < NS - 1), (4, -1, s > 0))

    def start():
        @pl.when(ends)
        def _():
            to_join().start()

        for n, d, where in steps:

            @pl.when(where)
            def _():
                direct(n, d).start()

    def join():
        @pl.when(middle)
        def _():
            to_join().wait_recv()
            copy = pltpu.make_async_copy(comb, join_v, sems.at[7])
            copy.start()
            copy.wait()
            join_v[...] = (join_v[...].astype(F32) + value(far).astype(F32)).astype(BF16)
            joined().start()

    def finish(total):
        total[...] = value(s).astype(F32)

        def comes(t):
            return (s != t) & (s + t != NS - 1) if t in (0, NS - 1) else (s != t)

        def slot(t):
            return jnp.minimum(jnp.where(s < t, t - 1, t), NS - 2)

        def take(t):
            return pltpu.make_async_copy(got.at[t], bufs.at[slot(t)], sems.at[3 + t])

        for t in range(NS):

            @pl.when(comes(t))
            def _():
                remote(got.at[t], got.at[t], send.at[0], recv.at[t], (net.h, s)).wait_recv()
                take(t).start()

        for t in range(NS):

            @pl.when(comes(t))
            def _():
                take(t).wait()
                total[...] += bufs[pl.ds(slot(t), 1)].reshape(bufs.shape[1:]).astype(F32)

    def drain():
        @pl.when(ends)
        def _():
            to_join().wait_send()

        for n, d, where in steps:

            @pl.when(where)
            def _():
                direct(n, d).wait_send()

        @pl.when(middle)
        def _():
            joined().wait_send()

    return start, join, finish, drain


def make_places(order, lengths, place_q, place_k):
    group, count = place_q.shape[0], order.shape[1]
    width = group // count
    for shape, dim in (((group, 1), 0), ((1, group), 1)):
        slots = lax.broadcasted_iota(jnp.int32, shape, dim)
        position = slots
        for c in range(count):
            inside = (slots >= c * width) & (slots < (c + 1) * width)
            position = jnp.where(inside, slots + (order[0, c] - c) * width, position)
        segment = jnp.zeros(shape, jnp.int32)
        bound = 0
        for j in range(lengths.shape[1]):
            bound = bound + lengths[0, j]
            segment = segment + (position >= bound).astype(jnp.int32)
        if dim == 0:
            place_q[:, 0:1] = position
            place_q[:, 1:2] = segment
        else:
            place_k[0:1, :] = position
            place_k[1:2, :] = segment


def mask(place_q, place_k, rows):
    return (place_q[rows, 1:2] == place_k[1:2, :]) & (place_k[0:1, :] <= place_q[rows, 0:1])


def lane_block(w, p, wide):
    return w.at[:, pl.ds(pl.multiple_of(p * wide, wide), wide)]


def load(pairs, sems, base):
    copies = [pltpu.make_async_copy(a, b, sems.at[base + i]) for i, (a, b) in enumerate(pairs)]
    for copy in copies:
        copy.start()

    def finish():
        for copy in copies:
            copy.wait()

    return finish


def layer_kernel(
    q_weight,
    gate_weight,
    up_weight,
    down_rows,
    gain_one,
    gain_two,
    tokens,
    o_own,
    keys,
    values,
    cot_own,
    order,
    lengths,
    mixed_out,
    d_tokens,
    o_out,
    d_keys,
    d_values,
    q_out,
    gate_out,
    up_out,
    down_out,
    down_tail_out,
    pair_tail_out,
    n1_all,
    hidden_all,
    mixed_near,
    mixed_far,
    got_ffn,
    comb_ffn,
    got_q,
    comb_q,
    got_o,
    comb_o,
    got_dt,
    comb_dt,
    got_pt,
    comb_pt,
    place_q,
    place_k,
    q_own,
    parts,
    tails_own,
    tails_in,
    tails,
    wq_v,
    wo_v,
    wg_v,
    wu_v,
    wd_v,
    norm_v,
    wide_v,
    k_v,
    v_v,
    query,
    attended,
    lse,
    norm_own,
    hidden_v,
    near_out,
    core_in,
    held,
    far_in,
    act_v,
    grad_gate,
    grad_up,
    down_term,
    stage,
    stage_two,
    down_tail,
    pair_tail,
    dq_v,
    dk_sum,
    dv_sum,
    joins,
    q_join,
    o_join,
    dt_join,
    pt_join,
    bufs,
    q_bufs,
    o_bufs,
    dt_bufs,
    pt_bufs,
    total,
    q_total,
    dt_total,
    pt_total,
    dt_back,
    pt_back,
    swap_send,
    swap_recv,
    ag_send,
    ag_recv,
    rs_send,
    rs_recv,
    zg_send,
    zg_recv,
    zs_send,
    zs_recv,
    own,
    load_sem,
):
    net = Net()
    h, s = net.h, net.s
    local, width = tokens.shape
    group = NH * local
    wide, hid = query.shape[1], act_v.shape[1]
    main = parts.shape[3]
    rest = hid - main
    step = 256
    tiles = group // step
    fold = width // NH
    scale = 1.0 / math.sqrt(HEAD_DIM)
    body = pl.ds(0, main)
    net.greet()

    def swap(j, src, dst):
        return net.swap(src, dst, swap_send.at[j], swap_recv.at[j], own.at[j])

    def gather(j, src, dst):
        return net.gather(src, dst, ag_send.at[j], ag_recv.at[j], own.at[20 + j])

    def z_gather(j, src, block):
        return net.z_gather(src, block, zg_send.at[j], zg_recv.at[j])

    def slab(w):
        return lambda t: w.at[:, t, :, body]

    def tile_rows(i):
        return pl.ds(pl.multiple_of(i * step, step), step)

    def token_tile(field, i):
        return field[pl.ds(i * (step // local), step // local)].reshape(step, width)

    def own_rows(p):
        return pl.ds(pl.multiple_of(p * local, local), local)

    zo = z_gather(0, o_own, lambda t: wo_v.at[t])
    o_here = load([(o_own, wo_v.at[s])], load_sem, 0)
    field = (q_weight[...].astype(F32) * gain_one[...]).astype(BF16)
    for p in range(NH):
        q_own[p] = field[:, p * wide : (p + 1) * wide]
    q_there = swap(0, lambda p: q_own.at[p], lambda p: wq_v.at[p, s])
    ffn = ((gate_weight, gain_two), (up_weight, gain_two), (down_rows, None))
    ffn_v = (wg_v, wu_v, wd_v)

    def slices(j):
        weight, gain = ffn[j]
        field = weight[...]
        if gain is not None:
            field = (field.astype(F32) * gain[...]).astype(BF16)
        for p in range(NH):
            parts[j, p] = field[:, p * hid : p * hid + main]
            tails_own[p, :, j * LANES : j * LANES + rest] = field[:, p * hid + main : (p + 1) * hid]
        return swap(
            1 + j, lambda p: parts.at[j, p], lambda p: ffn_v[j].at[p, s, :, body]
        )

    gate_there = slices(0)
    inputs = tokens[...].astype(F32)
    norm_own[...] = (inputs * rms_scale(inputs)).astype(BF16)
    n1_there = gather(0, norm_own, n1_all)
    q_there()
    zq = z_gather(1, wq_v.at[:, s], lambda t: wq_v.at[:, t])
    up_there = slices(1)
    k_there = swap(5, lambda p: lane_block(keys, p, wide), lambda p: k_v.at[p])
    v_there = swap(6, lambda p: lane_block(values, p, wide), lambda p: v_v.at[p])
    down_there = slices(2)
    tails_there = swap(4, lambda p: tails_own.at[p], lambda p: tails_in.at[p])
    gate_there()
    zg = z_gather(2, wg_v.at[:, s, :, body], slab(wg_v))
    make_places(order, lengths, place_q, place_k)
    n1_there()
    n1_here = load([(n1_all, norm_v)], load_sem, 1)
    tails_there()
    for j in range(3):
        for p in range(NH):
            at = (j * NH + p) * rest
            tails[s, :, at : at + rest] = tails_in[p, :, j * LANES : j * LANES + rest]
    zt = z_gather(3, tails.at[s], lambda t: tails.at[t])
    zo[0]()
    zq[0]()
    cot_there = gather(1, cot_own, wide_v)
    up_there()
    zu = z_gather(4, wu_v.at[:, s, :, body], slab(wu_v))
    down_there()
    zd = z_gather(5, wd_v.at[:, s, :, body], slab(wd_v))
    zq[1]()
    n1_here()

    @pl.loop(0, tiles)
    def _(i):
        query[tile_rows(i), :] = dot(
            token_tile(norm_v, i), wq_v[...].reshape(width, wide), ((1,), (0,))
        ).astype(BF16)

    cot_there()
    k_there()
    v_there()
    zt[0]()

    for head in range(wide // HEAD_DIM):
        cols = slice(head * HEAD_DIM, (head + 1) * HEAD_DIM)

        @pl.loop(0, tiles)
        def _(i):
            rows = tile_rows(i)
            raw = dot(query[rows, cols], k_v[:, :, cols].reshape(group, HEAD_DIM), ((1,), (1,)))
            logits = jnp.where(mask(place_q, place_k, rows), raw * scale, -1e30)
            top = jnp.max(logits, axis=-1, keepdims=True)
            expo = jnp.exp(logits - top)
            norm = jnp.sum(expo, axis=-1, keepdims=True)
            probs = (expo * (1.0 / norm)).astype(BF16)
            attended[rows, cols] = dot(
                probs, v_v[:, :, cols].reshape(group, HEAD_DIM), ((1,), (0,))
            ).astype(BF16)
            lse[rows, head : head + 1] = top + jnp.log(norm)

    zg[0]()
    zo[1]()
    o_here()

    def near(block):
        def source(i, p):
            near_out[i] = block(i, p).astype(BF16)
            return near_out.at[i]

        return source

    def scatter(j, block, core=core_in, far=far_in, read=lambda ref: ref[...]):
        return net.scatter(near(block), block, core, held, far, rs_send.at[j], rs_recv.at[j], read)

    def o_block(i, p):
        return dot(attended[own_rows(p), :], wo_v[...].reshape(wide, width), ((1,), (0,)))

    o_sum = scatter(0, o_block)
    hidden = tokens[...].astype(F32) + o_sum()
    hidden_v[...] = hidden
    save = load([(hidden_v, hidden_all)], load_sem, 1)
    norm_own[...] = (hidden * rms_scale(hidden)).astype(BF16)
    n2_there = gather(2, norm_own, norm_v)
    zt[1]()

    def matrix(w):
        return w[...].reshape(width, hid)

    def add_tail(j):
        for p in range(NH):
            at = (j * NH + p) * rest
            ffn_v[j][p, :, :, main:hid] = tails[:, :, at : at + rest]

    zg[1]()
    add_tail(0)
    zu[0]()
    n2_there()
    zu[1]()
    add_tail(1)

    @pl.loop(0, tiles)
    def _(i):
        rows = tile_rows(i)
        part = token_tile(norm_v, i)
        gate = dot(part, matrix(wg_v), ((1,), (0,)))
        up = dot(part, matrix(wu_v), ((1,), (0,)))
        sigma = jax.nn.sigmoid(gate)
        silu = gate * sigma
        act_v[rows, :] = (silu * up).astype(BF16)
        grad_gate[rows, :] = (up * sigma * (1.0 + gate * (1.0 - sigma))).astype(BF16)
        grad_up[rows, :] = silu.astype(BF16)

    def columns(field, i):
        cols = pl.ds(pl.multiple_of(i * fold, fold), fold)
        return field[:, :, cols].reshape(group, fold)

    def put_term(i, left, right, body_ref, tail_ref):
        value = dot(left, right, ((0,), (0,))).astype(BF16)
        body_ref[i, :, :, body] = value[:, :main].reshape(NS, fold // NS, main)
        tail_ref[i, :, 0:rest] = value[:, main:]

    def pack(tail_ref, out, base):
        for p in range(NH):
            at = (base * NH + p) * rest
            out[:, :, at : at + rest] = tail_ref[p, :, 0:rest].reshape(NS, fold // NS, rest)

    @pl.loop(0, NH)
    def _(i):
        put_term(i, columns(wide_v, i), act_v[...], down_term, stage)

    pack(stage, down_tail, 0)

    def z_sum(j, block, value, got, comb, join, buf):
        z = z_scatter(net, block, value, got, comb, join, buf, zs_send.at[j], zs_recv.at[j], load_sem)
        z[0]()
        return z

    def slab_value(w):
        return lambda t: w[:, pl.ds(t, 1), :, body].reshape(NH, fold // NS, main)

    def block_value(w):
        return lambda t: w[pl.ds(t, 1)].reshape(w.shape[1:])

    z_down = z_sum(
        0, slab(down_term), slab_value(down_term), got_ffn.at[0], comb_ffn.at[0], joins.at[0], bufs
    )
    z_dt = z_sum(
        1, lambda t: down_tail.at[t], block_value(down_tail), got_dt, comb_dt, dt_join, dt_bufs
    )
    zd[0]()
    zd[1]()
    add_tail(2)

    @pl.loop(0, tiles)
    def _(i):
        rows = tile_rows(i)
        grad_act = dot(token_tile(wide_v, i), matrix(wd_v), ((1,), (0,)))
        grad_gate[rows, :] = (grad_act * grad_gate[rows, :].astype(F32)).astype(BF16)
        grad_up[rows, :] = (grad_act * grad_up[rows, :].astype(F32)).astype(BF16)

    def spread_block(i, p):
        rows = own_rows(p)
        value = dot(grad_gate[rows, :], matrix(wg_v), ((1,), (1,)))
        return value + dot(grad_up[rows, :], matrix(wu_v), ((1,), (1,)))

    ffn_sum = scatter(1, spread_block)
    z_down[1]()
    z_dt[1]()
    for z in (zo, zq, zt, zg, zu, zd):
        z[2]()

    @pl.loop(0, NH)
    def _(i):
        put_term(i, columns(norm_v, i), grad_gate[...], wg_v, stage)
        put_term(i, columns(norm_v, i), grad_up[...], wu_v, stage_two)

    z_gate = z_sum(
        2, slab(wg_v), slab_value(wg_v), got_ffn.at[1], comb_ffn.at[1], joins.at[1], bufs
    )
    pack(stage, pair_tail, 0)
    pack(stage_two, pair_tail, 1)
    z_pt = z_sum(
        3, lambda t: pair_tail.at[t], block_value(pair_tail), got_pt, comb_pt, pt_join, pt_bufs
    )
    z_up = z_sum(4, slab(wu_v), slab_value(wu_v), got_ffn.at[2], comb_ffn.at[2], joins.at[0], bufs)
    n1_here = load([(n1_all, norm_v)], load_sem, 0)

    hidden = hidden_v[...]
    scale_two = rms_scale(hidden)
    normed_two = hidden * scale_two
    scaled_two = ffn_sum()
    grad_hidden = cot_own[...].astype(F32) + scale_two * (
        scaled_two - normed_two * jnp.mean(scaled_two * normed_two, axis=-1, keepdims=True)
    )
    save()
    hidden_v[...] = grad_hidden
    norm_own[...] = grad_hidden.astype(BF16)
    dh_there = gather(3, norm_own, wide_v)
    backs = []

    def back(j, z, out, result):
        z[2](total)
        result[...] = total[...].astype(BF16)
        backs.append(swap(j, lambda p: result.at[p], lambda p: out.at[p]))

    back(7, z_down, down_out, parts.at[2])
    z_dt[2](dt_total)
    for p in range(NH):
        dt_back[p, :, 0:rest] = dt_total[:, p * rest : (p + 1) * rest].astype(BF16)
    backs.append(swap(8, lambda p: dt_back.at[p], lambda p: down_tail_out.at[p]))
    z_down[3]()
    z_gate[1]()
    z_pt[1]()
    dh_there()

    @pl.loop(0, tiles)
    def _(i):
        dq_v[tile_rows(i), :] = dot(
            token_tile(wide_v, i), wo_v[...].reshape(wide, width), ((1,), (1,))
        ).astype(BF16)

    for head in range(wide // HEAD_DIM):
        cols = slice(head * HEAD_DIM, (head + 1) * HEAD_DIM)
        dk_sum[...] = jnp.zeros_like(dk_sum)
        dv_sum[...] = jnp.zeros_like(dv_sum)

        @pl.loop(0, tiles)
        def _(i):
            rows = tile_rows(i)
            key_rows = k_v[:, :, cols].reshape(group, HEAD_DIM)
            part, grad = query[rows, cols], dq_v[rows, cols]
            raw = dot(part, key_rows, ((1,), (1,)))
            logits = jnp.where(mask(place_q, place_k, rows), raw * scale, -1e30)
            probs = jnp.exp(logits - lse[rows, head : head + 1])
            grad_probs = dot(grad, v_v[:, :, cols].reshape(group, HEAD_DIM), ((1,), (1,)))
            inner = jnp.sum(probs * grad_probs, axis=-1, keepdims=True)
            grad_raw = (probs * (grad_probs - inner) * scale).astype(BF16)
            dq_v[rows, cols] = dot(grad_raw, key_rows, ((1,), (0,))).astype(BF16)
            dk_sum[...] += dot(grad_raw, part, ((0,), (0,)))
            dv_sum[...] += dot(probs.astype(BF16), grad, ((0,), (0,)))

        k_v[:, :, cols] = dk_sum[...].astype(BF16).reshape(NH, local, HEAD_DIM)
        v_v[:, :, cols] = dv_sum[...].astype(BF16).reshape(NH, local, HEAD_DIM)

    def q_block(i, p):
        return dot(dq_v[own_rows(p), :], wq_v[...].reshape(width, wide), ((1,), (1,)))

    q_sum = scatter(2, q_block)
    n1_here()

    @pl.loop(0, NH)
    def _(i):
        part = dot(columns(norm_v, i), dq_v[...], ((0,), (0,)))
        wq_v[i] = part.astype(BF16).reshape(NS, fold // NS, wide)

    zq_sum = z_sum(
        5,
        lambda t: wq_v.at[:, t],
        lambda t: wq_v[:, pl.ds(t, 1)].reshape(NH, fold // NS, wide),
        got_q,
        comb_q,
        q_join,
        q_bufs,
    )

    @pl.loop(0, NH)
    def _(i):
        cols = pl.ds(pl.multiple_of(i * fold, fold), fold)
        part = dot(attended[...], columns(wide_v, i), ((0,), (0,)))
        wo_v[:, :, cols] = part.astype(BF16).reshape(NS, wide // NS, fold)

    zo_sum = z_sum(6, lambda t: wo_v.at[t], block_value(wo_v), got_o, comb_o, o_join, o_bufs)
    backs.append(swap(9, lambda p: k_v.at[p], lambda p: lane_block(d_keys, p, wide)))
    backs.append(swap(10, lambda p: v_v.at[p], lambda p: lane_block(d_values, p, wide)))
    z_up[1]()
    back(11, z_gate, gate_out, parts.at[0])

    inputs = tokens[...].astype(F32)
    scale_one = rms_scale(inputs)
    normed_one = inputs * scale_one
    scaled_one = q_sum()
    d_tokens[...] = (
        hidden_v[...]
        + scale_one
        * (scaled_one - normed_one * jnp.mean(scaled_one * normed_one, axis=-1, keepdims=True))
    ).astype(BF16)

    back_here = load([(hidden_all, hidden_v)], load_sem, 1)

    def mixed_block(i, p):
        return dot(act_v[own_rows(p), :], matrix(wd_v), ((1,), (1,)))

    def staged(ref):
        load([(ref, norm_own)], load_sem, 2)()
        return norm_own[...]

    mixed_sum = scatter(3, mixed_block, mixed_near, mixed_far, staged)
    zq_sum[1]()
    zo_sum[1]()
    back(12, z_up, up_out, parts.at[1])
    z_pt[2](pt_total)
    for j in range(2):
        for p in range(NH):
            at = (j * NH + p) * rest
            pt_back[p, :, j * LANES : j * LANES + rest] = pt_total[:, at : at + rest].astype(BF16)
    backs.append(swap(13, lambda p: pt_back.at[p], lambda p: pair_tail_out.at[p]))
    back_here()
    mixed_out[...] = (hidden_v[...] + mixed_sum()).astype(BF16)
    zq_sum[2](q_total)
    q_own[...] = q_total[...].astype(BF16)
    backs.append(swap(14, lambda p: q_own.at[p], lambda p: lane_block(q_out, p, wide)))
    zo_sum[2](o_out)
    for done in backs:
        done()
    for z in (z_dt, z_gate, z_pt, z_up, zq_sum, zo_sum):
        z[3]()


def layer_call(q_weight, gate_weight, up_weight, down_rows, gain_one, gain_two, tokens, o_own, keys, values, cot_own, order, lengths):
    local, width = tokens.shape
    group = NH * local
    rows = o_own.shape[0]
    wide, hid = width // NH, gate_weight.shape[1] // NH
    main = hid // LANES * LANES
    rest = hid - main

    def bf(*shape):
        return jax.ShapeDtypeStruct(shape, BF16)

    def vm(*shape, dtype=BF16):
        return pltpu.VMEM(shape, dtype)

    out_shape = [
        bf(local, width),
        bf(local, width),
        jax.ShapeDtypeStruct((rows, width), F32),
        bf(local, width),
        bf(local, width),
        bf(rows, width),
        bf(NH, rows, main),
        bf(NH, rows, main),
        bf(NH, rows, main),
        bf(NH, rows, LANES),
        bf(NH, rows, 2 * LANES),
        bf(NH, local, width),
        jax.ShapeDtypeStruct((local, width), F32),
        bf(4, local, width),
        bf(3, local, width),
        bf(3, NS, NH, rows, main),
        bf(3, NH, rows, main),
        bf(NS, NH, rows, wide),
        bf(NH, rows, wide),
        bf(NS, rows, width),
        bf(rows, width),
        bf(NS, rows, NH * rest),
        bf(rows, NH * rest),
        bf(NS, rows, 2 * NH * rest),
        bf(rows, 2 * NH * rest),
    ]
    dma = pltpu.SemaphoreType.DMA
    return pl.pallas_call(
        layer_kernel,
        out_shape=out_shape,
        in_specs=[VMEM] * 7 + [ANY] * 3 + [VMEM] + [SMEM] * 2,
        out_specs=[VMEM] * 3 + [ANY] * 22,
        scratch_shapes=[
            vm(group, 2, dtype=jnp.int32),
            vm(2, group, dtype=jnp.int32),
            vm(NH, rows, wide),
            vm(3, NH, rows, main),
            vm(NH, rows, 3 * LANES),
            vm(NH, rows, 3 * LANES),
            vm(NS, rows, 3 * NH * rest),
            vm(NH, NS, rows, wide),
            vm(NS, rows, width),
            vm(NH, NS, rows, hid),
            vm(NH, NS, rows, hid),
            vm(NH, NS, rows, hid),
            vm(NH, local, width),
            vm(NH, local, width),
            vm(NH, local, wide),
            vm(NH, local, wide),
            vm(group, wide),
            vm(group, wide),
            vm(group, wide // HEAD_DIM, dtype=F32),
            vm(local, width),
            vm(local, width, dtype=F32),
            vm(4, local, width),
            vm(4, local, width),
            vm(3, local, width),
            vm(3, local, width),
            vm(group, hid),
            vm(group, hid),
            vm(group, hid),
            vm(NH, NS, rows, main),
            vm(NH, NS * rows, LANES),
            vm(NH, NS * rows, LANES),
            vm(NS, rows, NH * rest),
            vm(NS, rows, 2 * NH * rest),
            vm(group, wide),
            vm(group, HEAD_DIM, dtype=F32),
            vm(group, HEAD_DIM, dtype=F32),
            vm(2, NH, rows, main),
            vm(NH, rows, wide),
            vm(rows, width),
            vm(rows, NH * rest),
            vm(rows, 2 * NH * rest),
            vm(3, NH, rows, main),
            vm(3, NH, rows, wide),
            vm(3, rows, width),
            vm(3, rows, NH * rest),
            vm(3, rows, 2 * NH * rest),
            vm(NH, rows, main, dtype=F32),
            vm(NH, rows, wide, dtype=F32),
            vm(rows, NH * rest, dtype=F32),
            vm(rows, 2 * NH * rest, dtype=F32),
            vm(NH, rows, LANES),
            vm(NH, rows, 2 * LANES),
            dma((15, 7)),
            dma((15, 7)),
            dma((4, 13)),
            dma((4, 13)),
            dma((4, 7)),
            dma((4, 7)),
            dma((6, 5)),
            dma((6, NS)),
            dma((7, 5)),
            dma((7, NS + 1)),
            dma((24,)),
            dma((8,)),
        ],
        compiler_params=pltpu.CompilerParams(
            collective_id=0, has_side_effects=True, vmem_limit_bytes=63 << 20
        ),
        name="layer",
    )(q_weight, gate_weight, up_weight, down_rows, gain_one, gain_two, tokens, o_own, keys, values, cot_own, order, lengths)


def per_device(
    nh,
    ns,
    tokens,
    keys,
    values,
    q_weight,
    o_weight,
    gate_weight,
    up_weight,
    down_weight,
    attn_gain,
    ffn_gain,
    span_order,
    doc_lengths,
    cotangent,
):
    gain_one = attn_gain.astype(F32)[:, None]
    gain_two = ffn_gain.astype(F32)[:, None]
    (
        mixed_out, grad_tokens, o_sum, grad_keys, grad_values, q_sum,
        gate_main, up_main, down_main, down_tail, pair_tail,
    ) = layer_call(
        q_weight,
        gate_weight,
        up_weight,
        down_weight.T,
        gain_one,
        gain_two,
        tokens,
        o_weight,
        keys,
        values,
        cotangent,
        span_order,
        doc_lengths,
    )[:11]
    rest = gate_weight.shape[1] // nh - gate_main.shape[2]

    def whole(part, tail):
        return rows_of(jnp.concatenate([part, tail[..., :rest]], axis=2)).astype(F32)

    q_sum = q_sum.astype(F32)
    gate_sum = whole(gate_main, pair_tail)
    up_sum = whole(up_main, pair_tail[..., LANES:])
    down_sum = whole(down_main, down_tail)
    grad_gain_one = jnp.sum(q_weight.astype(F32) * q_sum, axis=1)
    grad_gain_two = jnp.sum(
        gate_weight.astype(F32) * gate_sum + up_weight.astype(F32) * up_sum, axis=1
    )
    return (
        mixed_out,
        grad_tokens,
        grad_keys,
        grad_values,
        gain_one * q_sum,
        o_sum,
        gain_two * gate_sum,
        gain_two * up_sum,
        down_sum.T,
        grad_gain_one,
        grad_gain_two,
    )


def to_slices(weight, nh):
    rows, cols = weight.shape
    parts = weight.reshape(rows, nh, cols // nh).swapaxes(0, 1)
    return lax.all_to_all(parts, "head", 0, 0, tiled=False).reshape(nh * rows, cols // nh)


def from_slices(part, nh):
    rows, cols = part.shape
    parts = part.reshape(nh, rows // nh, cols)
    parts = lax.all_to_all(parts, "head", 0, 0, tiled=False)
    return parts.swapaxes(0, 1).reshape(rows // nh, nh * cols)


def gather_seq(part):
    return lax.all_gather(part, "seq", axis=0, tiled=True)


def scatter_seq(full):
    return lax.psum_scatter(full.astype(BF16), "seq", scatter_dimension=0, tiled=True)


def gather_head(part):
    return lax.all_gather(part, "head", axis=0, tiled=True)


def scatter_head(full):
    return lax.psum_scatter(full.astype(BF16), "head", scatter_dimension=0, tiled=True)


def per_device_plain(
    nh,
    ns,
    tokens,
    keys,
    values,
    q_weight,
    o_weight,
    gate_weight,
    up_weight,
    down_weight,
    attn_gain,
    ffn_gain,
    span_order,
    doc_lengths,
    cotangent,
):
    local, width = tokens.shape
    rows = q_weight.shape[0]

    def shuffle(field):
        return field.reshape(local, nh, ns, rows).swapaxes(1, 2).reshape(local, width)

    def unshuffle(field):
        return field.reshape(local, ns, nh, rows).swapaxes(1, 2).reshape(local, width)

    gain_one = attn_gain.astype(F32)[:, None]
    gain_two = ffn_gain.astype(F32)[:, None]
    inputs = tokens.astype(F32)
    scale_one = rms_scale(inputs)
    normed_one = inputs * scale_one
    normed_one_all = gather_head(shuffle(normed_one.astype(BF16)))
    w_q = gather_seq(to_slices((q_weight * gain_one).astype(BF16), nh))
    key_heads = to_slices(keys, nh)
    value_heads = to_slices(values, nh)
    w_o = gather_seq(o_weight)
    w_gate = gather_seq(to_slices((gate_weight * gain_two).astype(BF16), nh))
    w_up = gather_seq(to_slices((up_weight * gain_two).astype(BF16), nh))
    w_down = gather_seq(to_slices(down_weight.T, nh))
    cotangent_all = gather_head(shuffle(cotangent))

    group = normed_one_all.shape[0]
    position, segment = places(span_order[0], doc_lengths[0], group)
    place_q = jnp.stack([position, segment], axis=1)
    place_k = jnp.stack([position, segment], axis=0)

    query = dot(normed_one_all, w_q, ((1,), (0,))).astype(BF16)
    attended, lse = attend(query, key_heads, value_heads, place_q, place_k)
    hidden = inputs + scatter_head(dot(attended, w_o, ((1,), (0,)))).astype(F32)
    scale_two = rms_scale(hidden)
    normed_two = hidden * scale_two
    normed_two_all = gather_head(shuffle(normed_two.astype(BF16)))

    gate = dot(normed_two_all, w_gate, ((1,), (0,)))
    up = dot(normed_two_all, w_up, ((1,), (0,)))
    sigma = jax.nn.sigmoid(gate)
    act = (gate * sigma * up).astype(BF16)
    down_sum = scatter_seq(dot(cotangent_all, act, ((0,), (0,))))
    grad_act = dot(cotangent_all, w_down, ((1,), (0,)))
    grad_gate = (grad_act * up * sigma * (1.0 + gate * (1.0 - sigma))).astype(BF16)
    grad_up = (grad_act * gate * sigma).astype(BF16)
    spread_two = dot(grad_gate, w_gate, ((1,), (1,))) + dot(grad_up, w_up, ((1,), (1,)))
    scaled_two = unshuffle(scatter_head(spread_two)).astype(F32)
    gate_sum = scatter_seq(dot(normed_two_all, grad_gate, ((0,), (0,))))
    up_sum = scatter_seq(dot(normed_two_all, grad_up, ((0,), (0,))))
    mixed = unshuffle(scatter_head(dot(act, w_down, ((1,), (1,)))))
    mixed_out = (hidden + mixed.astype(F32)).astype(BF16)

    grad_hidden = cotangent.astype(F32) + scale_two * (
        scaled_two - normed_two * jnp.mean(scaled_two * normed_two, axis=-1, keepdims=True)
    )
    grad_hidden_all = gather_head(grad_hidden.astype(BF16))
    grad_attended = dot(grad_hidden_all, w_o, ((1,), (1,))).astype(BF16)
    o_sum = scatter_seq(dot(attended, grad_hidden_all, ((0,), (0,))))
    grad_query, grad_keys, grad_values = attend_back(
        query, key_heads, value_heads, grad_attended, lse, place_q, place_k
    )
    grad_keys = from_slices(grad_keys, nh)
    grad_values = from_slices(grad_values, nh)
    scaled_one = unshuffle(scatter_head(dot(grad_query, w_q, ((1,), (1,))))).astype(F32)
    q_sum = scatter_seq(dot(normed_one_all, grad_query, ((0,), (0,))))
    grad_tokens = grad_hidden + scale_one * (
        scaled_one - normed_one * jnp.mean(scaled_one * normed_one, axis=-1, keepdims=True)
    )
    q_sum = from_slices(q_sum, nh).astype(F32)
    gate_sum = from_slices(gate_sum, nh).astype(F32)
    up_sum = from_slices(up_sum, nh).astype(F32)
    down_sum = from_slices(down_sum, nh).astype(F32)
    grad_gain_one = jnp.sum(q_weight.astype(F32) * q_sum, axis=1)
    grad_gain_two = jnp.sum(
        gate_weight.astype(F32) * gate_sum + up_weight.astype(F32) * up_sum, axis=1
    )
    return (
        mixed_out,
        grad_tokens.astype(BF16),
        grad_keys,
        grad_values,
        gain_one * q_sum,
        o_sum.astype(F32),
        gain_two * gate_sum,
        gain_two * up_sum,
        down_sum.T,
        grad_gain_one,
        grad_gain_two,
    )


def solution(mesh):
    both = ("head", "seq")
    nh, ns = mesh.shape["head"], mesh.shape["seq"]
    body = per_device if (nh, ns) == (NH, NS) else per_device_plain
    rows, cols, line, own = P(both, None), P(None, both), P(both), P("seq", None)
    return jax.shard_map(
        functools.partial(body, nh, ns),
        mesh=mesh,
        in_specs=(rows,) * 7 + (cols, line, line, own, own, rows),
        out_specs=(rows,) * 8 + (cols, line, line),
        check_vma=False,
    )
```

```python
import functools
import math

import jax
import jax.numpy as jnp
from jax import lax
from jax.experimental import pallas as pl
from jax.experimental.pallas import tpu as pltpu
from jax.sharding import PartitionSpec as P

HEAD_DIM = 128
NH, NS = 8, 4
EPS = 1e-06
BF16 = jnp.bfloat16
F32 = jnp.float32


def rms_scale(field):
    return lax.rsqrt(jnp.mean(field * field, axis=-1, keepdims=True) + EPS)


def dot(left, right, dims):
    return lax.dot_general(left, right, (dims, ((), ())), preferred_element_type=F32)


def places(order_row, length_row, group):
    count = order_row.shape[0]
    width = group // count
    slots = jnp.arange(group, dtype=jnp.int32)
    which = slots // width
    picked = jnp.where(
        which[:, None] == jnp.arange(count, dtype=jnp.int32)[None, :], order_row[None, :], 0
    )
    position = jnp.sum(picked, axis=1) * width + slots % width
    bounds = jnp.cumsum(length_row)
    segment = jnp.sum((position[:, None] >= bounds[None, :]).astype(jnp.int32), axis=1)
    return (position, segment)


def attend_kernel(q_ref, k_ref, v_ref, place_q, place_k, out_ref, lse_ref):
    scale = 1.0 / math.sqrt(HEAD_DIM)
    raw = dot(q_ref[...], k_ref[...], ((1,), (1,)))
    allowed = (place_q[:, 1:2] == place_k[1:2, :]) & (place_k[0:1, :] <= place_q[:, 0:1])
    logits = jnp.where(allowed, raw * scale, -1e30)
    top = jnp.max(logits, axis=-1, keepdims=True)
    expo = jnp.exp(logits - top)
    total = jnp.sum(expo, axis=-1, keepdims=True)
    probs = expo * (1.0 / total)
    out_ref[...] = dot(probs.astype(BF16), v_ref[...], ((1,), (0,))).astype(BF16)
    lse_ref[...] = jnp.broadcast_to(top + jnp.log(total), lse_ref.shape)


def attend(query, keys, values, place_q, place_k):
    group, width = query.shape
    heads = width // HEAD_DIM
    rows = min(group, 256)
    block = pl.BlockSpec((rows, HEAD_DIM), lambda h, i: (i, h))
    whole = pl.BlockSpec((group, HEAD_DIM), lambda h, i: (0, h))
    return pl.pallas_call(
        attend_kernel,
        grid=(heads, group // rows),
        in_specs=[
            block,
            whole,
            whole,
            pl.BlockSpec((rows, 2), lambda h, i: (i, 0)),
            pl.BlockSpec((2, group), lambda h, i: (0, 0)),
        ],
        out_specs=[block, block],
        out_shape=[
            jax.ShapeDtypeStruct((group, width), BF16),
            jax.ShapeDtypeStruct((group, width), F32),
        ],
        compiler_params=pltpu.CompilerParams(vmem_limit_bytes=48 << 20),
        cost_estimate=pl.CostEstimate(
            flops=4 * group * group * width,
            bytes_accessed=12 * group * width,
            transcendentals=heads * group * group,
        ),
        name="attend",
    )(query, keys, values, place_q, place_k)


def attend_back_kernel(
    q_ref, k_ref, v_ref, do_ref, lse_ref, place_q, place_k, dq_ref, dk_ref, dv_ref, dk_sum, dv_sum
):
    step = pl.program_id(1)
    scale = 1.0 / math.sqrt(HEAD_DIM)
    query, keys, grad = q_ref[...], k_ref[...], do_ref[...]
    raw = dot(query, keys, ((1,), (1,)))
    allowed = (place_q[:, 1:2] == place_k[1:2, :]) & (place_k[0:1, :] <= place_q[:, 0:1])
    logits = jnp.where(allowed, raw * scale, -1e30)
    probs = jnp.exp(logits - lse_ref[:, :1])
    grad_probs = dot(grad, v_ref[...], ((1,), (1,)))
    inner = jnp.sum(probs * grad_probs, axis=-1, keepdims=True)
    grad_raw = (probs * (grad_probs - inner) * scale).astype(BF16)
    dq_ref[...] = dot(grad_raw, keys, ((1,), (0,))).astype(BF16)

    @pl.when(step == 0)
    def _():
        dk_sum[...] = jnp.zeros_like(dk_sum)
        dv_sum[...] = jnp.zeros_like(dv_sum)

    dk_sum[...] += dot(grad_raw, query, ((0,), (0,)))
    dv_sum[...] += dot(probs.astype(BF16), grad, ((0,), (0,)))

    @pl.when(step == pl.num_programs(1) - 1)
    def _():
        dk_ref[...] = dk_sum[...].astype(BF16)
        dv_ref[...] = dv_sum[...].astype(BF16)


def attend_back(query, keys, values, grad, lse, place_q, place_k):
    group, width = query.shape
    heads = width // HEAD_DIM
    rows = min(group, 256)
    block = pl.BlockSpec((rows, HEAD_DIM), lambda h, i: (i, h))
    whole = pl.BlockSpec((group, HEAD_DIM), lambda h, i: (0, h))
    full = jax.ShapeDtypeStruct((group, width), BF16)
    return pl.pallas_call(
        attend_back_kernel,
        grid=(heads, group // rows),
        in_specs=[
            block,
            whole,
            whole,
            block,
            block,
            pl.BlockSpec((rows, 2), lambda h, i: (i, 0)),
            pl.BlockSpec((2, group), lambda h, i: (0, 0)),
        ],
        out_specs=[block, whole, whole],
        out_shape=[full, full, full],
        scratch_shapes=[pltpu.VMEM((group, HEAD_DIM), F32)] * 2,
        compiler_params=pltpu.CompilerParams(vmem_limit_bytes=48 << 20),
        cost_estimate=pl.CostEstimate(
            flops=10 * group * group * width,
            bytes_accessed=18 * group * width,
            transcendentals=heads * group * group,
        ),
        name="attend_back",
    )(query, keys, values, grad, lse, place_q, place_k)


MESH = pl.DeviceIdType.MESH
ANY = pl.BlockSpec(memory_space=pl.ANY)
VMEM = pl.BlockSpec(memory_space=pltpu.VMEM)
SMEM = pl.BlockSpec(memory_space=pltpu.SMEM)
LANES = 128


def slices_of(weight, nh):
    rows, cols = weight.shape
    return weight.reshape(rows, nh, cols // nh).swapaxes(0, 1)


def rows_of(parts):
    nh, rows, cols = parts.shape
    return parts.swapaxes(0, 1).reshape(rows, nh * cols)


def flat(parts):
    return parts.reshape(parts.shape[0] * parts.shape[1], parts.shape[2])


def remote(src, dst, send, recv, to):
    return pltpu.make_async_remote_copy(
        src_ref=src, dst_ref=dst, send_sem=send, recv_sem=recv, device_id=to, device_id_type=MESH
    )


class Net:
    def __init__(self):
        self.h = lax.axis_index("head")
        self.s = lax.axis_index("seq")

    def peer(self, k):
        return (lax.bitwise_xor(self.h, k), self.s)

    def greet(self):
        barrier = pltpu.get_barrier_semaphore()
        for k in range(1, NH):
            pl.semaphore_signal(barrier, inc=1, device_id=self.peer(k), device_id_type=MESH)
        for k in range(1, NS):
            there = (self.h, lax.rem(self.s + k, NS))
            pl.semaphore_signal(barrier, inc=1, device_id=there, device_id_type=MESH)
        pl.semaphore_wait(barrier, NH - 1 + NS - 1)

    def swap(self, src, dst, send, recv, own):
        mine = pltpu.make_async_copy(src(self.h), dst(self.h), own)
        mine.start()
        copies = []
        for k in (6, 2, 4, 1, 5, 3, 7):
            to = self.peer(k)
            copy = remote(src(to[0]), dst(self.h), send.at[k - 1], recv.at[k - 1], to)
            copy.start()
            copies.append(copy)

        def finish():
            for copy in copies:
                copy.wait()
            mine.wait()

        return finish

    def gather(self, src, dst, send, recv, own):
        half = src.shape[0] // 2
        lo, hi = pl.ds(0, half), pl.ds(half, half)
        h, core, px, py = self.h, self.peer(1), self.peer(2), self.peer(4)
        x, y, d = px[0], py[0], lax.bitwise_xor(h, 6)
        mine = pltpu.make_async_copy(src, dst.at[h], own)
        mine.start()
        copies = []

        def put(i, a, b, to):
            copy = remote(a, b, send.at[i], recv.at[i], to)
            copy.start()
            copies.append(copy)
            return copy

        def on(i, block, rows, to):
            return put(i, dst.at[block, rows], dst.at[block, rows], to)

        xa = put(0, src.at[lo], dst.at[h, lo], px)
        yb = put(1, src.at[hi], dst.at[h, hi], py)
        near = [put(2, src, dst.at[h], core)]
        xb = put(3, src.at[hi], dst.at[h, hi], px)
        ya = put(4, src.at[lo], dst.at[h, lo], py)
        far = []

        def relay():
            xa.wait_recv()
            far.append(on(5, x, lo, py))
            near.append(on(6, x, lo, core))
            yb.wait_recv()
            far.append(on(7, y, hi, px))
            near.append(on(8, y, hi, core))
            xb.wait_recv()
            near.append(on(9, x, hi, core))
            ya.wait_recv()
            near.append(on(10, y, lo, core))

        def finish():
            far[0].wait_recv()
            near.append(on(11, d, lo, core))
            far[1].wait_recv()
            near.append(on(12, d, hi, core))
            for copy in near:
                copy.wait_recv()
            mine.wait()
            for copy in copies:
                copy.wait_send()

        return relay, finish

    def scatter(self, source, block, core_in, held, far_in, send, recv, read):
        core, px, py = self.peer(1), self.peer(2), self.peer(4)
        half = held.shape[1] // 2
        lo, hi = pl.ds(0, half), pl.ds(half, half)
        copies = []

        def put(i, a, b, to):
            copy = remote(a, b, send.at[i], recv.at[i], to)
            copy.start()
            copies.append(copy)
            return copy

        order = (6, 2, 4, 0)
        near = [
            put(i, source(i, lax.bitwise_xor(core[0], k)), core_in.at[i], core)
            for i, k in enumerate(order)
        ]
        far = []
        for i, k in enumerate(order):
            value = block(i, lax.bitwise_xor(self.h, k))
            near[i].wait_recv()
            value = value + read(core_in.at[i]).astype(F32)
            if k:
                held[i] = value.astype(BF16)
            if k == 6:
                far.append(put(4, held.at[0, lo], far_in.at[0], px))
                far.append(put(5, held.at[0, hi], far_in.at[1], py))
            elif k == 2:
                far.append(put(6, held.at[1, lo], far_in.at[2], px))
            elif k == 4:
                far.append(put(7, held.at[2, hi], far_in.at[3], py))

        def pass_on(i, slot, rows, arrived, to):
            arrived.wait_recv()
            joined = held[slot, rows].astype(F32) + read(far_in.at[i]).astype(F32)
            held[slot, rows] = joined.astype(BF16)
            far.append(put(8 + i, held.at[slot, rows], far_in.at[4 + i], to))

        def relay():
            pass_on(0, 2, lo, far[0], py)
            pass_on(1, 1, hi, far[1], px)

        def finish():
            parts = []
            for i, rows in enumerate((slice(0, half), slice(half, 2 * half))):
                part = value[rows]
                for j in (2 + i, 4 + i):
                    far[j].wait_recv()
                    part = part + read(far_in.at[j]).astype(F32)
                parts.append(part)
            for copy in copies:
                copy.wait_send()
            return jnp.concatenate(parts, axis=0)

        return relay, finish

    def z_gather(self, src, block, send, recv):
        s = self.s
        ends = (s == 0) | (s == NS - 1)
        middle = jnp.logical_not(ends)
        across = NS - 1 - s
        near = jnp.where(s == 1, 0, NS - 1)
        steps = ((2, s == 0), (-2, s == NS - 1), (1, s < NS - 1), (-1, s > 0))
        relayed = (across, NS - 1 - near)

        def copy(n):
            return remote(src, block(s), send.at[n], recv.at[s], (self.h, s + steps[n][0]))

        def relay(k):
            origin = relayed[k]
            return remote(block(origin), block(origin), send.at[4 + k], recv.at[origin], (self.h, near))

        for n, (_, where) in enumerate(steps):

            @pl.when(where)
            def _():
                copy(n).start()

        def forward():
            @pl.when(middle)
            def _():
                for k in range(2):
                    relay(k).wait_recv()
                    relay(k).start()

        def finish():
            for t in range(NS):
                waited = ((s == 1) & (t >= 2)) | ((s == 2) & (t < 2))

                @pl.when((s != t) & jnp.logical_not(waited))
                def _():
                    remote(block(t), block(t), send.at[0], recv.at[t], (self.h, s)).wait_recv()

        def drain():
            for n, (_, where) in enumerate(steps):

                @pl.when(where)
                def _():
                    copy(n).wait_send()

            @pl.when(middle)
            def _():
                for k in range(2):
                    relay(k).wait_send()

        return forward, finish, drain


def z_scatter(net, block, value, got, comb, join_v, bufs, send, recv, sems):
    s = net.s
    ends = (s == 0) | (s == NS - 1)
    middle = jnp.logical_not(ends)
    inner = jnp.where(s == 0, 1, NS - 2)
    near = jnp.where(s == 1, 0, NS - 1)
    goals = (NS - 1 - s, NS - 1 - near)
    end_blocks = (NS - 1 - inner, NS - 1 - s)

    def to_join(k):
        return remote(block(end_blocks[k]), comb.at[k], send.at[k], recv.at[2 + k], (net.h, inner))

    def joined(k):
        return remote(join_v.at[k], got.at[1], send.at[k], recv.at[1], (net.h, goals[k]))

    def direct(t):
        return remote(block(t), got.at[0], send.at[2], recv.at[0], (net.h, t))

    def start():
        @pl.when(ends)
        def _():
            to_join(1).start()
            to_join(0).start()
            direct(inner).start()

        @pl.when(middle)
        def _():
            direct(near).start()

    def join():
        @pl.when(middle)
        def _():
            for k in (1, 0):
                to_join(k).wait_recv()
                copy = pltpu.make_async_copy(comb.at[k], join_v.at[k], sems.at[6 + k])
                copy.start()
                copy.wait()
                term = join_v[k].astype(F32) + value(goals[k]).astype(F32)
                join_v[k] = term.astype(BF16)
                joined(k).start()

    def finish(total):
        total[...] = value(s).astype(F32)
        takes = []
        for k in range(2):
            remote(got.at[k], got.at[k], send.at[0], recv.at[k], (net.h, s)).wait_recv()
            takes.append(pltpu.make_async_copy(got.at[k], bufs.at[k], sems.at[4 + k]))
            takes[k].start()
        for k in range(2):
            takes[k].wait()
            total[...] += bufs[k].astype(F32)

    def drain():
        @pl.when(ends)
        def _():
            to_join(0).wait_send()
            to_join(1).wait_send()
            direct(inner).wait_send()

        @pl.when(middle)
        def _():
            joined(0).wait_send()
            joined(1).wait_send()
            direct(near).wait_send()

    return start, join, finish, drain


def make_places(order, lengths, place_q, place_k):
    group, count = place_q.shape[0], order.shape[1]
    width = group // count
    for shape, dim in (((group, 1), 0), ((1, group), 1)):
        slots = lax.broadcasted_iota(jnp.int32, shape, dim)
        position = slots
        for c in range(count):
            inside = (slots >= c * width) & (slots < (c + 1) * width)
            position = jnp.where(inside, slots + (order[0, c] - c) * width, position)
        segment = jnp.zeros(shape, jnp.int32)
        bound = 0
        for j in range(lengths.shape[1]):
            bound = bound + lengths[0, j]
            segment = segment + (position >= bound).astype(jnp.int32)
        if dim == 0:
            place_q[:, 0:1] = position
            place_q[:, 1:2] = segment
        else:
            place_k[0:1, :] = position
            place_k[1:2, :] = segment


def mask(place_q, place_k, rows):
    return (place_q[rows, 1:2] == place_k[1:2, :]) & (place_k[0:1, :] <= place_q[rows, 0:1])


def lane_block(w, p, wide):
    return w.at[:, pl.ds(pl.multiple_of(p * wide, wide), wide)]


def load(pairs, sems, base):
    copies = [pltpu.make_async_copy(a, b, sems.at[base + i]) for i, (a, b) in enumerate(pairs)]
    for copy in copies:
        copy.start()

    def finish():
        for copy in copies:
            copy.wait()

    return finish


def layer_kernel(
    q_weight,
    gate_weight,
    up_weight,
    down_rows,
    gain_one,
    gain_two,
    tokens,
    o_own,
    keys,
    values,
    cot_own,
    order,
    lengths,
    mixed_out,
    d_tokens,
    o_out,
    d_keys,
    d_values,
    q_out,
    gate_out,
    up_out,
    down_out,
    down_tail_out,
    pair_tail_out,
    n1_all,
    mixed_near,
    mixed_far,
    got_ffn,
    comb_ffn,
    got_q,
    comb_q,
    got_o,
    comb_o,
    got_dt,
    comb_dt,
    got_pt,
    comb_pt,
    place_q,
    place_k,
    q_own,
    parts,
    tails_own,
    tails_in,
    tails,
    wq_v,
    wo_v,
    wg_v,
    wu_v,
    wd_v,
    norm_v,
    wide_v,
    k_v,
    v_v,
    query,
    attended,
    lse,
    norm_own,
    hidden_v,
    dh_v,
    near_out,
    core_in,
    held,
    far_in,
    act_v,
    grad_gate,
    grad_up,
    down_term,
    stage,
    stage_two,
    down_tail,
    pair_tail,
    dq_v,
    dk_sum,
    dv_sum,
    joins,
    q_join,
    o_join,
    dt_join,
    pt_join,
    bufs,
    o_bufs,
    dt_bufs,
    pt_bufs,
    total,
    dt_total,
    pt_total,
    dt_back,
    pt_back,
    swap_send,
    swap_recv,
    ag_send,
    ag_recv,
    rs_send,
    rs_recv,
    zg_send,
    zg_recv,
    zs_send,
    zs_recv,
    own,
    load_sem,
):
    net = Net()
    h, s = net.h, net.s
    local, width = tokens.shape
    group = NH * local
    wide, hid = query.shape[1], act_v.shape[1]
    main = parts.shape[3]
    rest = hid - main
    step = 256
    tiles = group // step
    fold = width // NH
    scale = 1.0 / math.sqrt(HEAD_DIM)
    body = pl.ds(0, main)
    net.greet()

    def swap(j, src, dst):
        return net.swap(src, dst, swap_send.at[j], swap_recv.at[j], own.at[j])

    def gather(j, src, dst):
        return net.gather(src, dst, ag_send.at[j], ag_recv.at[j], own.at[20 + j])

    def z_gather(j, src, block):
        return net.z_gather(src, block, zg_send.at[j], zg_recv.at[j])

    def slab(w):
        return lambda t: w.at[:, t, :, body]

    def tile_rows(i):
        return pl.ds(pl.multiple_of(i * step, step), step)

    def token_tile(field, i):
        return field[pl.ds(i * (step // local), step // local)].reshape(step, width)

    def own_rows(p):
        return pl.ds(pl.multiple_of(p * local, local), local)

    zo = z_gather(0, o_own, lambda t: wo_v.at[t])
    o_here = load([(o_own, wo_v.at[s])], load_sem, 0)
    rows = q_weight.shape[0]
    diagonal = lax.broadcasted_iota(jnp.int32, (rows, rows), 0) == lax.broadcasted_iota(
        jnp.int32, (rows, rows), 1
    )

    def column(gain):
        field = jnp.broadcast_to(gain[...].astype(F32), (rows, rows))
        return jnp.sum(jnp.where(diagonal, field, 0.0), axis=1, keepdims=True)

    field = (q_weight[...].astype(F32) * column(gain_one)).astype(BF16)
    for p in range(NH):
        q_own[p] = field[:, p * wide : (p + 1) * wide]
    q_there = swap(0, lambda p: q_own.at[p], lambda p: wq_v.at[p, s])
    ffn = ((gate_weight, gain_two), (up_weight, gain_two), (down_rows, None))
    ffn_v = (wg_v, wu_v, wd_v)

    def slices(j):
        weight, gain = ffn[j]
        field = weight[...]
        if gain is not None:
            field = (field.astype(F32) * column(gain)).astype(BF16)
        for p in range(NH):
            parts[j, p] = field[:, p * hid : p * hid + main]
            tails_own[p, :, j * LANES : j * LANES + rest] = field[:, p * hid + main : (p + 1) * hid]
        return swap(
            1 + j, lambda p: parts.at[j, p], lambda p: ffn_v[j].at[p, s, :, body]
        )

    inputs = tokens[...].astype(F32)
    norm_own[...] = (inputs * rms_scale(inputs)).astype(BF16)
    n1_there = gather(0, norm_own, n1_all)
    gate_there = slices(0)
    k_there = swap(5, lambda p: lane_block(keys, p, wide), lambda p: k_v.at[p])
    v_there = swap(6, lambda p: lane_block(values, p, wide), lambda p: v_v.at[p])
    q_there()
    zq = z_gather(1, wq_v.at[:, s], lambda t: wq_v.at[:, t])
    n1_there[0]()
    gate_there()
    zg = z_gather(2, wg_v.at[:, s, :, body], slab(wg_v))
    n1_there[1]()
    n1_here = load([(n1_all, norm_v)], load_sem, 1)
    up_there = slices(1)
    make_places(order, lengths, place_q, place_k)
    zo[0]()
    zq[0]()
    k_there()
    v_there()
    zq[1]()
    n1_here()

    @pl.loop(0, tiles)
    def _(i):
        query[tile_rows(i), :] = dot(
            token_tile(norm_v, i), wq_v[...].reshape(width, wide), ((1,), (0,))
        ).astype(BF16)

    down_there = slices(2)
    tails_there = swap(4, lambda p: tails_own.at[p], lambda p: tails_in.at[p])
    up_there()
    zu = z_gather(4, wu_v.at[:, s, :, body], slab(wu_v))

    for head in range(wide // HEAD_DIM):
        cols = slice(head * HEAD_DIM, (head + 1) * HEAD_DIM)

        @pl.loop(0, tiles)
        def _(i):
            rows = tile_rows(i)
            raw = dot(query[rows, cols], k_v[:, :, cols].reshape(group, HEAD_DIM), ((1,), (1,)))
            logits = jnp.where(mask(place_q, place_k, rows), raw * scale, -1e30)
            top = jnp.max(logits, axis=-1, keepdims=True)
            expo = jnp.exp(logits - top)
            norm = jnp.sum(expo, axis=-1, keepdims=True)
            probs = (expo * (1.0 / norm)).astype(BF16)
            attended[rows, cols] = dot(
                probs, v_v[:, :, cols].reshape(group, HEAD_DIM), ((1,), (0,))
            ).astype(BF16)
            lse[rows, head : head + 1] = top + jnp.log(norm)

    zg[0]()
    tails_there()
    for j in range(3):
        for p in range(NH):
            at = (j * NH + p) * rest
            tails[s, :, at : at + rest] = tails_in[p, :, j * LANES : j * LANES + rest]
    zt = z_gather(3, tails.at[s], lambda t: tails.at[t])
    down_there()
    zd = z_gather(5, wd_v.at[:, s, :, body], slab(wd_v))
    zo[1]()
    o_here()

    def scatter(
        j, block, core=core_in, far=far_in, read=lambda ref: ref[...], near=near_out, keep=held
    ):
        def source(i, p):
            near[i] = block(i, p).astype(BF16)
            return near.at[i]

        return net.scatter(source, block, core, keep, far, rs_send.at[j], rs_recv.at[j], read)

    def o_block(i, p):
        return dot(attended[own_rows(p), :], wo_v[...].reshape(wide, width), ((1,), (0,)))

    o_sum = scatter(0, o_block)
    o_sum[0]()
    hidden = tokens[...].astype(F32) + o_sum[1]()
    hidden_v[...] = hidden
    norm_own[...] = (hidden * rms_scale(hidden)).astype(BF16)
    n2_there = gather(2, norm_own, norm_v)
    n2_there[0]()
    zt[0]()
    zu[0]()
    n2_there[1]()
    cot_there = gather(1, cot_own, wide_v)
    cot_there[0]()
    zt[1]()

    def matrix(w):
        return w[...].reshape(width, hid)

    def add_tail(j):
        for p in range(NH):
            at = (j * NH + p) * rest
            ffn_v[j][p, :, :, main:hid] = tails[:, :, at : at + rest]

    zg[1]()
    add_tail(0)
    zd[0]()
    cot_there[1]()
    zu[1]()
    add_tail(1)

    @pl.loop(0, tiles)
    def _(i):
        rows = tile_rows(i)
        part = token_tile(norm_v, i)
        gate = dot(part, matrix(wg_v), ((1,), (0,)))
        up = dot(part, matrix(wu_v), ((1,), (0,)))
        sigma = jax.nn.sigmoid(gate)
        silu = gate * sigma
        act_v[rows, :] = (silu * up).astype(BF16)
        grad_gate[rows, :] = (up * sigma * (1.0 + gate * (1.0 - sigma))).astype(BF16)
        grad_up[rows, :] = silu.astype(BF16)

    def columns(field, i):
        cols = pl.ds(pl.multiple_of(i * fold, fold), fold)
        return field[:, :, cols].reshape(group, fold)

    def put_term(i, left, right, body_ref, tail_ref):
        value = dot(left, right, ((0,), (0,))).astype(BF16)
        body_ref[i, :, :, body] = value[:, :main].reshape(NS, fold // NS, main)
        tail_ref[i, :, 0:rest] = value[:, main:]

    def pack(tail_ref, out, base):
        for p in range(NH):
            at = (base * NH + p) * rest
            out[:, :, at : at + rest] = tail_ref[p, :, 0:rest].reshape(NS, fold // NS, rest)

    @pl.loop(0, NH)
    def _(i):
        put_term(i, columns(wide_v, i), act_v[...], down_term, stage)

    pack(stage, down_tail, 0)

    def z_sum(j, block, value, got, comb, join, buf):
        z = z_scatter(net, block, value, got, comb, join, buf, zs_send.at[j], zs_recv.at[j], load_sem)
        z[0]()
        return z

    def slab_value(w):
        return lambda t: w[:, pl.ds(t, 1), :, body].reshape(NH, fold // NS, main)

    def block_value(w):
        return lambda t: w[pl.ds(t, 1)].reshape(w.shape[1:])

    z_down = z_sum(
        0, slab(down_term), slab_value(down_term), got_ffn.at[0], comb_ffn.at[0], joins, bufs
    )
    z_dt = z_sum(
        1, lambda t: down_tail.at[t], block_value(down_tail), got_dt, comb_dt, dt_join, dt_bufs
    )
    zd[1]()
    add_tail(2)

    @pl.loop(0, tiles)
    def _(i):
        rows = tile_rows(i)
        grad_act = dot(token_tile(wide_v, i), matrix(wd_v), ((1,), (0,)))
        grad_gate[rows, :] = (grad_act * grad_gate[rows, :].astype(F32)).astype(BF16)
        grad_up[rows, :] = (grad_act * grad_up[rows, :].astype(F32)).astype(BF16)

    def spread_block(i, p):
        rows = own_rows(p)
        value = dot(grad_gate[rows, :], matrix(wg_v), ((1,), (1,)))
        return value + dot(grad_up[rows, :], matrix(wu_v), ((1,), (1,)))

    ffn_sum = scatter(1, spread_block)
    zg[2]()

    @pl.loop(0, NH)
    def _(i):
        put_term(i, columns(norm_v, i), grad_gate[...], wg_v, stage)

    z_gate = z_sum(
        2, slab(wg_v), slab_value(wg_v), got_ffn.at[1], comb_ffn.at[1], joins, bufs
    )
    ffn_sum[0]()
    z_down[1]()
    z_dt[1]()

    zu[2]()

    @pl.loop(0, NH)
    def _(i):
        put_term(i, columns(norm_v, i), grad_up[...], wu_v, stage_two)

    n1_here = load([(n1_all, norm_v)], load_sem, 0)
    z_up = z_sum(4, slab(wu_v), slab_value(wu_v), got_ffn.at[2], comb_ffn.at[2], joins, bufs)
    pack(stage, pair_tail, 0)
    pack(stage_two, pair_tail, 1)
    z_pt = z_sum(
        3, lambda t: pair_tail.at[t], block_value(pair_tail), got_pt, comb_pt, pt_join, pt_bufs
    )

    hidden = hidden_v[...]
    scale_two = rms_scale(hidden)
    normed_two = hidden * scale_two
    scaled_two = ffn_sum[1]()
    grad_hidden = cot_own[...].astype(F32) + scale_two * (
        scaled_two - normed_two * jnp.mean(scaled_two * normed_two, axis=-1, keepdims=True)
    )
    dh_v[...] = grad_hidden
    norm_own[...] = grad_hidden.astype(BF16)
    dh_there = gather(3, norm_own, wide_v)
    dh_there[0]()
    backs = []

    def back(j, z, out, result):
        z[2](total)
        result[...] = total[...].astype(BF16)
        backs.append(swap(j, lambda p: result.at[p], lambda p: out.at[p]))

    back(7, z_down, down_out, parts.at[2])
    z_dt[2](dt_total)
    for p in range(NH):
        dt_back[p, :, 0:rest] = dt_total[:, p * rest : (p + 1) * rest].astype(BF16)
    backs.append(swap(8, lambda p: dt_back.at[p], lambda p: down_tail_out.at[p]))
    dh_there[1]()
    z_down[3]()
    z_gate[1]()

    @pl.loop(0, tiles)
    def _(i):
        dq_v[tile_rows(i), :] = dot(
            token_tile(wide_v, i), wo_v[...].reshape(wide, width), ((1,), (1,))
        ).astype(BF16)

    for head in range(wide // HEAD_DIM):
        cols = slice(head * HEAD_DIM, (head + 1) * HEAD_DIM)
        dk_sum[...] = jnp.zeros_like(dk_sum)
        dv_sum[...] = jnp.zeros_like(dv_sum)

        @pl.loop(0, tiles)
        def _(i):
            rows = tile_rows(i)
            key_rows = k_v[:, :, cols].reshape(group, HEAD_DIM)
            part, grad = query[rows, cols], dq_v[rows, cols]
            raw = dot(part, key_rows, ((1,), (1,)))
            logits = jnp.where(mask(place_q, place_k, rows), raw * scale, -1e30)
            probs = jnp.exp(logits - lse[rows, head : head + 1])
            grad_probs = dot(grad, v_v[:, :, cols].reshape(group, HEAD_DIM), ((1,), (1,)))
            inner = jnp.sum(probs * grad_probs, axis=-1, keepdims=True)
            grad_raw = (probs * (grad_probs - inner) * scale).astype(BF16)
            dq_v[rows, cols] = dot(grad_raw, key_rows, ((1,), (0,))).astype(BF16)
            dk_sum[...] += dot(grad_raw, part, ((0,), (0,)))
            dv_sum[...] += dot(probs.astype(BF16), grad, ((0,), (0,)))

        k_v[:, :, cols] = dk_sum[...].astype(BF16).reshape(NH, local, HEAD_DIM)
        v_v[:, :, cols] = dv_sum[...].astype(BF16).reshape(NH, local, HEAD_DIM)

    def q_block(i, p):
        return dot(dq_v[own_rows(p), :], wq_v[...].reshape(width, wide), ((1,), (1,)))

    q_sum = scatter(2, q_block)
    q_sum[0]()
    n1_here()

    zq[2]()

    @pl.loop(0, NH)
    def _(i):
        part = dot(columns(norm_v, i), dq_v[...], ((0,), (0,)))
        wq_v[i] = part.astype(BF16).reshape(NS, fold // NS, wide)

    zq_sum = z_sum(
        5,
        lambda t: wq_v.at[:, t],
        lambda t: wq_v[:, pl.ds(t, 1)].reshape(NH, fold // NS, wide),
        got_q,
        comb_q,
        q_join,
        bufs.at[:, :, :, pl.ds(0, wide)],
    )

    zo[2]()

    @pl.loop(0, NH)
    def _(i):
        cols = pl.ds(pl.multiple_of(i * fold, fold), fold)
        part = dot(attended[...], columns(wide_v, i), ((0,), (0,)))
        wo_v[:, :, cols] = part.astype(BF16).reshape(NS, wide // NS, fold)

    zo_sum = z_sum(6, lambda t: wo_v.at[t], block_value(wo_v), got_o, comb_o, o_join, o_bufs)
    backs.append(swap(9, lambda p: k_v.at[p], lambda p: lane_block(d_keys, p, wide)))
    backs.append(swap(10, lambda p: v_v.at[p], lambda p: lane_block(d_values, p, wide)))
    z_gate[3]()
    z_up[1]()
    back(11, z_gate, gate_out, parts.at[0])

    inputs = tokens[...].astype(F32)
    scale_one = rms_scale(inputs)
    normed_one = inputs * scale_one
    scaled_one = q_sum[1]()
    d_tokens[...] = (
        dh_v[...]
        + scale_one
        * (scaled_one - normed_one * jnp.mean(scaled_one * normed_one, axis=-1, keepdims=True))
    ).astype(BF16)

    def mixed_block(i, p):
        return dot(act_v[own_rows(p), :], matrix(wd_v), ((1,), (1,)))

    def staged(ref):
        slot = norm_v.at[NH - 1, pl.ds(0, ref.shape[0])]
        load([(ref, slot)], load_sem, 2)()
        return slot[...]

    mixed_sum = scatter(
        3, mixed_block, mixed_near, mixed_far, staged, norm_v, norm_v.at[pl.ds(4, 3)]
    )
    back(12, z_up, up_out, parts.at[1])
    mixed_sum[0]()
    z_pt[1]()
    zq_sum[1]()
    zo_sum[1]()
    z_pt[2](pt_total)
    for j in range(2):
        for p in range(NH):
            at = (j * NH + p) * rest
            pt_back[p, :, j * LANES : j * LANES + rest] = pt_total[:, at : at + rest].astype(BF16)
    backs.append(swap(13, lambda p: pt_back.at[p], lambda p: pair_tail_out.at[p]))
    mixed_out[...] = (hidden_v[...] + mixed_sum[1]()).astype(BF16)
    q_total = total.at[:, :, pl.ds(0, wide)]
    zq_sum[2](q_total)
    q_own[...] = q_total[...].astype(BF16)
    backs.append(swap(14, lambda p: q_own.at[p], lambda p: lane_block(q_out, p, wide)))
    zo_sum[2](o_out)
    for done in backs:
        done()
    for z in (zt, zd):
        z[2]()
    for z in (z_dt, z_pt, z_up, zq_sum, zo_sum):
        z[3]()


def layer_call(q_weight, gate_weight, up_weight, down_rows, gain_one, gain_two, tokens, o_own, keys, values, cot_own, order, lengths):
    local, width = tokens.shape
    group = NH * local
    rows = o_own.shape[0]
    wide, hid = width // NH, gate_weight.shape[1] // NH
    main = hid // LANES * LANES
    rest = hid - main

    def bf(*shape):
        return jax.ShapeDtypeStruct(shape, BF16)

    def vm(*shape, dtype=BF16):
        return pltpu.VMEM(shape, dtype)

    out_shape = [
        bf(local, width),
        bf(local, width),
        jax.ShapeDtypeStruct((rows, width), F32),
        bf(local, width),
        bf(local, width),
        bf(rows, width),
        bf(NH, rows, main),
        bf(NH, rows, main),
        bf(NH, rows, main),
        bf(NH, rows, LANES),
        bf(NH, rows, 2 * LANES),
        bf(NH, local, width),
        bf(4, local, width),
        bf(6, local // 2, width),
        bf(3, 2, NH, rows, main),
        bf(3, 2, NH, rows, main),
        bf(2, NH, rows, wide),
        bf(2, NH, rows, wide),
        bf(2, rows, width),
        bf(2, rows, width),
        bf(2, rows, NH * rest),
        bf(2, rows, NH * rest),
        bf(2, rows, 2 * NH * rest),
        bf(2, rows, 2 * NH * rest),
    ]
    dma = pltpu.SemaphoreType.DMA
    return pl.pallas_call(
        layer_kernel,
        out_shape=out_shape,
        in_specs=[VMEM] * 7 + [ANY] * 3 + [VMEM] + [SMEM] * 2,
        out_specs=[VMEM] * 3 + [ANY] * 21,
        scratch_shapes=[
            vm(group, 2, dtype=jnp.int32),
            vm(2, group, dtype=jnp.int32),
            vm(NH, rows, wide),
            vm(3, NH, rows, main),
            vm(NH, rows, 3 * LANES),
            vm(NH, rows, 3 * LANES),
            vm(NS, rows, 3 * NH * rest),
            vm(NH, NS, rows, wide),
            vm(NS, rows, width),
            vm(NH, NS, rows, hid),
            vm(NH, NS, rows, hid),
            vm(NH, NS, rows, hid),
            vm(NH, local, width),
            vm(NH, local, width),
            vm(NH, local, wide),
            vm(NH, local, wide),
            vm(group, wide),
            vm(group, wide),
            vm(group, wide // HEAD_DIM, dtype=F32),
            vm(local, width),
            vm(local, width, dtype=F32),
            vm(local, width, dtype=F32),
            vm(4, local, width),
            vm(4, local, width),
            vm(3, local, width),
            vm(6, local // 2, width),
            vm(group, hid),
            vm(group, hid),
            vm(group, hid),
            vm(NH, NS, rows, main),
            vm(NH, NS * rows, LANES),
            vm(NH, NS * rows, LANES),
            vm(NS, rows, NH * rest),
            vm(NS, rows, 2 * NH * rest),
            vm(group, wide),
            vm(group, HEAD_DIM, dtype=F32),
            vm(group, HEAD_DIM, dtype=F32),
            vm(2, NH, rows, main),
            vm(2, NH, rows, wide),
            vm(2, rows, width),
            vm(2, rows, NH * rest),
            vm(2, rows, 2 * NH * rest),
            vm(2, NH, rows, main),
            vm(2, rows, width),
            vm(2, rows, NH * rest),
            vm(2, rows, 2 * NH * rest),
            vm(NH, rows, main, dtype=F32),
            vm(rows, NH * rest, dtype=F32),
            vm(rows, 2 * NH * rest, dtype=F32),
            vm(NH, rows, LANES),
            vm(NH, rows, 2 * LANES),
            dma((15, 7)),
            dma((15, 7)),
            dma((4, 13)),
            dma((4, 13)),
            dma((4, 10)),
            dma((4, 10)),
            dma((6, 6)),
            dma((6, NS)),
            dma((7, 3)),
            dma((7, 4)),
            dma((24,)),
            dma((8,)),
        ],
        compiler_params=pltpu.CompilerParams(
            collective_id=0, has_side_effects=True, vmem_limit_bytes=127 << 19
        ),
        name="layer",
    )(q_weight, gate_weight, up_weight, down_rows, gain_one, gain_two, tokens, o_own, keys, values, cot_own, order, lengths)


def finish_kernel(
    q_weight,
    gate_weight,
    up_weight,
    gain_one,
    gain_two,
    q_sum,
    gate_main,
    up_main,
    down_main,
    down_tail,
    pair_tail,
    mixed_in,
    tokens_in,
    o_in,
    keys_in,
    values_in,
    mixed_out,
    d_tokens,
    d_keys,
    d_values,
    d_o,
    d_q,
    d_gate,
    d_up,
    d_down,
    d_gain_one,
    d_gain_two,
):
    for source, out in (
        (mixed_in, mixed_out),
        (tokens_in, d_tokens),
        (keys_in, d_keys),
        (values_in, d_values),
        (o_in, d_o),
    ):
        out[...] = source[...]
    rows = q_weight.shape[0]
    diagonal = lax.broadcasted_iota(jnp.int32, (rows, rows), 0) == lax.broadcasted_iota(
        jnp.int32, (rows, rows), 1
    )

    def column(gain):
        field = jnp.broadcast_to(gain[...].astype(F32), (rows, rows))
        return jnp.sum(jnp.where(diagonal, field, 0.0), axis=1, keepdims=True)

    def row(field):
        return jnp.sum(jnp.where(diagonal, field, 0.0), axis=0, keepdims=True)

    main = gate_main.shape[2]
    hid = gate_weight.shape[1] // NH
    rest = hid - main
    raw = q_sum[...].astype(F32)
    d_q[...] = raw * column(gain_one)
    d_gain_one[...] = row(jnp.sum(raw * q_weight[...].astype(F32), axis=1, keepdims=True))
    gain = column(gain_two)
    total = jnp.zeros((rows, 1), F32)
    for part, tail, base, weight, out in (
        (gate_main, pair_tail, 0, gate_weight, d_gate),
        (up_main, pair_tail, LANES, up_weight, d_up),
        (down_main, down_tail, 0, None, d_down),
    ):
        for p in range(NH):
            at = p * hid
            whole = jnp.concatenate([part[p], tail[p, :, base : base + rest]], axis=1).astype(F32)
            if weight is None:
                out[:, at : at + hid] = whole
            else:
                out[:, at : at + hid] = whole * gain
                own = weight[:, at : at + hid].astype(F32)
                total = total + jnp.sum(whole * own, axis=1, keepdims=True)
    d_gain_two[...] = row(total)


def finish_call(q_weight, gate_weight, up_weight, gain_one, gain_two, sums):
    rows, width = q_weight.shape
    cols = gate_weight.shape[1]
    local = sums[0].shape[0]

    def bf(*shape):
        return jax.ShapeDtypeStruct(shape, BF16)

    def f32(*shape):
        return jax.ShapeDtypeStruct(shape, F32)

    mixed, d_tokens, o_sum, d_keys, d_values, q_sum, gate, up, down, down_tail, pair_tail = sums
    return pl.pallas_call(
        finish_kernel,
        out_shape=[
            bf(local, width),
            bf(local, width),
            bf(local, width),
            bf(local, width),
            f32(rows, width),
            f32(rows, width),
            f32(rows, cols),
            f32(rows, cols),
            f32(rows, cols),
            f32(1, rows),
            f32(1, rows),
        ],
        in_specs=[VMEM] * 16,
        out_specs=[VMEM] * 11,
        compiler_params=pltpu.CompilerParams(vmem_limit_bytes=60 << 20),
        name="finish",
    )(
        q_weight, gate_weight, up_weight, gain_one, gain_two,
        q_sum, gate, up, down, down_tail, pair_tail,
        mixed, d_tokens, o_sum, d_keys, d_values,
    )


def per_device(
    nh,
    ns,
    tokens,
    keys,
    values,
    q_weight,
    o_weight,
    gate_weight,
    up_weight,
    down_weight,
    attn_gain,
    ffn_gain,
    span_order,
    doc_lengths,
    cotangent,
):
    gain_one, gain_two = attn_gain[None], ffn_gain[None]
    sums = layer_call(
        q_weight,
        gate_weight,
        up_weight,
        down_weight.T,
        gain_one,
        gain_two,
        tokens,
        o_weight,
        keys,
        values,
        cotangent,
        span_order,
        doc_lengths,
    )[:11]
    (
        mixed_out, grad_tokens, grad_keys, grad_values, grad_o, grad_q, grad_gate, grad_up,
        grad_down, grad_gain_one, grad_gain_two,
    ) = finish_call(q_weight, gate_weight, up_weight, gain_one, gain_two, sums)
    return (
        mixed_out,
        grad_tokens,
        grad_keys,
        grad_values,
        grad_q,
        grad_o,
        grad_gate,
        grad_up,
        grad_down.T,
        grad_gain_one[0],
        grad_gain_two[0],
    )


def to_slices(weight, nh):
    rows, cols = weight.shape
    parts = weight.reshape(rows, nh, cols // nh).swapaxes(0, 1)
    return lax.all_to_all(parts, "head", 0, 0, tiled=False).reshape(nh * rows, cols // nh)


def from_slices(part, nh):
    rows, cols = part.shape
    parts = part.reshape(nh, rows // nh, cols)
    parts = lax.all_to_all(parts, "head", 0, 0, tiled=False)
    return parts.swapaxes(0, 1).reshape(rows // nh, nh * cols)


def gather_seq(part):
    return lax.all_gather(part, "seq", axis=0, tiled=True)


def scatter_seq(full):
    return lax.psum_scatter(full.astype(BF16), "seq", scatter_dimension=0, tiled=True)


def gather_head(part):
    return lax.all_gather(part, "head", axis=0, tiled=True)


def scatter_head(full):
    return lax.psum_scatter(full.astype(BF16), "head", scatter_dimension=0, tiled=True)


def per_device_plain(
    nh,
    ns,
    tokens,
    keys,
    values,
    q_weight,
    o_weight,
    gate_weight,
    up_weight,
    down_weight,
    attn_gain,
    ffn_gain,
    span_order,
    doc_lengths,
    cotangent,
):
    local, width = tokens.shape
    rows = q_weight.shape[0]

    def shuffle(field):
        return field.reshape(local, nh, ns, rows).swapaxes(1, 2).reshape(local, width)

    def unshuffle(field):
        return field.reshape(local, ns, nh, rows).swapaxes(1, 2).reshape(local, width)

    gain_one = attn_gain.astype(F32)[:, None]
    gain_two = ffn_gain.astype(F32)[:, None]
    inputs = tokens.astype(F32)
    scale_one = rms_scale(inputs)
    normed_one = inputs * scale_one
    normed_one_all = gather_head(shuffle(normed_one.astype(BF16)))
    w_q = gather_seq(to_slices((q_weight * gain_one).astype(BF16), nh))
    key_heads = to_slices(keys, nh)
    value_heads = to_slices(values, nh)
    w_o = gather_seq(o_weight)
    w_gate = gather_seq(to_slices((gate_weight * gain_two).astype(BF16), nh))
    w_up = gather_seq(to_slices((up_weight * gain_two).astype(BF16), nh))
    w_down = gather_seq(to_slices(down_weight.T, nh))
    cotangent_all = gather_head(shuffle(cotangent))

    group = normed_one_all.shape[0]
    position, segment = places(span_order[0], doc_lengths[0], group)
    place_q = jnp.stack([position, segment], axis=1)
    place_k = jnp.stack([position, segment], axis=0)

    query = dot(normed_one_all, w_q, ((1,), (0,))).astype(BF16)
    attended, lse = attend(query, key_heads, value_heads, place_q, place_k)
    hidden = inputs + scatter_head(dot(attended, w_o, ((1,), (0,)))).astype(F32)
    scale_two = rms_scale(hidden)
    normed_two = hidden * scale_two
    normed_two_all = gather_head(shuffle(normed_two.astype(BF16)))

    gate = dot(normed_two_all, w_gate, ((1,), (0,)))
    up = dot(normed_two_all, w_up, ((1,), (0,)))
    sigma = jax.nn.sigmoid(gate)
    act = (gate * sigma * up).astype(BF16)
    down_sum = scatter_seq(dot(cotangent_all, act, ((0,), (0,))))
    grad_act = dot(cotangent_all, w_down, ((1,), (0,)))
    grad_gate = (grad_act * up * sigma * (1.0 + gate * (1.0 - sigma))).astype(BF16)
    grad_up = (grad_act * gate * sigma).astype(BF16)
    spread_two = dot(grad_gate, w_gate, ((1,), (1,))) + dot(grad_up, w_up, ((1,), (1,)))
    scaled_two = unshuffle(scatter_head(spread_two)).astype(F32)
    gate_sum = scatter_seq(dot(normed_two_all, grad_gate, ((0,), (0,))))
    up_sum = scatter_seq(dot(normed_two_all, grad_up, ((0,), (0,))))
    mixed = unshuffle(scatter_head(dot(act, w_down, ((1,), (1,)))))
    mixed_out = (hidden + mixed.astype(F32)).astype(BF16)

    grad_hidden = cotangent.astype(F32) + scale_two * (
        scaled_two - normed_two * jnp.mean(scaled_two * normed_two, axis=-1, keepdims=True)
    )
    grad_hidden_all = gather_head(grad_hidden.astype(BF16))
    grad_attended = dot(grad_hidden_all, w_o, ((1,), (1,))).astype(BF16)
    o_sum = scatter_seq(dot(attended, grad_hidden_all, ((0,), (0,))))
    grad_query, grad_keys, grad_values = attend_back(
        query, key_heads, value_heads, grad_attended, lse, place_q, place_k
    )
    grad_keys = from_slices(grad_keys, nh)
    grad_values = from_slices(grad_values, nh)
    scaled_one = unshuffle(scatter_head(dot(grad_query, w_q, ((1,), (1,))))).astype(F32)
    q_sum = scatter_seq(dot(normed_one_all, grad_query, ((0,), (0,))))
    grad_tokens = grad_hidden + scale_one * (
        scaled_one - normed_one * jnp.mean(scaled_one * normed_one, axis=-1, keepdims=True)
    )
    q_sum = from_slices(q_sum, nh).astype(F32)
    gate_sum = from_slices(gate_sum, nh).astype(F32)
    up_sum = from_slices(up_sum, nh).astype(F32)
    down_sum = from_slices(down_sum, nh).astype(F32)
    grad_gain_one = jnp.sum(q_weight.astype(F32) * q_sum, axis=1)
    grad_gain_two = jnp.sum(
        gate_weight.astype(F32) * gate_sum + up_weight.astype(F32) * up_sum, axis=1
    )
    return (
        mixed_out,
        grad_tokens.astype(BF16),
        grad_keys,
        grad_values,
        gain_one * q_sum,
        o_sum.astype(F32),
        gain_two * gate_sum,
        gain_two * up_sum,
        down_sum.T,
        grad_gain_one,
        grad_gain_two,
    )


def solution(mesh):
    both = ("head", "seq")
    nh, ns = mesh.shape["head"], mesh.shape["seq"]
    body = per_device if (nh, ns) == (NH, NS) else per_device_plain
    rows, cols, line, own = P(both, None), P(None, both), P(both), P("seq", None)
    return jax.shard_map(
        functools.partial(body, nh, ns),
        mesh=mesh,
        in_specs=(rows,) * 7 + (cols, line, line, own, own, rows),
        out_specs=(rows,) * 8 + (cols, line, line),
        check_vma=False,
    )
```

```python
import functools
import math

import jax
import jax.numpy as jnp
from jax import lax
from jax.experimental import pallas as pl
from jax.experimental.pallas import tpu as pltpu
from jax.sharding import PartitionSpec as P

HEAD_DIM = 128
NH, NS = 8, 4
EPS = 1e-06
BF16 = jnp.bfloat16
F32 = jnp.float32


def rms_scale(field):
    return lax.rsqrt(jnp.mean(field * field, axis=-1, keepdims=True) + EPS)


def dot(left, right, dims):
    return lax.dot_general(left, right, (dims, ((), ())), preferred_element_type=F32)


def places(order_row, length_row, group):
    count = order_row.shape[0]
    width = group // count
    slots = jnp.arange(group, dtype=jnp.int32)
    which = slots // width
    picked = jnp.where(
        which[:, None] == jnp.arange(count, dtype=jnp.int32)[None, :], order_row[None, :], 0
    )
    position = jnp.sum(picked, axis=1) * width + slots % width
    bounds = jnp.cumsum(length_row)
    segment = jnp.sum((position[:, None] >= bounds[None, :]).astype(jnp.int32), axis=1)
    return (position, segment)


def attend_kernel(q_ref, k_ref, v_ref, place_q, place_k, out_ref, lse_ref):
    scale = 1.0 / math.sqrt(HEAD_DIM)
    raw = dot(q_ref[...], k_ref[...], ((1,), (1,)))
    allowed = (place_q[:, 1:2] == place_k[1:2, :]) & (place_k[0:1, :] <= place_q[:, 0:1])
    logits = jnp.where(allowed, raw * scale, -1e30)
    top = jnp.max(logits, axis=-1, keepdims=True)
    expo = jnp.exp(logits - top)
    total = jnp.sum(expo, axis=-1, keepdims=True)
    probs = expo * (1.0 / total)
    out_ref[...] = dot(probs.astype(BF16), v_ref[...], ((1,), (0,))).astype(BF16)
    lse_ref[...] = jnp.broadcast_to(top + jnp.log(total), lse_ref.shape)


def attend(query, keys, values, place_q, place_k):
    group, width = query.shape
    heads = width // HEAD_DIM
    rows = min(group, 256)
    block = pl.BlockSpec((rows, HEAD_DIM), lambda h, i: (i, h))
    whole = pl.BlockSpec((group, HEAD_DIM), lambda h, i: (0, h))
    return pl.pallas_call(
        attend_kernel,
        grid=(heads, group // rows),
        in_specs=[
            block,
            whole,
            whole,
            pl.BlockSpec((rows, 2), lambda h, i: (i, 0)),
            pl.BlockSpec((2, group), lambda h, i: (0, 0)),
        ],
        out_specs=[block, block],
        out_shape=[
            jax.ShapeDtypeStruct((group, width), BF16),
            jax.ShapeDtypeStruct((group, width), F32),
        ],
        compiler_params=pltpu.CompilerParams(vmem_limit_bytes=48 << 20),
        cost_estimate=pl.CostEstimate(
            flops=4 * group * group * width,
            bytes_accessed=12 * group * width,
            transcendentals=heads * group * group,
        ),
        name="attend",
    )(query, keys, values, place_q, place_k)


def attend_back_kernel(
    q_ref, k_ref, v_ref, do_ref, lse_ref, place_q, place_k, dq_ref, dk_ref, dv_ref, dk_sum, dv_sum
):
    step = pl.program_id(1)
    scale = 1.0 / math.sqrt(HEAD_DIM)
    query, keys, grad = q_ref[...], k_ref[...], do_ref[...]
    raw = dot(query, keys, ((1,), (1,)))
    allowed = (place_q[:, 1:2] == place_k[1:2, :]) & (place_k[0:1, :] <= place_q[:, 0:1])
    logits = jnp.where(allowed, raw * scale, -1e30)
    probs = jnp.exp(logits - lse_ref[:, :1])
    grad_probs = dot(grad, v_ref[...], ((1,), (1,)))
    inner = jnp.sum(probs * grad_probs, axis=-1, keepdims=True)
    grad_raw = (probs * (grad_probs - inner) * scale).astype(BF16)
    dq_ref[...] = dot(grad_raw, keys, ((1,), (0,))).astype(BF16)

    @pl.when(step == 0)
    def _():
        dk_sum[...] = jnp.zeros_like(dk_sum)
        dv_sum[...] = jnp.zeros_like(dv_sum)

    dk_sum[...] += dot(grad_raw, query, ((0,), (0,)))
    dv_sum[...] += dot(probs.astype(BF16), grad, ((0,), (0,)))

    @pl.when(step == pl.num_programs(1) - 1)
    def _():
        dk_ref[...] = dk_sum[...].astype(BF16)
        dv_ref[...] = dv_sum[...].astype(BF16)


def attend_back(query, keys, values, grad, lse, place_q, place_k):
    group, width = query.shape
    heads = width // HEAD_DIM
    rows = min(group, 256)
    block = pl.BlockSpec((rows, HEAD_DIM), lambda h, i: (i, h))
    whole = pl.BlockSpec((group, HEAD_DIM), lambda h, i: (0, h))
    full = jax.ShapeDtypeStruct((group, width), BF16)
    return pl.pallas_call(
        attend_back_kernel,
        grid=(heads, group // rows),
        in_specs=[
            block,
            whole,
            whole,
            block,
            block,
            pl.BlockSpec((rows, 2), lambda h, i: (i, 0)),
            pl.BlockSpec((2, group), lambda h, i: (0, 0)),
        ],
        out_specs=[block, whole, whole],
        out_shape=[full, full, full],
        scratch_shapes=[pltpu.VMEM((group, HEAD_DIM), F32)] * 2,
        compiler_params=pltpu.CompilerParams(vmem_limit_bytes=48 << 20),
        cost_estimate=pl.CostEstimate(
            flops=10 * group * group * width,
            bytes_accessed=18 * group * width,
            transcendentals=heads * group * group,
        ),
        name="attend_back",
    )(query, keys, values, grad, lse, place_q, place_k)


MESH = pl.DeviceIdType.MESH
ANY = pl.BlockSpec(memory_space=pl.ANY)
VMEM = pl.BlockSpec(memory_space=pltpu.VMEM)
SMEM = pl.BlockSpec(memory_space=pltpu.SMEM)
LANES = 128


def slices_of(weight, nh):
    rows, cols = weight.shape
    return weight.reshape(rows, nh, cols // nh).swapaxes(0, 1)


def rows_of(parts):
    nh, rows, cols = parts.shape
    return parts.swapaxes(0, 1).reshape(rows, nh * cols)


def flat(parts):
    return parts.reshape(parts.shape[0] * parts.shape[1], parts.shape[2])


def remote(src, dst, send, recv, to):
    return pltpu.make_async_remote_copy(
        src_ref=src, dst_ref=dst, send_sem=send, recv_sem=recv, device_id=to, device_id_type=MESH
    )


class Net:
    def __init__(self):
        self.h = lax.axis_index("head")
        self.s = lax.axis_index("seq")

    def peer(self, k):
        return (lax.bitwise_xor(self.h, k), self.s)

    def greet(self):
        barrier = pltpu.get_barrier_semaphore()
        for k in range(1, NH):
            pl.semaphore_signal(barrier, inc=1, device_id=self.peer(k), device_id_type=MESH)
        for k in range(1, NS):
            there = (self.h, lax.rem(self.s + k, NS))
            pl.semaphore_signal(barrier, inc=1, device_id=there, device_id_type=MESH)
        pl.semaphore_wait(barrier, NH - 1 + NS - 1)

    def swap(self, src, dst, send, recv, own):
        mine = pltpu.make_async_copy(src(self.h), dst(self.h), own)
        mine.start()
        copies = []
        for k in (6, 2, 4, 1, 5, 3, 7):
            to = self.peer(k)
            copy = remote(src(to[0]), dst(self.h), send.at[k - 1], recv.at[k - 1], to)
            copy.start()
            copies.append(copy)

        def finish():
            for copy in copies:
                copy.wait()
            mine.wait()

        return finish

    def gather(self, src, dst, send, recv, own):
        half = src.shape[0] // 2
        lo, hi = pl.ds(0, half), pl.ds(half, half)
        h, core, px, py = self.h, self.peer(1), self.peer(2), self.peer(4)
        x, y, d = px[0], py[0], lax.bitwise_xor(h, 6)
        mine = pltpu.make_async_copy(src, dst.at[h], own)
        mine.start()
        copies = []

        def put(i, a, b, to):
            copy = remote(a, b, send.at[i], recv.at[i], to)
            copy.start()
            copies.append(copy)
            return copy

        def on(i, block, rows, to):
            return put(i, dst.at[block, rows], dst.at[block, rows], to)

        xa = put(0, src.at[lo], dst.at[h, lo], px)
        yb = put(1, src.at[hi], dst.at[h, hi], py)
        near = [put(2, src, dst.at[h], core)]
        xb = put(3, src.at[hi], dst.at[h, hi], px)
        ya = put(4, src.at[lo], dst.at[h, lo], py)
        far = []

        def relay():
            xa.wait_recv()
            far.append(on(5, x, lo, py))
            near.append(on(6, x, lo, core))
            yb.wait_recv()
            far.append(on(7, y, hi, px))
            near.append(on(8, y, hi, core))
            xb.wait_recv()
            near.append(on(9, x, hi, core))
            ya.wait_recv()
            near.append(on(10, y, lo, core))

        def finish():
            far[0].wait_recv()
            near.append(on(11, d, lo, core))
            far[1].wait_recv()
            near.append(on(12, d, hi, core))
            for copy in near:
                copy.wait_recv()
            mine.wait()
            for copy in copies:
                copy.wait_send()

        return relay, finish

    def scatter(self, source, block, core_in, held, far_in, send, recv, read):
        core, px, py = self.peer(1), self.peer(2), self.peer(4)
        half = held.shape[1] // 2
        lo, hi = pl.ds(0, half), pl.ds(half, half)
        copies = []

        def put(i, a, b, to):
            copy = remote(a, b, send.at[i], recv.at[i], to)
            copy.start()
            copies.append(copy)
            return copy

        order = (6, 2, 4, 0)
        near = []
        for i in (0, 2):
            pair = [lax.bitwise_xor(core[0], k) for k in order[i : i + 2]]
            for j, value in enumerate(block(pair)):
                near.append(put(i + j, source(i + j, value), core_in.at[i + j], core))
        far = []
        for i, k in enumerate(order):
            if i % 2 == 0:
                pair = block([lax.bitwise_xor(self.h, k) for k in order[i : i + 2]])
            value = pair[i % 2]
            near[i].wait_recv()
            value = value + read(core_in.at[i]).astype(F32)
            if k:
                held[i] = value.astype(BF16)
            if k == 6:
                far.append(put(4, held.at[0, lo], far_in.at[0], px))
                far.append(put(5, held.at[0, hi], far_in.at[1], py))
            elif k == 2:
                far.append(put(6, held.at[1, lo], far_in.at[2], px))
            elif k == 4:
                far.append(put(7, held.at[2, hi], far_in.at[3], py))

        def pass_on(i, slot, rows, arrived, to):
            arrived.wait_recv()
            joined = held[slot, rows].astype(F32) + read(far_in.at[i]).astype(F32)
            held[slot, rows] = joined.astype(BF16)
            far.append(put(8 + i, held.at[slot, rows], far_in.at[4 + i], to))

        def relay():
            pass_on(0, 2, lo, far[0], py)
            pass_on(1, 1, hi, far[1], px)

        def finish():
            parts = []
            for i, rows in enumerate((slice(0, half), slice(half, 2 * half))):
                part = value[rows]
                for j in (2 + i, 4 + i):
                    far[j].wait_recv()
                    part = part + read(far_in.at[j]).astype(F32)
                parts.append(part)
            for copy in copies:
                copy.wait_send()
            return jnp.concatenate(parts, axis=0)

        return relay, finish

    def z_gather(self, src, block, send, recv):
        s = self.s
        ends = (s == 0) | (s == NS - 1)
        middle = jnp.logical_not(ends)
        across = NS - 1 - s
        near = jnp.where(s == 1, 0, NS - 1)
        steps = ((2, s == 0), (-2, s == NS - 1), (1, s < NS - 1), (-1, s > 0))
        relayed = (across, NS - 1 - near)

        def copy(n):
            return remote(src, block(s), send.at[n], recv.at[s], (self.h, s + steps[n][0]))

        def relay(k):
            origin = relayed[k]
            return remote(block(origin), block(origin), send.at[4 + k], recv.at[origin], (self.h, near))

        for n, (_, where) in enumerate(steps):

            @pl.when(where)
            def _():
                copy(n).start()

        def forward():
            @pl.when(middle)
            def _():
                for k in range(2):
                    relay(k).wait_recv()
                    relay(k).start()

        def finish():
            for t in range(NS):
                waited = ((s == 1) & (t >= 2)) | ((s == 2) & (t < 2))

                @pl.when((s != t) & jnp.logical_not(waited))
                def _():
                    remote(block(t), block(t), send.at[0], recv.at[t], (self.h, s)).wait_recv()

        def drain():
            for n, (_, where) in enumerate(steps):

                @pl.when(where)
                def _():
                    copy(n).wait_send()

            @pl.when(middle)
            def _():
                for k in range(2):
                    relay(k).wait_send()

        return forward, finish, drain


def z_scatter(net, block, value, got, comb, join_v, bufs, send, recv, sems):
    s = net.s
    ends = (s == 0) | (s == NS - 1)
    middle = jnp.logical_not(ends)
    inner = jnp.where(s == 0, 1, NS - 2)
    near = jnp.where(s == 1, 0, NS - 1)
    goals = (NS - 1 - s, NS - 1 - near)
    end_blocks = (NS - 1 - inner, NS - 1 - s)

    def to_join(k):
        return remote(block(end_blocks[k]), comb.at[k], send.at[k], recv.at[2 + k], (net.h, inner))

    def joined(k):
        return remote(join_v.at[k], got.at[1], send.at[k], recv.at[1], (net.h, goals[k]))

    def direct(t):
        return remote(block(t), got.at[0], send.at[2], recv.at[0], (net.h, t))

    def start():
        @pl.when(ends)
        def _():
            to_join(1).start()
            to_join(0).start()
            direct(inner).start()

        @pl.when(middle)
        def _():
            direct(near).start()

    def join():
        @pl.when(middle)
        def _():
            for k in (1, 0):
                to_join(k).wait_recv()
                copy = pltpu.make_async_copy(comb.at[k], join_v.at[k], sems.at[6 + k])
                copy.start()
                copy.wait()
                term = join_v[k].astype(F32) + value(goals[k]).astype(F32)
                join_v[k] = term.astype(BF16)
                joined(k).start()

    def finish(total):
        total[...] = value(s).astype(F32)
        takes = []
        for k in range(2):
            remote(got.at[k], got.at[k], send.at[0], recv.at[k], (net.h, s)).wait_recv()
            takes.append(pltpu.make_async_copy(got.at[k], bufs.at[k], sems.at[4 + k]))
            takes[k].start()
        for k in range(2):
            takes[k].wait()
            total[...] += bufs[k].astype(F32)

    def drain():
        @pl.when(ends)
        def _():
            to_join(0).wait_send()
            to_join(1).wait_send()
            direct(inner).wait_send()

        @pl.when(middle)
        def _():
            joined(0).wait_send()
            joined(1).wait_send()
            direct(near).wait_send()

    return start, join, finish, drain


def make_places(order, lengths, place_q, place_k):
    group, count = place_q.shape[0], order.shape[1]
    width = group // count
    for shape, dim in (((group, 1), 0), ((1, group), 1)):
        slots = lax.broadcasted_iota(jnp.int32, shape, dim)
        position = slots
        for c in range(count):
            inside = (slots >= c * width) & (slots < (c + 1) * width)
            position = jnp.where(inside, slots + (order[0, c] - c) * width, position)
        segment = jnp.zeros(shape, jnp.int32)
        bound = 0
        for j in range(lengths.shape[1]):
            bound = bound + lengths[0, j]
            segment = segment + (position >= bound).astype(jnp.int32)
        if dim == 0:
            place_q[:, 0:1] = position
            place_q[:, 1:2] = segment
        else:
            place_k[0:1, :] = position
            place_k[1:2, :] = segment


def mask(place_q, place_k, rows):
    return (place_q[rows, 1:2] == place_k[1:2, :]) & (place_k[0:1, :] <= place_q[rows, 0:1])


def lane_block(w, p, wide):
    return w.at[:, pl.ds(pl.multiple_of(p * wide, wide), wide)]


def load(pairs, sems, base):
    copies = [pltpu.make_async_copy(a, b, sems.at[base + i]) for i, (a, b) in enumerate(pairs)]
    for copy in copies:
        copy.start()

    def finish():
        for copy in copies:
            copy.wait()

    return finish


def layer_kernel(
    q_weight,
    gate_weight,
    up_weight,
    down_rows,
    gain_one,
    gain_two,
    tokens,
    o_own,
    keys,
    values,
    cot_own,
    order,
    lengths,
    mixed_out,
    d_tokens,
    o_out,
    d_keys,
    d_values,
    q_out,
    gate_out,
    up_out,
    down_out,
    down_tail_out,
    pair_tail_out,
    n1_all,
    mixed_near,
    mixed_far,
    got_ffn,
    comb_ffn,
    got_q,
    comb_q,
    got_o,
    comb_o,
    got_dt,
    comb_dt,
    got_pt,
    comb_pt,
    place_q,
    place_k,
    q_own,
    parts,
    tails_own,
    tails_in,
    tails,
    wq_v,
    wo_v,
    wg_v,
    wu_v,
    wd_v,
    norm_v,
    wide_v,
    k_v,
    v_v,
    query,
    attended,
    lse,
    norm_own,
    hidden_v,
    dh_v,
    near_out,
    core_in,
    held,
    far_in,
    act_v,
    grad_gate,
    grad_up,
    down_term,
    stage,
    stage_two,
    down_tail,
    pair_tail,
    dq_v,
    dk_sum,
    dv_sum,
    joins,
    q_join,
    o_join,
    dt_join,
    pt_join,
    bufs,
    o_bufs,
    dt_bufs,
    pt_bufs,
    total,
    dt_total,
    pt_total,
    dt_back,
    pt_back,
    swap_send,
    swap_recv,
    ag_send,
    ag_recv,
    rs_send,
    rs_recv,
    zg_send,
    zg_recv,
    zs_send,
    zs_recv,
    own,
    load_sem,
):
    net = Net()
    h, s = net.h, net.s
    local, width = tokens.shape
    group = NH * local
    wide, hid = query.shape[1], act_v.shape[1]
    main = parts.shape[3]
    rest = hid - main
    step = 256
    tiles = group // step
    fold = width // NH
    scale = 1.0 / math.sqrt(HEAD_DIM)
    body = pl.ds(0, main)
    net.greet()

    def swap(j, src, dst):
        return net.swap(src, dst, swap_send.at[j], swap_recv.at[j], own.at[j])

    def gather(j, src, dst):
        return net.gather(src, dst, ag_send.at[j], ag_recv.at[j], own.at[20 + j])

    def z_gather(j, src, block):
        return net.z_gather(src, block, zg_send.at[j], zg_recv.at[j])

    def slab(w):
        return lambda t: w.at[:, t, :, body]

    def tile_rows(i):
        return pl.ds(pl.multiple_of(i * step, step), step)

    def token_tile(field, i):
        return field[pl.ds(i * (step // local), step // local)].reshape(step, width)

    def own_rows(p):
        return pl.ds(pl.multiple_of(p * local, local), local)

    zo = z_gather(0, o_own, lambda t: wo_v.at[t])
    o_here = load([(o_own, wo_v.at[s])], load_sem, 0)
    rows = q_weight.shape[0]
    diagonal = lax.broadcasted_iota(jnp.int32, (rows, rows), 0) == lax.broadcasted_iota(
        jnp.int32, (rows, rows), 1
    )

    def column(gain):
        field = jnp.broadcast_to(gain[...].astype(F32), (rows, rows))
        return jnp.sum(jnp.where(diagonal, field, 0.0), axis=1, keepdims=True)

    field = (q_weight[...].astype(F32) * column(gain_one)).astype(BF16)
    for p in range(NH):
        q_own[p] = field[:, p * wide : (p + 1) * wide]
    q_there = swap(0, lambda p: q_own.at[p], lambda p: wq_v.at[p, s])
    ffn = ((gate_weight, gain_two), (up_weight, gain_two), (down_rows, None))
    ffn_v = (wg_v, wu_v, wd_v)

    def slices(j):
        weight, gain = ffn[j]
        field = weight[...]
        if gain is not None:
            field = (field.astype(F32) * column(gain)).astype(BF16)
        for p in range(NH):
            parts[j, p] = field[:, p * hid : p * hid + main]
            tails_own[p, :, j * LANES : j * LANES + rest] = field[:, p * hid + main : (p + 1) * hid]
        return swap(
            1 + j, lambda p: parts.at[j, p], lambda p: ffn_v[j].at[p, s, :, body]
        )

    gate_there = slices(0)
    inputs = tokens[...].astype(F32)
    norm_own[...] = (inputs * rms_scale(inputs)).astype(BF16)
    n1_there = gather(0, norm_own, n1_all)
    q_there()
    zq = z_gather(1, wq_v.at[:, s], lambda t: wq_v.at[:, t])
    k_there = swap(5, lambda p: lane_block(keys, p, wide), lambda p: k_v.at[p])
    v_there = swap(6, lambda p: lane_block(values, p, wide), lambda p: v_v.at[p])
    zo[0]()
    gate_there()
    zg = z_gather(2, wg_v.at[:, s, :, body], slab(wg_v))
    n1_there[0]()
    zq[0]()
    n1_there[1]()
    n1_here = load([(n1_all, norm_v)], load_sem, 1)
    up_there = slices(1)
    make_places(order, lengths, place_q, place_k)
    k_there()
    v_there()
    zq[1]()
    n1_here()

    @pl.loop(0, tiles)
    def _(i):
        query[tile_rows(i), :] = dot(
            token_tile(norm_v, i), wq_v[...].reshape(width, wide), ((1,), (0,))
        ).astype(BF16)

    down_there = slices(2)
    tails_there = swap(4, lambda p: tails_own.at[p], lambda p: tails_in.at[p])
    up_there()
    zu = z_gather(4, wu_v.at[:, s, :, body], slab(wu_v))

    for head in range(wide // HEAD_DIM):
        cols = slice(head * HEAD_DIM, (head + 1) * HEAD_DIM)

        @pl.loop(0, tiles)
        def _(i):
            rows = tile_rows(i)
            raw = dot(query[rows, cols], k_v[:, :, cols].reshape(group, HEAD_DIM), ((1,), (1,)))
            logits = jnp.where(mask(place_q, place_k, rows), raw * scale, -1e30)
            top = jnp.max(logits, axis=-1, keepdims=True)
            expo = jnp.exp(logits - top)
            norm = jnp.sum(expo, axis=-1, keepdims=True)
            probs = (expo * (1.0 / norm)).astype(BF16)
            attended[rows, cols] = dot(
                probs, v_v[:, :, cols].reshape(group, HEAD_DIM), ((1,), (0,))
            ).astype(BF16)
            lse[rows, head : head + 1] = top + jnp.log(norm)

        if head == 0:
            zg[0]()

    tails_there()
    for j in range(3):
        for p in range(NH):
            at = (j * NH + p) * rest
            tails[s, :, at : at + rest] = tails_in[p, :, j * LANES : j * LANES + rest]
    pair, last = pl.ds(0, 2 * NH * rest), pl.ds(2 * NH * rest, NH * rest)
    zt = z_gather(3, tails.at[s, :, pair], lambda t: tails.at[t, :, pair])
    zl = z_gather(6, tails.at[s, :, last], lambda t: tails.at[t, :, last])
    down_there()
    zd = z_gather(5, wd_v.at[:, s, :, body], slab(wd_v))
    zo[1]()
    o_here()

    def scatter(
        j, block, core=core_in, far=far_in, read=lambda ref: ref[...], near=near_out, keep=held
    ):
        def source(i, value):
            near[i] = value.astype(BF16)
            return near.at[i]

        return net.scatter(source, block, core, keep, far, rs_send.at[j], rs_recv.at[j], read)

    def rows_of_heads(field, heads):
        return jnp.concatenate([field[own_rows(p), :] for p in heads], axis=0)

    def halves(value):
        return value[:local], value[local:]

    def o_block(heads):
        part = rows_of_heads(attended, heads)
        return halves(dot(part, wo_v[...].reshape(wide, width), ((1,), (0,))))

    o_sum = scatter(0, o_block)
    o_sum[0]()
    zu[0]()
    hidden = tokens[...].astype(F32) + o_sum[1]()
    hidden_v[...] = hidden
    norm_own[...] = (hidden * rms_scale(hidden)).astype(BF16)
    n2_there = gather(2, norm_own, norm_v)
    n2_there[0]()
    zt[0]()
    n2_there[1]()
    zl[0]()
    zd[0]()
    cot_there = gather(1, cot_own, wide_v)
    cot_there[0]()
    zt[1]()

    def matrix(w):
        return w[...].reshape(width, hid)

    def add_tail(j):
        for p in range(NH):
            at = (j * NH + p) * rest
            ffn_v[j][p, :, :, main:hid] = tails[:, :, at : at + rest]

    zg[1]()
    add_tail(0)
    @pl.loop(0, tiles)
    def _(i):
        rows = tile_rows(i)
        gate = dot(token_tile(norm_v, i), matrix(wg_v), ((1,), (0,)))
        sigma = jax.nn.sigmoid(gate)
        grad_up[rows, :] = (gate * sigma).astype(BF16)
        grad_gate[rows, :] = (sigma * (1.0 + gate * (1.0 - sigma))).astype(BF16)

    zu[1]()
    add_tail(1)

    @pl.loop(0, tiles)
    def _(i):
        rows = tile_rows(i)
        up = dot(token_tile(norm_v, i), matrix(wu_v), ((1,), (0,)))
        act_v[rows, :] = (grad_up[rows, :].astype(F32) * up).astype(BF16)
        grad_gate[rows, :] = (grad_gate[rows, :].astype(F32) * up).astype(BF16)

    cot_there[1]()

    def columns(field, i):
        cols = pl.ds(pl.multiple_of(i * fold, fold), fold)
        return field[:, :, cols].reshape(group, fold)

    def put_term(i, left, right, body_ref, tail_ref):
        value = dot(left, right, ((0,), (0,))).astype(BF16)
        body_ref[i, :, :, body] = value[:, :main].reshape(NS, fold // NS, main)
        tail_ref[i, :, 0:rest] = value[:, main:]

    def pack(tail_ref, out, base):
        for p in range(NH):
            at = (base * NH + p) * rest
            out[:, :, at : at + rest] = tail_ref[p, :, 0:rest].reshape(NS, fold // NS, rest)

    @pl.loop(0, NH)
    def _(i):
        put_term(i, columns(wide_v, i), act_v[...], down_term, stage)

    pack(stage, down_tail, 0)

    def z_sum(j, block, value, got, comb, join, buf):
        z = z_scatter(net, block, value, got, comb, join, buf, zs_send.at[j], zs_recv.at[j], load_sem)
        z[0]()
        return z

    def slab_value(w):
        return lambda t: w[:, pl.ds(t, 1), :, body].reshape(NH, fold // NS, main)

    def block_value(w):
        return lambda t: w[pl.ds(t, 1)].reshape(w.shape[1:])

    z_down = z_sum(
        0, slab(down_term), slab_value(down_term), got_ffn.at[0], comb_ffn.at[0], joins, bufs
    )
    z_dt = z_sum(
        1, lambda t: down_tail.at[t], block_value(down_tail), got_dt, comb_dt, dt_join, dt_bufs
    )
    zl[1]()
    zd[1]()
    add_tail(2)

    @pl.loop(0, tiles)
    def _(i):
        rows = tile_rows(i)
        grad_act = dot(token_tile(wide_v, i), matrix(wd_v), ((1,), (0,)))
        grad_gate[rows, :] = (grad_act * grad_gate[rows, :].astype(F32)).astype(BF16)
        grad_up[rows, :] = (grad_act * grad_up[rows, :].astype(F32)).astype(BF16)

    def spread_block(heads):
        value = dot(rows_of_heads(grad_gate, heads), matrix(wg_v), ((1,), (1,)))
        return halves(value + dot(rows_of_heads(grad_up, heads), matrix(wu_v), ((1,), (1,))))

    ffn_sum = scatter(1, spread_block)
    zg[2]()

    @pl.loop(0, NH)
    def _(i):
        put_term(i, columns(norm_v, i), grad_gate[...], wg_v, stage)

    z_gate = z_sum(
        2, slab(wg_v), slab_value(wg_v), got_ffn.at[1], comb_ffn.at[1], joins, bufs
    )
    ffn_sum[0]()
    z_down[1]()
    z_dt[1]()

    zu[2]()

    @pl.loop(0, NH)
    def _(i):
        put_term(i, columns(norm_v, i), grad_up[...], wu_v, stage_two)

    n1_here = load([(n1_all, norm_v)], load_sem, 0)
    z_up = z_sum(4, slab(wu_v), slab_value(wu_v), got_ffn.at[2], comb_ffn.at[2], joins, bufs)
    pack(stage, pair_tail, 0)
    pack(stage_two, pair_tail, 1)
    z_pt = z_sum(
        3, lambda t: pair_tail.at[t], block_value(pair_tail), got_pt, comb_pt, pt_join, pt_bufs
    )

    hidden = hidden_v[...]
    scale_two = rms_scale(hidden)
    normed_two = hidden * scale_two
    scaled_two = ffn_sum[1]()
    grad_hidden = cot_own[...].astype(F32) + scale_two * (
        scaled_two - normed_two * jnp.mean(scaled_two * normed_two, axis=-1, keepdims=True)
    )
    dh_v[...] = grad_hidden
    norm_own[...] = grad_hidden.astype(BF16)
    dh_there = gather(3, norm_own, wide_v)
    dh_there[0]()
    backs = []

    def back(j, z, out, result):
        z[2](total)
        result[...] = total[...].astype(BF16)
        backs.append(swap(j, lambda p: result.at[p], lambda p: out.at[p]))

    back(7, z_down, down_out, parts.at[2])
    z_dt[2](dt_total)
    for p in range(NH):
        dt_back[p, :, 0:rest] = dt_total[:, p * rest : (p + 1) * rest].astype(BF16)
    backs.append(swap(8, lambda p: dt_back.at[p], lambda p: down_tail_out.at[p]))
    dh_there[1]()
    z_down[3]()
    z_gate[1]()

    @pl.loop(0, tiles)
    def _(i):
        dq_v[tile_rows(i), :] = dot(
            token_tile(wide_v, i), wo_v[...].reshape(wide, width), ((1,), (1,))
        ).astype(BF16)

    for head in range(wide // HEAD_DIM):
        cols = slice(head * HEAD_DIM, (head + 1) * HEAD_DIM)
        dk_sum[...] = jnp.zeros_like(dk_sum)
        dv_sum[...] = jnp.zeros_like(dv_sum)

        @pl.loop(0, tiles)
        def _(i):
            rows = tile_rows(i)
            key_rows = k_v[:, :, cols].reshape(group, HEAD_DIM)
            part, grad = query[rows, cols], dq_v[rows, cols]
            raw = dot(part, key_rows, ((1,), (1,)))
            logits = jnp.where(mask(place_q, place_k, rows), raw * scale, -1e30)
            probs = jnp.exp(logits - lse[rows, head : head + 1])
            grad_probs = dot(grad, v_v[:, :, cols].reshape(group, HEAD_DIM), ((1,), (1,)))
            inner = jnp.sum(probs * grad_probs, axis=-1, keepdims=True)
            grad_raw = (probs * (grad_probs - inner) * scale).astype(BF16)
            dq_v[rows, cols] = dot(grad_raw, key_rows, ((1,), (0,))).astype(BF16)
            dk_sum[...] += dot(grad_raw, part, ((0,), (0,)))
            dv_sum[...] += dot(probs.astype(BF16), grad, ((0,), (0,)))

        k_v[:, :, cols] = dk_sum[...].astype(BF16).reshape(NH, local, HEAD_DIM)
        v_v[:, :, cols] = dv_sum[...].astype(BF16).reshape(NH, local, HEAD_DIM)

    def q_block(heads):
        part = rows_of_heads(dq_v, heads)
        return halves(dot(part, wq_v[...].reshape(width, wide), ((1,), (1,))))

    q_sum = scatter(2, q_block)
    q_sum[0]()
    n1_here()

    zq[2]()

    @pl.loop(0, NH)
    def _(i):
        part = dot(columns(norm_v, i), dq_v[...], ((0,), (0,)))
        wq_v[i] = part.astype(BF16).reshape(NS, fold // NS, wide)

    zq_sum = z_sum(
        5,
        lambda t: wq_v.at[:, t],
        lambda t: wq_v[:, pl.ds(t, 1)].reshape(NH, fold // NS, wide),
        got_q,
        comb_q,
        q_join,
        bufs.at[:, :, :, pl.ds(0, wide)],
    )

    zo[2]()

    @pl.loop(0, NH)
    def _(i):
        cols = pl.ds(pl.multiple_of(i * fold, fold), fold)
        part = dot(attended[...], columns(wide_v, i), ((0,), (0,)))
        wo_v[:, :, cols] = part.astype(BF16).reshape(NS, wide // NS, fold)

    zo_sum = z_sum(6, lambda t: wo_v.at[t], block_value(wo_v), got_o, comb_o, o_join, o_bufs)
    backs.append(swap(9, lambda p: k_v.at[p], lambda p: lane_block(d_keys, p, wide)))
    backs.append(swap(10, lambda p: v_v.at[p], lambda p: lane_block(d_values, p, wide)))
    z_gate[3]()
    z_up[1]()
    back(11, z_gate, gate_out, parts.at[0])

    inputs = tokens[...].astype(F32)
    scale_one = rms_scale(inputs)
    normed_one = inputs * scale_one
    scaled_one = q_sum[1]()
    d_tokens[...] = (
        dh_v[...]
        + scale_one
        * (scaled_one - normed_one * jnp.mean(scaled_one * normed_one, axis=-1, keepdims=True))
    ).astype(BF16)

    def mixed_block(heads):
        return halves(dot(rows_of_heads(act_v, heads), matrix(wd_v), ((1,), (1,))))

    def staged(ref):
        slot = norm_v.at[NH - 1, pl.ds(0, ref.shape[0])]
        load([(ref, slot)], load_sem, 2)()
        return slot[...]

    mixed_sum = scatter(
        3, mixed_block, mixed_near, mixed_far, staged, norm_v, norm_v.at[pl.ds(4, 3)]
    )
    back(12, z_up, up_out, parts.at[1])
    mixed_sum[0]()
    z_pt[1]()
    zq_sum[1]()
    zo_sum[1]()
    z_pt[2](pt_total)
    for j in range(2):
        for p in range(NH):
            at = (j * NH + p) * rest
            pt_back[p, :, j * LANES : j * LANES + rest] = pt_total[:, at : at + rest].astype(BF16)
    backs.append(swap(13, lambda p: pt_back.at[p], lambda p: pair_tail_out.at[p]))
    mixed_out[...] = (hidden_v[...] + mixed_sum[1]()).astype(BF16)
    q_total = total.at[:, :, pl.ds(0, wide)]
    zq_sum[2](q_total)
    q_own[...] = q_total[...].astype(BF16)
    backs.append(swap(14, lambda p: q_own.at[p], lambda p: lane_block(q_out, p, wide)))
    zo_sum[2](o_out)
    for done in backs:
        done()
    for z in (zt, zl, zd):
        z[2]()
    for z in (z_dt, z_pt, z_up, zq_sum, zo_sum):
        z[3]()


def layer_call(q_weight, gate_weight, up_weight, down_rows, gain_one, gain_two, tokens, o_own, keys, values, cot_own, order, lengths):
    local, width = tokens.shape
    group = NH * local
    rows = o_own.shape[0]
    wide, hid = width // NH, gate_weight.shape[1] // NH
    main = hid // LANES * LANES
    rest = hid - main

    def bf(*shape):
        return jax.ShapeDtypeStruct(shape, BF16)

    def vm(*shape, dtype=BF16):
        return pltpu.VMEM(shape, dtype)

    out_shape = [
        bf(local, width),
        bf(local, width),
        jax.ShapeDtypeStruct((rows, width), F32),
        bf(local, width),
        bf(local, width),
        bf(rows, width),
        bf(NH, rows, main),
        bf(NH, rows, main),
        bf(NH, rows, main),
        bf(NH, rows, LANES),
        bf(NH, rows, 2 * LANES),
        bf(NH, local, width),
        bf(4, local, width),
        bf(6, local // 2, width),
        bf(3, 2, NH, rows, main),
        bf(3, 2, NH, rows, main),
        bf(2, NH, rows, wide),
        bf(2, NH, rows, wide),
        bf(2, rows, width),
        bf(2, rows, width),
        bf(2, rows, NH * rest),
        bf(2, rows, NH * rest),
        bf(2, rows, 2 * NH * rest),
        bf(2, rows, 2 * NH * rest),
    ]
    dma = pltpu.SemaphoreType.DMA
    return pl.pallas_call(
        layer_kernel,
        out_shape=out_shape,
        in_specs=[VMEM] * 7 + [ANY] * 3 + [VMEM] + [SMEM] * 2,
        out_specs=[VMEM] * 3 + [ANY] * 21,
        scratch_shapes=[
            vm(group, 2, dtype=jnp.int32),
            vm(2, group, dtype=jnp.int32),
            vm(NH, rows, wide),
            vm(3, NH, rows, main),
            vm(NH, rows, 3 * LANES),
            vm(NH, rows, 3 * LANES),
            vm(NS, rows, 3 * NH * rest),
            vm(NH, NS, rows, wide),
            vm(NS, rows, width),
            vm(NH, NS, rows, hid),
            vm(NH, NS, rows, hid),
            vm(NH, NS, rows, hid),
            vm(NH, local, width),
            vm(NH, local, width),
            vm(NH, local, wide),
            vm(NH, local, wide),
            vm(group, wide),
            vm(group, wide),
            vm(group, wide // HEAD_DIM, dtype=F32),
            vm(local, width),
            vm(local, width, dtype=F32),
            vm(local, width, dtype=F32),
            vm(4, local, width),
            vm(4, local, width),
            vm(3, local, width),
            vm(6, local // 2, width),
            vm(group, hid),
            vm(group, hid),
            vm(group, hid),
            vm(NH, NS, rows, main),
            vm(NH, NS * rows, LANES),
            vm(NH, NS * rows, LANES),
            vm(NS, rows, NH * rest),
            vm(NS, rows, 2 * NH * rest),
            vm(group, wide),
            vm(group, HEAD_DIM, dtype=F32),
            vm(group, HEAD_DIM, dtype=F32),
            vm(2, NH, rows, main),
            vm(2, NH, rows, wide),
            vm(2, rows, width),
            vm(2, rows, NH * rest),
            vm(2, rows, 2 * NH * rest),
            vm(2, NH, rows, main),
            vm(2, rows, width),
            vm(2, rows, NH * rest),
            vm(2, rows, 2 * NH * rest),
            vm(NH, rows, main, dtype=F32),
            vm(rows, NH * rest, dtype=F32),
            vm(rows, 2 * NH * rest, dtype=F32),
            vm(NH, rows, LANES),
            vm(NH, rows, 2 * LANES),
            dma((15, 7)),
            dma((15, 7)),
            dma((4, 13)),
            dma((4, 13)),
            dma((4, 10)),
            dma((4, 10)),
            dma((7, 6)),
            dma((7, NS)),
            dma((7, 3)),
            dma((7, 4)),
            dma((24,)),
            dma((8,)),
        ],
        compiler_params=pltpu.CompilerParams(
            collective_id=0, has_side_effects=True, vmem_limit_bytes=127 << 19
        ),
        name="layer",
    )(q_weight, gate_weight, up_weight, down_rows, gain_one, gain_two, tokens, o_own, keys, values, cot_own, order, lengths)


def finish_kernel(*refs):
    ins, refs = refs[:16], refs[16:]
    outs, refs = refs[:11], refs[11:]
    vin, refs = refs[:16], refs[16:]
    vout, (in_sem, out_sem) = refs[:6], refs[6:]
    loads = [pltpu.make_async_copy(a, b, in_sem.at[i]) for i, (a, b) in enumerate(zip(ins, vin))]
    for copy in loads:
        copy.start()
    stores = []

    def store(i, source):
        copy = pltpu.make_async_copy(source, outs[i], out_sem.at[i])
        copy.start()
        stores.append(copy)

    q_weight, gate_weight, up_weight, gain_one, gain_two, q_sum = vin[:6]
    gate_main, up_main, down_main, down_tail, pair_tail = vin[6:11]
    d_q, d_gate, d_up, d_down, d_gain_one, d_gain_two = vout
    rows = q_weight.shape[0]
    diagonal = lax.broadcasted_iota(jnp.int32, (rows, rows), 0) == lax.broadcasted_iota(
        jnp.int32, (rows, rows), 1
    )

    def column(gain):
        field = jnp.broadcast_to(gain[...].astype(F32), (rows, rows))
        return jnp.sum(jnp.where(diagonal, field, 0.0), axis=1, keepdims=True)

    def row(field):
        return jnp.sum(jnp.where(diagonal, field, 0.0), axis=0, keepdims=True)

    hid = gate_weight.shape[1] // NH
    rest = hid - gate_main.shape[2]
    for i in (3, 4, 1, 6, 9, 10):
        loads[i].wait()
    gain = column(gain_two)
    total = jnp.zeros((rows, 1), F32)
    for i, part, tail, base, weight, out in (
        (6, gate_main, pair_tail, 0, gate_weight, d_gate),
        (7, up_main, pair_tail, LANES, up_weight, d_up),
        (8, down_main, down_tail, 0, None, d_down),
    ):
        if i > 6:
            loads[i].wait()
        if i == 7:
            loads[2].wait()
        for p in range(NH):
            at = p * hid
            whole = jnp.concatenate([part[p], tail[p, :, base : base + rest]], axis=1).astype(F32)
            if weight is None:
                out[:, at : at + hid] = whole
            else:
                out[:, at : at + hid] = whole * gain
                own = weight[:, at : at + hid].astype(F32)
                total = total + jnp.sum(whole * own, axis=1, keepdims=True)
        store(i, out)
    for i in range(5):
        loads[11 + i].wait()
        store(i, vin[11 + i])
    loads[0].wait()
    loads[5].wait()
    raw = q_sum[...].astype(F32)
    d_q[...] = raw * column(gain_one)
    store(5, d_q)
    d_gain_one[...] = row(jnp.sum(raw * q_weight[...].astype(F32), axis=1, keepdims=True))
    store(9, d_gain_one)
    d_gain_two[...] = row(total)
    store(10, d_gain_two)
    for copy in stores:
        copy.wait()


def finish_call(q_weight, gate_weight, up_weight, gain_one, gain_two, sums):
    rows, width = q_weight.shape
    cols = gate_weight.shape[1]
    mixed, d_tokens, o_sum, d_keys, d_values, q_sum, gate, up, down, down_tail, pair_tail = sums
    ins = (
        q_weight, gate_weight, up_weight, gain_one, gain_two,
        q_sum, gate, up, down, down_tail, pair_tail,
        mixed, d_tokens, d_keys, d_values, o_sum,
    )
    made = [(rows, width), (rows, cols), (rows, cols), (rows, cols), (1, rows), (1, rows)]
    return pl.pallas_call(
        finish_kernel,
        out_shape=[jax.ShapeDtypeStruct(x.shape, x.dtype) for x in ins[11:]]
        + [jax.ShapeDtypeStruct(shape, F32) for shape in made],
        in_specs=[ANY] * len(ins),
        out_specs=[ANY] * 11,
        scratch_shapes=[pltpu.VMEM(x.shape, x.dtype) for x in ins]
        + [pltpu.VMEM(shape, F32) for shape in made]
        + [pltpu.SemaphoreType.DMA((len(ins),)), pltpu.SemaphoreType.DMA((11,))],
        compiler_params=pltpu.CompilerParams(vmem_limit_bytes=60 << 20),
        name="finish",
    )(*ins)


def per_device(
    nh,
    ns,
    tokens,
    keys,
    values,
    q_weight,
    o_weight,
    gate_weight,
    up_weight,
    down_weight,
    attn_gain,
    ffn_gain,
    span_order,
    doc_lengths,
    cotangent,
):
    gain_one, gain_two = attn_gain[None], ffn_gain[None]
    sums = layer_call(
        q_weight,
        gate_weight,
        up_weight,
        down_weight.T,
        gain_one,
        gain_two,
        tokens,
        o_weight,
        keys,
        values,
        cotangent,
        span_order,
        doc_lengths,
    )[:11]
    (
        mixed_out, grad_tokens, grad_keys, grad_values, grad_o, grad_q, grad_gate, grad_up,
        grad_down, grad_gain_one, grad_gain_two,
    ) = finish_call(q_weight, gate_weight, up_weight, gain_one, gain_two, sums)
    return (
        mixed_out,
        grad_tokens,
        grad_keys,
        grad_values,
        grad_q,
        grad_o,
        grad_gate,
        grad_up,
        grad_down.T,
        grad_gain_one[0],
        grad_gain_two[0],
    )


def to_slices(weight, nh):
    rows, cols = weight.shape
    parts = weight.reshape(rows, nh, cols // nh).swapaxes(0, 1)
    return lax.all_to_all(parts, "head", 0, 0, tiled=False).reshape(nh * rows, cols // nh)


def from_slices(part, nh):
    rows, cols = part.shape
    parts = part.reshape(nh, rows // nh, cols)
    parts = lax.all_to_all(parts, "head", 0, 0, tiled=False)
    return parts.swapaxes(0, 1).reshape(rows // nh, nh * cols)


def gather_seq(part):
    return lax.all_gather(part, "seq", axis=0, tiled=True)


def scatter_seq(full):
    return lax.psum_scatter(full.astype(BF16), "seq", scatter_dimension=0, tiled=True)


def gather_head(part):
    return lax.all_gather(part, "head", axis=0, tiled=True)


def scatter_head(full):
    return lax.psum_scatter(full.astype(BF16), "head", scatter_dimension=0, tiled=True)


def per_device_plain(
    nh,
    ns,
    tokens,
    keys,
    values,
    q_weight,
    o_weight,
    gate_weight,
    up_weight,
    down_weight,
    attn_gain,
    ffn_gain,
    span_order,
    doc_lengths,
    cotangent,
):
    local, width = tokens.shape
    rows = q_weight.shape[0]

    def shuffle(field):
        return field.reshape(local, nh, ns, rows).swapaxes(1, 2).reshape(local, width)

    def unshuffle(field):
        return field.reshape(local, ns, nh, rows).swapaxes(1, 2).reshape(local, width)

    gain_one = attn_gain.astype(F32)[:, None]
    gain_two = ffn_gain.astype(F32)[:, None]
    inputs = tokens.astype(F32)
    scale_one = rms_scale(inputs)
    normed_one = inputs * scale_one
    normed_one_all = gather_head(shuffle(normed_one.astype(BF16)))
    w_q = gather_seq(to_slices((q_weight * gain_one).astype(BF16), nh))
    key_heads = to_slices(keys, nh)
    value_heads = to_slices(values, nh)
    w_o = gather_seq(o_weight)
    w_gate = gather_seq(to_slices((gate_weight * gain_two).astype(BF16), nh))
    w_up = gather_seq(to_slices((up_weight * gain_two).astype(BF16), nh))
    w_down = gather_seq(to_slices(down_weight.T, nh))
    cotangent_all = gather_head(shuffle(cotangent))

    group = normed_one_all.shape[0]
    position, segment = places(span_order[0], doc_lengths[0], group)
    place_q = jnp.stack([position, segment], axis=1)
    place_k = jnp.stack([position, segment], axis=0)

    query = dot(normed_one_all, w_q, ((1,), (0,))).astype(BF16)
    attended, lse = attend(query, key_heads, value_heads, place_q, place_k)
    hidden = inputs + scatter_head(dot(attended, w_o, ((1,), (0,)))).astype(F32)
    scale_two = rms_scale(hidden)
    normed_two = hidden * scale_two
    normed_two_all = gather_head(shuffle(normed_two.astype(BF16)))

    gate = dot(normed_two_all, w_gate, ((1,), (0,)))
    up = dot(normed_two_all, w_up, ((1,), (0,)))
    sigma = jax.nn.sigmoid(gate)
    act = (gate * sigma * up).astype(BF16)
    down_sum = scatter_seq(dot(cotangent_all, act, ((0,), (0,))))
    grad_act = dot(cotangent_all, w_down, ((1,), (0,)))
    grad_gate = (grad_act * up * sigma * (1.0 + gate * (1.0 - sigma))).astype(BF16)
    grad_up = (grad_act * gate * sigma).astype(BF16)
    spread_two = dot(grad_gate, w_gate, ((1,), (1,))) + dot(grad_up, w_up, ((1,), (1,)))
    scaled_two = unshuffle(scatter_head(spread_two)).astype(F32)
    gate_sum = scatter_seq(dot(normed_two_all, grad_gate, ((0,), (0,))))
    up_sum = scatter_seq(dot(normed_two_all, grad_up, ((0,), (0,))))
    mixed = unshuffle(scatter_head(dot(act, w_down, ((1,), (1,)))))
    mixed_out = (hidden + mixed.astype(F32)).astype(BF16)

    grad_hidden = cotangent.astype(F32) + scale_two * (
        scaled_two - normed_two * jnp.mean(scaled_two * normed_two, axis=-1, keepdims=True)
    )
    grad_hidden_all = gather_head(grad_hidden.astype(BF16))
    grad_attended = dot(grad_hidden_all, w_o, ((1,), (1,))).astype(BF16)
    o_sum = scatter_seq(dot(attended, grad_hidden_all, ((0,), (0,))))
    grad_query, grad_keys, grad_values = attend_back(
        query, key_heads, value_heads, grad_attended, lse, place_q, place_k
    )
    grad_keys = from_slices(grad_keys, nh)
    grad_values = from_slices(grad_values, nh)
    scaled_one = unshuffle(scatter_head(dot(grad_query, w_q, ((1,), (1,))))).astype(F32)
    q_sum = scatter_seq(dot(normed_one_all, grad_query, ((0,), (0,))))
    grad_tokens = grad_hidden + scale_one * (
        scaled_one - normed_one * jnp.mean(scaled_one * normed_one, axis=-1, keepdims=True)
    )
    q_sum = from_slices(q_sum, nh).astype(F32)
    gate_sum = from_slices(gate_sum, nh).astype(F32)
    up_sum = from_slices(up_sum, nh).astype(F32)
    down_sum = from_slices(down_sum, nh).astype(F32)
    grad_gain_one = jnp.sum(q_weight.astype(F32) * q_sum, axis=1)
    grad_gain_two = jnp.sum(
        gate_weight.astype(F32) * gate_sum + up_weight.astype(F32) * up_sum, axis=1
    )
    return (
        mixed_out,
        grad_tokens.astype(BF16),
        grad_keys,
        grad_values,
        gain_one * q_sum,
        o_sum.astype(F32),
        gain_two * gate_sum,
        gain_two * up_sum,
        down_sum.T,
        grad_gain_one,
        grad_gain_two,
    )


def solution(mesh):
    both = ("head", "seq")
    nh, ns = mesh.shape["head"], mesh.shape["seq"]
    body = per_device if (nh, ns) == (NH, NS) else per_device_plain
    rows, cols, line, own = P(both, None), P(None, both), P(both), P("seq", None)
    return jax.shard_map(
        functools.partial(body, nh, ns),
        mesh=mesh,
        in_specs=(rows,) * 7 + (cols, line, line, own, own, rows),
        out_specs=(rows,) * 8 + (cols, line, line),
        check_vma=False,
    )
```

```python
import functools
import math

import jax
import jax.numpy as jnp
from jax import lax
from jax.experimental import pallas as pl
from jax.experimental.pallas import tpu as pltpu
from jax.sharding import PartitionSpec as P

HEAD_DIM = 128
NH, NS = 8, 4
EPS = 1e-06
BF16 = jnp.bfloat16
F32 = jnp.float32


def rms_scale(field):
    return lax.rsqrt(jnp.mean(field * field, axis=-1, keepdims=True) + EPS)


def dot(left, right, dims):
    return lax.dot_general(left, right, (dims, ((), ())), preferred_element_type=F32)


def places(order_row, length_row, group):
    count = order_row.shape[0]
    width = group // count
    slots = jnp.arange(group, dtype=jnp.int32)
    which = slots // width
    picked = jnp.where(
        which[:, None] == jnp.arange(count, dtype=jnp.int32)[None, :], order_row[None, :], 0
    )
    position = jnp.sum(picked, axis=1) * width + slots % width
    bounds = jnp.cumsum(length_row)
    segment = jnp.sum((position[:, None] >= bounds[None, :]).astype(jnp.int32), axis=1)
    return (position, segment)


def attend_kernel(q_ref, k_ref, v_ref, place_q, place_k, out_ref, lse_ref):
    scale = 1.0 / math.sqrt(HEAD_DIM)
    raw = dot(q_ref[...], k_ref[...], ((1,), (1,)))
    allowed = (place_q[:, 1:2] == place_k[1:2, :]) & (place_k[0:1, :] <= place_q[:, 0:1])
    logits = jnp.where(allowed, raw * scale, -1e30)
    top = jnp.max(logits, axis=-1, keepdims=True)
    expo = jnp.exp(logits - top)
    total = jnp.sum(expo, axis=-1, keepdims=True)
    probs = expo * (1.0 / total)
    out_ref[...] = dot(probs.astype(BF16), v_ref[...], ((1,), (0,))).astype(BF16)
    lse_ref[...] = jnp.broadcast_to(top + jnp.log(total), lse_ref.shape)


def attend(query, keys, values, place_q, place_k):
    group, width = query.shape
    heads = width // HEAD_DIM
    rows = min(group, 256)
    block = pl.BlockSpec((rows, HEAD_DIM), lambda h, i: (i, h))
    whole = pl.BlockSpec((group, HEAD_DIM), lambda h, i: (0, h))
    return pl.pallas_call(
        attend_kernel,
        grid=(heads, group // rows),
        in_specs=[
            block,
            whole,
            whole,
            pl.BlockSpec((rows, 2), lambda h, i: (i, 0)),
            pl.BlockSpec((2, group), lambda h, i: (0, 0)),
        ],
        out_specs=[block, block],
        out_shape=[
            jax.ShapeDtypeStruct((group, width), BF16),
            jax.ShapeDtypeStruct((group, width), F32),
        ],
        compiler_params=pltpu.CompilerParams(vmem_limit_bytes=48 << 20),
        cost_estimate=pl.CostEstimate(
            flops=4 * group * group * width,
            bytes_accessed=12 * group * width,
            transcendentals=heads * group * group,
        ),
        name="attend",
    )(query, keys, values, place_q, place_k)


def attend_back_kernel(
    q_ref, k_ref, v_ref, do_ref, lse_ref, place_q, place_k, dq_ref, dk_ref, dv_ref, dk_sum, dv_sum
):
    step = pl.program_id(1)
    scale = 1.0 / math.sqrt(HEAD_DIM)
    query, keys, grad = q_ref[...], k_ref[...], do_ref[...]
    raw = dot(query, keys, ((1,), (1,)))
    allowed = (place_q[:, 1:2] == place_k[1:2, :]) & (place_k[0:1, :] <= place_q[:, 0:1])
    logits = jnp.where(allowed, raw * scale, -1e30)
    probs = jnp.exp(logits - lse_ref[:, :1])
    grad_probs = dot(grad, v_ref[...], ((1,), (1,)))
    inner = jnp.sum(probs * grad_probs, axis=-1, keepdims=True)
    grad_raw = (probs * (grad_probs - inner) * scale).astype(BF16)
    dq_ref[...] = dot(grad_raw, keys, ((1,), (0,))).astype(BF16)

    @pl.when(step == 0)
    def _():
        dk_sum[...] = jnp.zeros_like(dk_sum)
        dv_sum[...] = jnp.zeros_like(dv_sum)

    dk_sum[...] += dot(grad_raw, query, ((0,), (0,)))
    dv_sum[...] += dot(probs.astype(BF16), grad, ((0,), (0,)))

    @pl.when(step == pl.num_programs(1) - 1)
    def _():
        dk_ref[...] = dk_sum[...].astype(BF16)
        dv_ref[...] = dv_sum[...].astype(BF16)


def attend_back(query, keys, values, grad, lse, place_q, place_k):
    group, width = query.shape
    heads = width // HEAD_DIM
    rows = min(group, 256)
    block = pl.BlockSpec((rows, HEAD_DIM), lambda h, i: (i, h))
    whole = pl.BlockSpec((group, HEAD_DIM), lambda h, i: (0, h))
    full = jax.ShapeDtypeStruct((group, width), BF16)
    return pl.pallas_call(
        attend_back_kernel,
        grid=(heads, group // rows),
        in_specs=[
            block,
            whole,
            whole,
            block,
            block,
            pl.BlockSpec((rows, 2), lambda h, i: (i, 0)),
            pl.BlockSpec((2, group), lambda h, i: (0, 0)),
        ],
        out_specs=[block, whole, whole],
        out_shape=[full, full, full],
        scratch_shapes=[pltpu.VMEM((group, HEAD_DIM), F32)] * 2,
        compiler_params=pltpu.CompilerParams(vmem_limit_bytes=48 << 20),
        cost_estimate=pl.CostEstimate(
            flops=10 * group * group * width,
            bytes_accessed=18 * group * width,
            transcendentals=heads * group * group,
        ),
        name="attend_back",
    )(query, keys, values, grad, lse, place_q, place_k)


MESH = pl.DeviceIdType.MESH
ANY = pl.BlockSpec(memory_space=pl.ANY)
VMEM = pl.BlockSpec(memory_space=pltpu.VMEM)
SMEM = pl.BlockSpec(memory_space=pltpu.SMEM)
LANES = 128


def slices_of(weight, nh):
    rows, cols = weight.shape
    return weight.reshape(rows, nh, cols // nh).swapaxes(0, 1)


def rows_of(parts):
    nh, rows, cols = parts.shape
    return parts.swapaxes(0, 1).reshape(rows, nh * cols)


def flat(parts):
    return parts.reshape(parts.shape[0] * parts.shape[1], parts.shape[2])


def remote(src, dst, send, recv, to):
    return pltpu.make_async_remote_copy(
        src_ref=src, dst_ref=dst, send_sem=send, recv_sem=recv, device_id=to, device_id_type=MESH
    )


class Net:
    def __init__(self):
        self.h = lax.axis_index("head")
        self.s = lax.axis_index("seq")

    def peer(self, k):
        return (lax.bitwise_xor(self.h, k), self.s)

    def greet(self):
        barrier = pltpu.get_barrier_semaphore()
        for k in range(1, NH):
            pl.semaphore_signal(barrier, inc=1, device_id=self.peer(k), device_id_type=MESH)
        for k in range(1, NS):
            there = (self.h, lax.rem(self.s + k, NS))
            pl.semaphore_signal(barrier, inc=1, device_id=there, device_id_type=MESH)
        pl.semaphore_wait(barrier, NH - 1 + NS - 1)

    def swap(self, src, dst, send, recv, own):
        mine = pltpu.make_async_copy(src(self.h), dst(self.h), own)
        mine.start()
        copies = []
        for k in (6, 2, 4, 1, 5, 3, 7):
            to = self.peer(k)
            copy = remote(src(to[0]), dst(self.h), send.at[k - 1], recv.at[k - 1], to)
            copy.start()
            copies.append(copy)

        def finish():
            for copy in copies:
                copy.wait()
            mine.wait()

        return finish

    def gather(self, src, dst, send, recv, own):
        half = src.shape[0] // 2
        lo, hi = pl.ds(0, half), pl.ds(half, half)
        h, core, px, py = self.h, self.peer(1), self.peer(2), self.peer(4)
        x, y, d = px[0], py[0], lax.bitwise_xor(h, 6)
        mine = pltpu.make_async_copy(src, dst.at[h], own)
        mine.start()
        copies = []

        def put(i, a, b, to):
            copy = remote(a, b, send.at[i], recv.at[i], to)
            copy.start()
            copies.append(copy)
            return copy

        def on(i, block, rows, to):
            return put(i, dst.at[block, rows], dst.at[block, rows], to)

        xa = put(0, src.at[lo], dst.at[h, lo], px)
        yb = put(1, src.at[hi], dst.at[h, hi], py)
        near = [put(2, src, dst.at[h], core)]
        xb = put(3, src.at[hi], dst.at[h, hi], px)
        ya = put(4, src.at[lo], dst.at[h, lo], py)
        far = []

        def relay():
            xa.wait_recv()
            far.append(on(5, x, lo, py))
            near.append(on(6, x, lo, core))
            yb.wait_recv()
            far.append(on(7, y, hi, px))
            near.append(on(8, y, hi, core))
            xb.wait_recv()
            near.append(on(9, x, hi, core))
            ya.wait_recv()
            near.append(on(10, y, lo, core))

        def finish():
            far[0].wait_recv()
            near.append(on(11, d, lo, core))
            far[1].wait_recv()
            near.append(on(12, d, hi, core))
            for copy in near:
                copy.wait_recv()
            mine.wait()
            for copy in copies:
                copy.wait_send()

        return relay, finish

    def scatter(self, source, block, core_in, held, far_in, send, recv, read):
        core, px, py = self.peer(1), self.peer(2), self.peer(4)
        half = held.shape[1] // 2
        lo, hi = pl.ds(0, half), pl.ds(half, half)
        copies = []

        def put(i, a, b, to):
            copy = remote(a, b, send.at[i], recv.at[i], to)
            copy.start()
            copies.append(copy)
            return copy

        order = (6, 2, 4, 0)
        near = []
        for i in (0, 2):
            pair = [lax.bitwise_xor(core[0], k) for k in order[i : i + 2]]
            for j, value in enumerate(block(pair)):
                near.append(put(i + j, source(i + j, value), core_in.at[i + j], core))
        far = []
        for i, k in enumerate(order):
            if i % 2 == 0:
                pair = block([lax.bitwise_xor(self.h, k) for k in order[i : i + 2]])
            value = pair[i % 2]
            near[i].wait_recv()
            value = value + read(core_in.at[i]).astype(F32)
            if k:
                held[i] = value.astype(BF16)
            if k == 6:
                far.append(put(4, held.at[0, lo], far_in.at[0], px))
                far.append(put(5, held.at[0, hi], far_in.at[1], py))
            elif k == 2:
                far.append(put(6, held.at[1, lo], far_in.at[2], px))
            elif k == 4:
                far.append(put(7, held.at[2, hi], far_in.at[3], py))

        def pass_on(i, slot, rows, arrived, to):
            arrived.wait_recv()
            joined = held[slot, rows].astype(F32) + read(far_in.at[i]).astype(F32)
            held[slot, rows] = joined.astype(BF16)
            far.append(put(8 + i, held.at[slot, rows], far_in.at[4 + i], to))

        def relay():
            pass_on(0, 2, lo, far[0], py)
            pass_on(1, 1, hi, far[1], px)

        def finish():
            parts = []
            for i, rows in enumerate((slice(0, half), slice(half, 2 * half))):
                part = value[rows]
                for j in (2 + i, 4 + i):
                    far[j].wait_recv()
                    part = part + read(far_in.at[j]).astype(F32)
                parts.append(part)
            for copy in copies:
                copy.wait_send()
            return jnp.concatenate(parts, axis=0)

        return relay, finish

    def z_gather(self, src, block, send, recv):
        s = self.s
        ends = (s == 0) | (s == NS - 1)
        middle = jnp.logical_not(ends)
        across = NS - 1 - s
        near = jnp.where(s == 1, 0, NS - 1)
        steps = ((2, s == 0), (-2, s == NS - 1), (1, s < NS - 1), (-1, s > 0))
        relayed = (across, NS - 1 - near)

        def copy(n):
            return remote(src, block(s), send.at[n], recv.at[s], (self.h, s + steps[n][0]))

        def relay(k):
            origin = relayed[k]
            return remote(block(origin), block(origin), send.at[4 + k], recv.at[origin], (self.h, near))

        for n, (_, where) in enumerate(steps):

            @pl.when(where)
            def _():
                copy(n).start()

        def forward():
            @pl.when(middle)
            def _():
                for k in range(2):
                    relay(k).wait_recv()
                    relay(k).start()

        def finish():
            for t in range(NS):
                waited = ((s == 1) & (t >= 2)) | ((s == 2) & (t < 2))

                @pl.when((s != t) & jnp.logical_not(waited))
                def _():
                    remote(block(t), block(t), send.at[0], recv.at[t], (self.h, s)).wait_recv()

        def drain():
            for n, (_, where) in enumerate(steps):

                @pl.when(where)
                def _():
                    copy(n).wait_send()

            @pl.when(middle)
            def _():
                for k in range(2):
                    relay(k).wait_send()

        return forward, finish, drain


def z_scatter(net, block, value, got, comb, join_v, bufs, send, recv, sems, late):
    s = net.s
    ends = (s == 0) | (s == NS - 1)
    middle = jnp.logical_not(ends)
    inner = jnp.where(s == 0, 1, NS - 2)
    near = jnp.where(s == 1, 0, NS - 1)
    landing = join_v if comb is None else comb
    arrivals = bufs if got is None else got
    goals = (NS - 1 - s, NS - 1 - near)
    end_blocks = (NS - 1 - inner, NS - 1 - s)

    def to_join(k):
        return remote(block(end_blocks[k]), landing.at[k], send.at[k], recv.at[2 + k], (net.h, inner))

    def joined(k):
        return remote(join_v.at[k], arrivals.at[1], send.at[k], recv.at[1], (net.h, goals[k]))

    def direct(t):
        return remote(block(t), arrivals.at[0], send.at[2], recv.at[0], (net.h, t))

    def start():
        @pl.when(ends)
        def _():
            to_join(1).start()
            to_join(0).start()
            direct(inner).start()

        if not late:

            @pl.when(middle)
            def _():
                direct(near).start()

    def join():
        @pl.when(middle)
        def _():
            copies = {}
            for k in (1, 0):
                to_join(k).wait_recv()
                if comb is not None:
                    copies[k] = pltpu.make_async_copy(comb.at[k], join_v.at[k], sems.at[6 + k])
                    copies[k].start()
            for k in (1, 0):
                if comb is not None:
                    copies[k].wait()
                term = join_v[k].astype(F32) + value(goals[k]).astype(F32)
                join_v[k] = term.astype(BF16)
                joined(k).start()
            if late:
                direct(near).start()

    def finish(total):
        total[...] = value(s).astype(F32)
        takes = []
        for k in range(2):
            remote(arrivals.at[k], arrivals.at[k], send.at[0], recv.at[k], (net.h, s)).wait_recv()
            if got is not None:
                takes.append(pltpu.make_async_copy(got.at[k], bufs.at[k], sems.at[4 + k]))
                takes[k].start()
        for k in range(2):
            if got is not None:
                takes[k].wait()
            total[...] += bufs[k].astype(F32)

    def drain():
        @pl.when(ends)
        def _():
            to_join(0).wait_send()
            to_join(1).wait_send()
            direct(inner).wait_send()

        @pl.when(middle)
        def _():
            joined(0).wait_send()
            joined(1).wait_send()
            direct(near).wait_send()

    return start, join, finish, drain


def make_places(order, lengths, place_q, place_k):
    group, count = place_q.shape[0], order.shape[1]
    width = group // count
    for shape, dim in (((group, 1), 0), ((1, group), 1)):
        slots = lax.broadcasted_iota(jnp.int32, shape, dim)
        position = slots
        for c in range(count):
            inside = (slots >= c * width) & (slots < (c + 1) * width)
            position = jnp.where(inside, slots + (order[0, c] - c) * width, position)
        segment = jnp.zeros(shape, jnp.int32)
        bound = 0
        for j in range(lengths.shape[1]):
            bound = bound + lengths[0, j]
            segment = segment + (position >= bound).astype(jnp.int32)
        if dim == 0:
            place_q[:, 0:1] = position
            place_q[:, 1:2] = segment
        else:
            place_k[0:1, :] = position
            place_k[1:2, :] = segment


def mask(place_q, place_k, rows):
    return (place_q[rows, 1:2] == place_k[1:2, :]) & (place_k[0:1, :] <= place_q[rows, 0:1])


def lane_block(w, p, wide):
    return w.at[:, pl.ds(pl.multiple_of(p * wide, wide), wide)]


def load(pairs, sems, base):
    copies = [pltpu.make_async_copy(a, b, sems.at[base + i]) for i, (a, b) in enumerate(pairs)]
    for copy in copies:
        copy.start()

    def finish():
        for copy in copies:
            copy.wait()

    return finish


def layer_kernel(
    q_weight,
    gate_weight,
    up_weight,
    down_rows,
    gain_one,
    gain_two,
    tokens,
    o_own,
    keys,
    values,
    cot_own,
    order,
    lengths,
    mixed_out,
    d_tokens,
    o_out,
    d_keys,
    d_values,
    q_out,
    gate_out,
    up_out,
    down_out,
    down_tail_out,
    pair_tail_out,
    n1_all,
    mixed_near,
    mixed_far,
    got_ffn,
    comb_ffn,
    place_q,
    place_k,
    q_own,
    parts,
    tails_own,
    tails_in,
    tails,
    wq_v,
    wo_v,
    wg_v,
    wu_v,
    wd_v,
    norm_v,
    wide_v,
    k_v,
    v_v,
    query,
    attended,
    lse,
    norm_own,
    hidden_v,
    dh_v,
    near_out,
    core_in,
    held,
    far_in,
    act_v,
    grad_gate,
    grad_up,
    down_term,
    stage,
    stage_two,
    down_tail,
    pair_tail,
    dq_v,
    dk_sum,
    dv_sum,
    joins,
    q_join,
    o_join,
    dt_join,
    pt_join,
    bufs,
    q_bufs,
    o_bufs,
    dt_bufs,
    pt_bufs,
    total,
    dt_total,
    pt_total,
    dt_back,
    pt_back,
    swap_send,
    swap_recv,
    ag_send,
    ag_recv,
    rs_send,
    rs_recv,
    zg_send,
    zg_recv,
    zs_send,
    zs_recv,
    own,
    load_sem,
):
    net = Net()
    h, s = net.h, net.s
    local, width = tokens.shape
    group = NH * local
    wide, hid = query.shape[1], act_v.shape[1]
    main = parts.shape[3]
    rest = hid - main
    step = 256
    tiles = group // step
    fold = width // NH
    scale = 1.0 / math.sqrt(HEAD_DIM)
    body = pl.ds(0, main)
    net.greet()

    def swap(j, src, dst):
        return net.swap(src, dst, swap_send.at[j], swap_recv.at[j], own.at[j])

    def gather(j, src, dst):
        return net.gather(src, dst, ag_send.at[j], ag_recv.at[j], own.at[20 + j])

    def z_gather(j, src, block):
        return net.z_gather(src, block, zg_send.at[j], zg_recv.at[j])

    def slab(w):
        return lambda t: w.at[:, t, :, body]

    def tile_rows(i):
        return pl.ds(pl.multiple_of(i * step, step), step)

    def token_tile(field, i):
        return field[pl.ds(i * (step // local), step // local)].reshape(step, width)

    def own_rows(p):
        return pl.ds(pl.multiple_of(p * local, local), local)

    zo = z_gather(0, o_own, lambda t: wo_v.at[t])
    o_here = load([(o_own, wo_v.at[s])], load_sem, 0)
    rows = q_weight.shape[0]
    diagonal = lax.broadcasted_iota(jnp.int32, (rows, rows), 0) == lax.broadcasted_iota(
        jnp.int32, (rows, rows), 1
    )

    def column(gain):
        field = jnp.broadcast_to(gain[...].astype(F32), (rows, rows))
        return jnp.sum(jnp.where(diagonal, field, 0.0), axis=1, keepdims=True)

    field = (q_weight[...].astype(F32) * column(gain_one)).astype(BF16)
    for p in range(NH):
        q_own[p] = field[:, p * wide : (p + 1) * wide]
    q_there = swap(0, lambda p: q_own.at[p], lambda p: wq_v.at[p, s])
    ffn = ((gate_weight, gain_two), (up_weight, gain_two), (down_rows, None))
    ffn_v = (wg_v, wu_v, wd_v)

    def slices(j):
        weight, gain = ffn[j]
        field = weight[...]
        if gain is not None:
            field = (field.astype(F32) * column(gain)).astype(BF16)
        for p in range(NH):
            parts[j, p] = field[:, p * hid : p * hid + main]
            tails_own[p, :, j * LANES : j * LANES + rest] = field[:, p * hid + main : (p + 1) * hid]
        return swap(
            1 + j, lambda p: parts.at[j, p], lambda p: ffn_v[j].at[p, s, :, body]
        )

    gate_there = slices(0)
    inputs = tokens[...].astype(F32)
    norm_own[...] = (inputs * rms_scale(inputs)).astype(BF16)
    n1_there = gather(0, norm_own, n1_all)
    q_there()
    zq = z_gather(1, wq_v.at[:, s], lambda t: wq_v.at[:, t])
    k_there = swap(5, lambda p: lane_block(keys, p, wide), lambda p: k_v.at[p])
    v_there = swap(6, lambda p: lane_block(values, p, wide), lambda p: v_v.at[p])
    zo[0]()
    gate_there()
    zg = z_gather(2, wg_v.at[:, s, :, body], slab(wg_v))
    n1_there[0]()
    zq[0]()
    n1_there[1]()
    n1_here = load([(n1_all, norm_v)], load_sem, 1)
    up_there = slices(1)
    make_places(order, lengths, place_q, place_k)
    k_there()
    v_there()
    zq[1]()
    n1_here()

    @pl.loop(0, tiles)
    def _(i):
        query[tile_rows(i), :] = dot(
            token_tile(norm_v, i), wq_v[...].reshape(width, wide), ((1,), (0,))
        ).astype(BF16)

    down_there = slices(2)
    tails_there = swap(4, lambda p: tails_own.at[p], lambda p: tails_in.at[p])
    up_there()
    zu = z_gather(4, wu_v.at[:, s, :, body], slab(wu_v))

    for head in range(wide // HEAD_DIM):
        cols = slice(head * HEAD_DIM, (head + 1) * HEAD_DIM)

        @pl.loop(0, tiles)
        def _(i):
            rows = tile_rows(i)
            raw = dot(query[rows, cols], k_v[:, :, cols].reshape(group, HEAD_DIM), ((1,), (1,)))
            logits = jnp.where(mask(place_q, place_k, rows), raw * scale, -1e30)
            top = jnp.max(logits, axis=-1, keepdims=True)
            expo = jnp.exp(logits - top)
            norm = jnp.sum(expo, axis=-1, keepdims=True)
            probs = (expo * (1.0 / norm)).astype(BF16)
            attended[rows, cols] = dot(
                probs, v_v[:, :, cols].reshape(group, HEAD_DIM), ((1,), (0,))
            ).astype(BF16)
            lse[rows, head : head + 1] = top + jnp.log(norm)

        if head == 0:
            zg[0]()

    tails_there()
    for j in range(3):
        for p in range(NH):
            at = (j * NH + p) * rest
            tails[s, :, at : at + rest] = tails_in[p, :, j * LANES : j * LANES + rest]
    pair, last = pl.ds(0, 2 * NH * rest), pl.ds(2 * NH * rest, NH * rest)
    zt = z_gather(3, tails.at[s, :, pair], lambda t: tails.at[t, :, pair])
    zo[1]()
    o_here()

    def scatter(
        j, block, core=core_in, far=far_in, read=lambda ref: ref[...], near=near_out, keep=held
    ):
        def source(i, value):
            near[i] = value.astype(BF16)
            return near.at[i]

        return net.scatter(source, block, core, keep, far, rs_send.at[j], rs_recv.at[j], read)

    def rows_of_heads(field, heads):
        return jnp.concatenate([field[own_rows(p), :] for p in heads], axis=0)

    def halves(value):
        return value[:local], value[local:]

    def o_block(heads):
        part = rows_of_heads(attended, heads)
        return halves(dot(part, wo_v[...].reshape(wide, width), ((1,), (0,))))

    o_sum = scatter(0, o_block)
    o_sum[0]()
    zu[0]()
    down_there()
    zl = z_gather(6, tails.at[s, :, last], lambda t: tails.at[t, :, last])
    zd = z_gather(5, wd_v.at[:, s, :, body], slab(wd_v))
    hidden = tokens[...].astype(F32) + o_sum[1]()
    hidden_v[...] = hidden
    norm_own[...] = (hidden * rms_scale(hidden)).astype(BF16)
    n2_there = gather(2, norm_own, norm_v)
    n2_there[0]()
    zt[0]()
    n2_there[1]()
    zl[0]()
    zd[0]()
    cot_there = gather(1, cot_own, wide_v)
    cot_there[0]()
    zt[1]()

    def matrix(w):
        return w[...].reshape(width, hid)

    def add_tail(j):
        for p in range(NH):
            at = (j * NH + p) * rest
            ffn_v[j][p, :, :, main:hid] = tails[:, :, at : at + rest]

    add_tail(0)
    zg[1]()
    @pl.loop(0, tiles)
    def _(i):
        rows = tile_rows(i)
        gate = dot(token_tile(norm_v, i), matrix(wg_v), ((1,), (0,)))
        sigma = jax.nn.sigmoid(gate)
        grad_up[rows, :] = (gate * sigma).astype(BF16)
        grad_gate[rows, :] = (sigma * (1.0 + gate * (1.0 - sigma))).astype(BF16)

    add_tail(1)
    cot_there[1]()
    zu[1]()

    @pl.loop(0, tiles)
    def _(i):
        rows = tile_rows(i)
        up = dot(token_tile(norm_v, i), matrix(wu_v), ((1,), (0,)))
        act_v[rows, :] = (grad_up[rows, :].astype(F32) * up).astype(BF16)
        grad_gate[rows, :] = (grad_gate[rows, :].astype(F32) * up).astype(BF16)

    def columns(field, i):
        cols = pl.ds(pl.multiple_of(i * fold, fold), fold)
        return field[:, :, cols].reshape(group, fold)

    def put_term(i, left, right, body_ref, tail_ref):
        value = dot(left, right, ((0,), (0,))).astype(BF16)
        body_ref[i, :, :, body] = value[:, :main].reshape(NS, fold // NS, main)
        tail_ref[i, :, 0:rest] = value[:, main:]

    def pack(tail_ref, out, base):
        for p in range(NH):
            at = (base * NH + p) * rest
            out[:, :, at : at + rest] = tail_ref[p, :, 0:rest].reshape(NS, fold // NS, rest)

    @pl.loop(0, NH)
    def _(i):
        put_term(i, columns(wide_v, i), act_v[...], down_term, stage)

    def z_sum(j, block, value, got, comb, join, buf):
        z = z_scatter(net, block, value, got, comb, join, buf, zs_send.at[j], zs_recv.at[j], load_sem, j < 3)
        z[0]()
        return z

    def slab_value(w):
        return lambda t: w[:, pl.ds(t, 1), :, body].reshape(NH, fold // NS, main)

    def block_value(w):
        return lambda t: w[pl.ds(t, 1)].reshape(w.shape[1:])

    z_down = z_sum(
        0, slab(down_term), slab_value(down_term), got_ffn.at[0], comb_ffn.at[0], joins, bufs
    )
    pack(stage, down_tail, 0)
    z_dt = z_sum(
        1, lambda t: down_tail.at[t], block_value(down_tail), None, None, dt_join, dt_bufs
    )
    zl[1]()
    add_tail(2)
    zd[1]()

    @pl.loop(0, tiles)
    def _(i):
        rows = tile_rows(i)
        grad_act = dot(token_tile(wide_v, i), matrix(wd_v), ((1,), (0,)))
        grad_gate[rows, :] = (grad_act * grad_gate[rows, :].astype(F32)).astype(BF16)
        grad_up[rows, :] = (grad_act * grad_up[rows, :].astype(F32)).astype(BF16)

    def spread_block(heads):
        value = dot(rows_of_heads(grad_gate, heads), matrix(wg_v), ((1,), (1,)))
        return halves(value + dot(rows_of_heads(grad_up, heads), matrix(wu_v), ((1,), (1,))))

    ffn_sum = scatter(1, spread_block)
    zg[2]()

    @pl.loop(0, NH)
    def _(i):
        put_term(i, columns(norm_v, i), grad_gate[...], wg_v, stage)

    z_gate = z_sum(
        2, slab(wg_v), slab_value(wg_v), got_ffn.at[1], comb_ffn.at[1], joins, bufs
    )
    ffn_sum[0]()
    z_down[1]()
    z_dt[1]()

    zu[2]()

    @pl.loop(0, NH)
    def _(i):
        put_term(i, columns(norm_v, i), grad_up[...], wu_v, stage_two)

    n1_here = load([(n1_all, norm_v)], load_sem, 0)
    z_up = z_sum(4, slab(wu_v), slab_value(wu_v), got_ffn.at[2], comb_ffn.at[2], joins, bufs)
    pack(stage, pair_tail, 0)
    pack(stage_two, pair_tail, 1)
    z_pt = z_sum(
        3, lambda t: pair_tail.at[t], block_value(pair_tail), None, None, pt_join, pt_bufs
    )

    hidden = hidden_v[...]
    scale_two = rms_scale(hidden)
    normed_two = hidden * scale_two
    scaled_two = ffn_sum[1]()
    grad_hidden = cot_own[...].astype(F32) + scale_two * (
        scaled_two - normed_two * jnp.mean(scaled_two * normed_two, axis=-1, keepdims=True)
    )
    dh_v[...] = grad_hidden
    norm_own[...] = grad_hidden.astype(BF16)
    dh_there = gather(3, norm_own, wide_v)
    dh_there[0]()
    backs = []

    def back(j, z, out, result):
        z[2](total)
        result[...] = total[...].astype(BF16)
        backs.append(swap(j, lambda p: result.at[p], lambda p: out.at[p]))

    back(7, z_down, down_out, parts.at[2])
    z_dt[2](dt_total)
    for p in range(NH):
        dt_back[p, :, 0:rest] = dt_total[:, p * rest : (p + 1) * rest].astype(BF16)
    backs.append(swap(8, lambda p: dt_back.at[p], lambda p: down_tail_out.at[p]))
    dh_there[1]()
    z_down[3]()
    z_gate[1]()

    @pl.loop(0, tiles)
    def _(i):
        dq_v[tile_rows(i), :] = dot(
            token_tile(wide_v, i), wo_v[...].reshape(wide, width), ((1,), (1,))
        ).astype(BF16)

    for head in range(wide // HEAD_DIM):
        cols = slice(head * HEAD_DIM, (head + 1) * HEAD_DIM)
        dk_sum[...] = jnp.zeros_like(dk_sum)
        dv_sum[...] = jnp.zeros_like(dv_sum)

        @pl.loop(0, tiles)
        def _(i):
            rows = tile_rows(i)
            key_rows = k_v[:, :, cols].reshape(group, HEAD_DIM)
            part, grad = query[rows, cols], dq_v[rows, cols]
            raw = dot(part, key_rows, ((1,), (1,)))
            logits = jnp.where(mask(place_q, place_k, rows), raw * scale, -1e30)
            probs = jnp.exp(logits - lse[rows, head : head + 1])
            grad_probs = dot(grad, v_v[:, :, cols].reshape(group, HEAD_DIM), ((1,), (1,)))
            inner = jnp.sum(probs * grad_probs, axis=-1, keepdims=True)
            grad_raw = (probs * (grad_probs - inner) * scale).astype(BF16)
            dq_v[rows, cols] = dot(grad_raw, key_rows, ((1,), (0,))).astype(BF16)
            dk_sum[...] += dot(grad_raw, part, ((0,), (0,)))
            dv_sum[...] += dot(probs.astype(BF16), grad, ((0,), (0,)))

        k_v[:, :, cols] = dk_sum[...].astype(BF16).reshape(NH, local, HEAD_DIM)
        v_v[:, :, cols] = dv_sum[...].astype(BF16).reshape(NH, local, HEAD_DIM)

    def q_block(heads):
        part = rows_of_heads(dq_v, heads)
        return halves(dot(part, wq_v[...].reshape(width, wide), ((1,), (1,))))

    q_sum = scatter(2, q_block)
    q_sum[0]()
    n1_here()

    zq[2]()

    @pl.loop(0, NH)
    def _(i):
        part = dot(columns(norm_v, i), dq_v[...], ((0,), (0,)))
        wq_v[i] = part.astype(BF16).reshape(NS, fold // NS, wide)

    zq_sum = z_sum(
        5,
        lambda t: wq_v.at[:, t],
        lambda t: wq_v[:, pl.ds(t, 1)].reshape(NH, fold // NS, wide),
        None,
        None,
        q_join,
        q_bufs,
    )

    zo[2]()

    @pl.loop(0, NH)
    def _(i):
        cols = pl.ds(pl.multiple_of(i * fold, fold), fold)
        part = dot(attended[...], columns(wide_v, i), ((0,), (0,)))
        wo_v[:, :, cols] = part.astype(BF16).reshape(NS, wide // NS, fold)

    zo_sum = z_sum(6, lambda t: wo_v.at[t], block_value(wo_v), None, None, o_join, o_bufs)
    backs.append(swap(9, lambda p: k_v.at[p], lambda p: lane_block(d_keys, p, wide)))
    backs.append(swap(10, lambda p: v_v.at[p], lambda p: lane_block(d_values, p, wide)))
    z_gate[3]()
    z_up[1]()
    back(11, z_gate, gate_out, parts.at[0])

    inputs = tokens[...].astype(F32)
    scale_one = rms_scale(inputs)
    normed_one = inputs * scale_one
    scaled_one = q_sum[1]()
    d_tokens[...] = (
        dh_v[...]
        + scale_one
        * (scaled_one - normed_one * jnp.mean(scaled_one * normed_one, axis=-1, keepdims=True))
    ).astype(BF16)

    def mixed_block(heads):
        return halves(dot(rows_of_heads(act_v, heads), matrix(wd_v), ((1,), (1,))))

    def staged(ref):
        slot = norm_v.at[NH - 1, pl.ds(0, ref.shape[0])]
        load([(ref, slot)], load_sem, 2)()
        return slot[...]

    mixed_sum = scatter(
        3, mixed_block, mixed_near, mixed_far, staged, norm_v, norm_v.at[pl.ds(4, 3)]
    )
    back(12, z_up, up_out, parts.at[1])
    mixed_sum[0]()
    z_pt[1]()
    zq_sum[1]()
    zo_sum[1]()
    z_pt[2](pt_total)
    for j in range(2):
        for p in range(NH):
            at = (j * NH + p) * rest
            pt_back[p, :, j * LANES : j * LANES + rest] = pt_total[:, at : at + rest].astype(BF16)
    backs.append(swap(13, lambda p: pt_back.at[p], lambda p: pair_tail_out.at[p]))
    mixed_out[...] = (hidden_v[...] + mixed_sum[1]()).astype(BF16)
    q_total = total.at[:, :, pl.ds(0, wide)]
    zq_sum[2](q_total)
    q_own[...] = q_total[...].astype(BF16)
    backs.append(swap(14, lambda p: q_own.at[p], lambda p: lane_block(q_out, p, wide)))
    zo_sum[2](o_out)
    for done in backs:
        done()
    for z in (zt, zl, zd):
        z[2]()
    for z in (z_dt, z_pt, z_up, zq_sum, zo_sum):
        z[3]()


def layer_call(q_weight, gate_weight, up_weight, down_rows, gain_one, gain_two, tokens, o_own, keys, values, cot_own, order, lengths):
    local, width = tokens.shape
    group = NH * local
    rows = o_own.shape[0]
    wide, hid = width // NH, gate_weight.shape[1] // NH
    main = hid // LANES * LANES
    rest = hid - main

    def bf(*shape):
        return jax.ShapeDtypeStruct(shape, BF16)

    def vm(*shape, dtype=BF16):
        return pltpu.VMEM(shape, dtype)

    out_shape = [
        bf(local, width),
        bf(local, width),
        jax.ShapeDtypeStruct((rows, width), F32),
        bf(local, width),
        bf(local, width),
        bf(rows, width),
        bf(NH, rows, main),
        bf(NH, rows, main),
        bf(NH, rows, main),
        bf(NH, rows, LANES),
        bf(NH, rows, 2 * LANES),
        bf(NH, local, width),
        bf(4, local, width),
        bf(6, local // 2, width),
        bf(3, 2, NH, rows, main),
        bf(3, 2, NH, rows, main),
    ]
    dma = pltpu.SemaphoreType.DMA
    return pl.pallas_call(
        layer_kernel,
        out_shape=out_shape,
        in_specs=[VMEM] * 7 + [ANY] * 3 + [VMEM] + [SMEM] * 2,
        out_specs=[VMEM] * 3 + [ANY] * 13,
        scratch_shapes=[
            vm(group, 2, dtype=jnp.int32),
            vm(2, group, dtype=jnp.int32),
            vm(NH, rows, wide),
            vm(3, NH, rows, main),
            vm(NH, rows, 3 * LANES),
            vm(NH, rows, 3 * LANES),
            vm(NS, rows, 3 * NH * rest),
            vm(NH, NS, rows, wide),
            vm(NS, rows, width),
            vm(NH, NS, rows, hid),
            vm(NH, NS, rows, hid),
            vm(NH, NS, rows, hid),
            vm(NH, local, width),
            vm(NH, local, width),
            vm(NH, local, wide),
            vm(NH, local, wide),
            vm(group, wide),
            vm(group, wide),
            vm(group, wide // HEAD_DIM, dtype=F32),
            vm(local, width),
            vm(local, width, dtype=F32),
            vm(local, width, dtype=F32),
            vm(4, local, width),
            vm(4, local, width),
            vm(3, local, width),
            vm(6, local // 2, width),
            vm(group, hid),
            vm(group, hid),
            vm(group, hid),
            vm(NH, NS, rows, main),
            vm(NH, NS * rows, LANES),
            vm(NH, NS * rows, LANES),
            vm(NS, rows, NH * rest),
            vm(NS, rows, 2 * NH * rest),
            vm(group, wide),
            vm(group, HEAD_DIM, dtype=F32),
            vm(group, HEAD_DIM, dtype=F32),
            vm(2, NH, rows, main),
            vm(2, NH, rows, wide),
            vm(2, rows, width),
            vm(2, rows, NH * rest),
            vm(2, rows, 2 * NH * rest),
            vm(2, NH, rows, main),
            vm(2, NH, rows, wide),
            vm(2, rows, width),
            vm(2, rows, NH * rest),
            vm(2, rows, 2 * NH * rest),
            vm(NH, rows, main, dtype=F32),
            vm(rows, NH * rest, dtype=F32),
            vm(rows, 2 * NH * rest, dtype=F32),
            vm(NH, rows, LANES),
            vm(NH, rows, 2 * LANES),
            dma((15, 7)),
            dma((15, 7)),
            dma((4, 13)),
            dma((4, 13)),
            dma((4, 10)),
            dma((4, 10)),
            dma((7, 6)),
            dma((7, NS)),
            dma((7, 3)),
            dma((7, 4)),
            dma((24,)),
            dma((8,)),
        ],
        compiler_params=pltpu.CompilerParams(
            collective_id=0, has_side_effects=True, vmem_limit_bytes=127 << 19
        ),
        name="layer",
    )(q_weight, gate_weight, up_weight, down_rows, gain_one, gain_two, tokens, o_own, keys, values, cot_own, order, lengths)


def finish_kernel(*refs):
    ins, refs = refs[:16], refs[16:]
    outs, refs = refs[:11], refs[11:]
    vin, refs = refs[:16], refs[16:]
    vout, (in_sem, out_sem) = refs[:6], refs[6:]
    loads = [pltpu.make_async_copy(a, b, in_sem.at[i]) for i, (a, b) in enumerate(zip(ins, vin))]
    for i in (6, 10, 1, 3, 4, 7, 2, 8, 9, 0, 5, 11, 12, 13, 14, 15):
        loads[i].start()
    stores = []

    def store(i, source):
        copy = pltpu.make_async_copy(source, outs[i], out_sem.at[i])
        copy.start()
        stores.append(copy)

    q_weight, gate_weight, up_weight, gain_one, gain_two, q_sum = vin[:6]
    gate_main, up_main, down_main, down_tail, pair_tail = vin[6:11]
    d_q, d_gate, d_up, d_down, d_gain_one, d_gain_two = vout
    rows = q_weight.shape[0]
    diagonal = lax.broadcasted_iota(jnp.int32, (rows, rows), 0) == lax.broadcasted_iota(
        jnp.int32, (rows, rows), 1
    )

    def column(gain):
        field = jnp.broadcast_to(gain[...].astype(F32), (rows, rows))
        return jnp.sum(jnp.where(diagonal, field, 0.0), axis=1, keepdims=True)

    def row(field):
        return jnp.sum(jnp.where(diagonal, field, 0.0), axis=0, keepdims=True)

    hid = gate_weight.shape[1] // NH
    rest = hid - gate_main.shape[2]
    for i in (3, 4, 1, 6, 10):
        loads[i].wait()
    gain = column(gain_two)
    total = jnp.zeros((rows, hid), F32)
    for i, part, tail, base, weight, out in (
        (6, gate_main, pair_tail, 0, gate_weight, d_gate),
        (7, up_main, pair_tail, LANES, up_weight, d_up),
        (8, down_main, down_tail, 0, None, d_down),
    ):
        if i > 6:
            loads[i].wait()
        if i > 6:
            loads[{7: 2, 8: 9}[i]].wait()
        for p in range(NH):
            at = p * hid
            whole = jnp.concatenate([part[p], tail[p, :, base : base + rest]], axis=1).astype(F32)
            if weight is None:
                out[:, at : at + hid] = whole
            else:
                out[:, at : at + hid] = whole * gain
                own = weight[:, at : at + hid].astype(F32)
                total = total + whole * own
        store(i, out)
    for i in range(5):
        loads[11 + i].wait()
        store(i, vin[11 + i])
    loads[0].wait()
    loads[5].wait()
    raw = q_sum[...].astype(F32)
    d_q[...] = raw * column(gain_one)
    store(5, d_q)
    d_gain_one[...] = row(jnp.sum(raw * q_weight[...].astype(F32), axis=1, keepdims=True))
    store(9, d_gain_one)
    d_gain_two[...] = row(jnp.sum(total, axis=1, keepdims=True))
    store(10, d_gain_two)
    for copy in stores:
        copy.wait()


def finish_call(q_weight, gate_weight, up_weight, gain_one, gain_two, sums):
    rows, width = q_weight.shape
    cols = gate_weight.shape[1]
    mixed, d_tokens, o_sum, d_keys, d_values, q_sum, gate, up, down, down_tail, pair_tail = sums
    ins = (
        q_weight, gate_weight, up_weight, gain_one, gain_two,
        q_sum, gate, up, down, down_tail, pair_tail,
        mixed, d_tokens, d_keys, d_values, o_sum,
    )
    made = [(rows, width), (rows, cols), (rows, cols), (rows, cols), (1, rows), (1, rows)]
    return pl.pallas_call(
        finish_kernel,
        out_shape=[jax.ShapeDtypeStruct(x.shape, x.dtype) for x in ins[11:]]
        + [jax.ShapeDtypeStruct(shape, F32) for shape in made],
        in_specs=[ANY] * len(ins),
        out_specs=[ANY] * 11,
        scratch_shapes=[pltpu.VMEM(x.shape, x.dtype) for x in ins]
        + [pltpu.VMEM(shape, F32) for shape in made]
        + [pltpu.SemaphoreType.DMA((len(ins),)), pltpu.SemaphoreType.DMA((11,))],
        compiler_params=pltpu.CompilerParams(vmem_limit_bytes=60 << 20),
        name="finish",
    )(*ins)


def per_device(
    nh,
    ns,
    tokens,
    keys,
    values,
    q_weight,
    o_weight,
    gate_weight,
    up_weight,
    down_weight,
    attn_gain,
    ffn_gain,
    span_order,
    doc_lengths,
    cotangent,
):
    gain_one, gain_two = attn_gain[None], ffn_gain[None]
    sums = layer_call(
        q_weight,
        gate_weight,
        up_weight,
        down_weight.T,
        gain_one,
        gain_two,
        tokens,
        o_weight,
        keys,
        values,
        cotangent,
        span_order,
        doc_lengths,
    )[:11]
    (
        mixed_out, grad_tokens, grad_keys, grad_values, grad_o, grad_q, grad_gate, grad_up,
        grad_down, grad_gain_one, grad_gain_two,
    ) = finish_call(q_weight, gate_weight, up_weight, gain_one, gain_two, sums)
    return (
        mixed_out,
        grad_tokens,
        grad_keys,
        grad_values,
        grad_q,
        grad_o,
        grad_gate,
        grad_up,
        grad_down.T,
        grad_gain_one[0],
        grad_gain_two[0],
    )


def to_slices(weight, nh):
    rows, cols = weight.shape
    parts = weight.reshape(rows, nh, cols // nh).swapaxes(0, 1)
    return lax.all_to_all(parts, "head", 0, 0, tiled=False).reshape(nh * rows, cols // nh)


def from_slices(part, nh):
    rows, cols = part.shape
    parts = part.reshape(nh, rows // nh, cols)
    parts = lax.all_to_all(parts, "head", 0, 0, tiled=False)
    return parts.swapaxes(0, 1).reshape(rows // nh, nh * cols)


def gather_seq(part):
    return lax.all_gather(part, "seq", axis=0, tiled=True)


def scatter_seq(full):
    return lax.psum_scatter(full.astype(BF16), "seq", scatter_dimension=0, tiled=True)


def gather_head(part):
    return lax.all_gather(part, "head", axis=0, tiled=True)


def scatter_head(full):
    return lax.psum_scatter(full.astype(BF16), "head", scatter_dimension=0, tiled=True)


def per_device_plain(
    nh,
    ns,
    tokens,
    keys,
    values,
    q_weight,
    o_weight,
    gate_weight,
    up_weight,
    down_weight,
    attn_gain,
    ffn_gain,
    span_order,
    doc_lengths,
    cotangent,
):
    local, width = tokens.shape
    rows = q_weight.shape[0]

    def shuffle(field):
        return field.reshape(local, nh, ns, rows).swapaxes(1, 2).reshape(local, width)

    def unshuffle(field):
        return field.reshape(local, ns, nh, rows).swapaxes(1, 2).reshape(local, width)

    gain_one = attn_gain.astype(F32)[:, None]
    gain_two = ffn_gain.astype(F32)[:, None]
    inputs = tokens.astype(F32)
    scale_one = rms_scale(inputs)
    normed_one = inputs * scale_one
    normed_one_all = gather_head(shuffle(normed_one.astype(BF16)))
    w_q = gather_seq(to_slices((q_weight * gain_one).astype(BF16), nh))
    key_heads = to_slices(keys, nh)
    value_heads = to_slices(values, nh)
    w_o = gather_seq(o_weight)
    w_gate = gather_seq(to_slices((gate_weight * gain_two).astype(BF16), nh))
    w_up = gather_seq(to_slices((up_weight * gain_two).astype(BF16), nh))
    w_down = gather_seq(to_slices(down_weight.T, nh))
    cotangent_all = gather_head(shuffle(cotangent))

    group = normed_one_all.shape[0]
    position, segment = places(span_order[0], doc_lengths[0], group)
    place_q = jnp.stack([position, segment], axis=1)
    place_k = jnp.stack([position, segment], axis=0)

    query = dot(normed_one_all, w_q, ((1,), (0,))).astype(BF16)
    attended, lse = attend(query, key_heads, value_heads, place_q, place_k)
    hidden = inputs + scatter_head(dot(attended, w_o, ((1,), (0,)))).astype(F32)
    scale_two = rms_scale(hidden)
    normed_two = hidden * scale_two
    normed_two_all = gather_head(shuffle(normed_two.astype(BF16)))

    gate = dot(normed_two_all, w_gate, ((1,), (0,)))
    up = dot(normed_two_all, w_up, ((1,), (0,)))
    sigma = jax.nn.sigmoid(gate)
    act = (gate * sigma * up).astype(BF16)
    down_sum = scatter_seq(dot(cotangent_all, act, ((0,), (0,))))
    grad_act = dot(cotangent_all, w_down, ((1,), (0,)))
    grad_gate = (grad_act * up * sigma * (1.0 + gate * (1.0 - sigma))).astype(BF16)
    grad_up = (grad_act * gate * sigma).astype(BF16)
    spread_two = dot(grad_gate, w_gate, ((1,), (1,))) + dot(grad_up, w_up, ((1,), (1,)))
    scaled_two = unshuffle(scatter_head(spread_two)).astype(F32)
    gate_sum = scatter_seq(dot(normed_two_all, grad_gate, ((0,), (0,))))
    up_sum = scatter_seq(dot(normed_two_all, grad_up, ((0,), (0,))))
    mixed = unshuffle(scatter_head(dot(act, w_down, ((1,), (1,)))))
    mixed_out = (hidden + mixed.astype(F32)).astype(BF16)

    grad_hidden = cotangent.astype(F32) + scale_two * (
        scaled_two - normed_two * jnp.mean(scaled_two * normed_two, axis=-1, keepdims=True)
    )
    grad_hidden_all = gather_head(grad_hidden.astype(BF16))
    grad_attended = dot(grad_hidden_all, w_o, ((1,), (1,))).astype(BF16)
    o_sum = scatter_seq(dot(attended, grad_hidden_all, ((0,), (0,))))
    grad_query, grad_keys, grad_values = attend_back(
        query, key_heads, value_heads, grad_attended, lse, place_q, place_k
    )
    grad_keys = from_slices(grad_keys, nh)
    grad_values = from_slices(grad_values, nh)
    scaled_one = unshuffle(scatter_head(dot(grad_query, w_q, ((1,), (1,))))).astype(F32)
    q_sum = scatter_seq(dot(normed_one_all, grad_query, ((0,), (0,))))
    grad_tokens = grad_hidden + scale_one * (
        scaled_one - normed_one * jnp.mean(scaled_one * normed_one, axis=-1, keepdims=True)
    )
    q_sum = from_slices(q_sum, nh).astype(F32)
    gate_sum = from_slices(gate_sum, nh).astype(F32)
    up_sum = from_slices(up_sum, nh).astype(F32)
    down_sum = from_slices(down_sum, nh).astype(F32)
    grad_gain_one = jnp.sum(q_weight.astype(F32) * q_sum, axis=1)
    grad_gain_two = jnp.sum(
        gate_weight.astype(F32) * gate_sum + up_weight.astype(F32) * up_sum, axis=1
    )
    return (
        mixed_out,
        grad_tokens.astype(BF16),
        grad_keys,
        grad_values,
        gain_one * q_sum,
        o_sum.astype(F32),
        gain_two * gate_sum,
        gain_two * up_sum,
        down_sum.T,
        grad_gain_one,
        grad_gain_two,
    )


def solution(mesh):
    both = ("head", "seq")
    nh, ns = mesh.shape["head"], mesh.shape["seq"]
    body = per_device if (nh, ns) == (NH, NS) else per_device_plain
    rows, cols, line, own = P(both, None), P(None, both), P(both), P("seq", None)
    return jax.shard_map(
        functools.partial(body, nh, ns),
        mesh=mesh,
        in_specs=(rows,) * 7 + (cols, line, line, own, own, rows),
        out_specs=(rows,) * 8 + (cols, line, line),
        check_vma=False,
    )
```
